32 devices in a mesh: groups: 2 (over y), seq: 16 (over z, x, core).
Axes of the slice: x: 2, y: 2, z: 4, core: 2. Of those that a mesh axis runs over, the one named last changes fastest.
Arguments:
- queries: bfloat16 [4, 32, 64, 3072], P('groups', 'seq'), parts along dimension 0, may hold values from -10 to 10
- own_kv: bfloat16 [4, 32, 64, 1024], P('groups', 'seq'), parts along dimension 0, may hold values from -10 to 10
- past_kv: bfloat16 [64, 16, 1024], P(('groups', 'seq')), parts along dimension 0, may hold values from -8 to 8
- block_home: int32 [64], P('groups'), parts along dimension 0, may hold values from 0 to 31, as said below
- block_list: int32 [32, 16], P('groups'), parts along dimension 0, may hold values from 0 to 31, as said below
- list_len: int32 [32], P('groups'), parts along dimension 0, may hold values from 1 to 16, as said below
- final_weight: bfloat16 [3072, 64], P('seq'), may hold values from -0.4375 to 0.4375
- decoder_weight: bfloat16 [432, 512], P(None, 'seq'), may hold values from -0.3125 to 0.3125
Outputs:
- features: bfloat16 [4, 64, 128, 512], P('groups', 'seq'), parts along dimension 0
The draws below stay inside these ranges and needn't reach their ends.
There are 2 independent parts, one for each index of `groups`. The reference program is written for one: setup_inputs(seed, part) draws one part's arguments, and reference() takes and returns one part's arrays. A program takes and returns all parts, laid end to end along the dimension named above; an argument that names none is the same for every part. Nothing has to cross between parts.
Inputs may be any that keep to these rules, and one draw needn't show every extreme that they name: Block i is stored at row block_home[i] of past_kv; every row holds one block. `block_list`: for each tile b the first list_len[b] entries name blocks stored by pairwise different devices (storage row // 2); later entries are not read. `list_len`: some tile lists 16 blocks.
All inputs are finite; a program needn't handle non-finite values.
Results may differ from the reference program's by a relative error of at most 0.0064.
Values may be sent and summed in bfloat16 or wider, within the bound.
No kernel may reach another device: no remote copies, remote signals or barrier semaphores. Data moves between devices by JAX's collectives and lax.ppermute only.
A program may use at most 64 MiB of HBM per device.

```python
import math
import jax
import jax.numpy as jnp
from jax import lax

FRAMES = 2
WP = 64
HEADS = 24
KV_HEADS = 4
HEAD_DIM = 128
LAT = 16
CH = 512
BT = 16
BLK_DEV = 2
PROWS_ALL = 32
NB = 32
N_SEQ = 16


def segment_fields(key):
    folded = jax.random.fold_in(key, 7)
    query_shape = (FRAMES, PROWS_ALL, WP, HEADS * HEAD_DIM)
    key_shape = (FRAMES, PROWS_ALL, WP, 2 * KV_HEADS * HEAD_DIM)
    query_field = jnp.clip(1.4 * jax.random.normal(jax.random.fold_in(folded, 1), query_shape, jnp.float32), -8.0, 8.0)
    key_field = jnp.clip(1.4 * jax.random.normal(jax.random.fold_in(folded, 2), key_shape, jnp.float32), -8.0, 8.0)
    return (query_field, key_field)


def draw_queries(key, part):
    return segment_fields(key)[0].astype(jnp.bfloat16)


def draw_own_kv(key, part):
    return segment_fields(key)[1].astype(jnp.bfloat16)


def cache_tables(key):
    folded = jax.random.fold_in(key, 5)
    home_rows = jax.random.permutation(jax.random.fold_in(folded, 1), NB).astype(jnp.int32)
    stored_block = jnp.zeros((NB,), jnp.int32).at[home_rows].set(jnp.arange(NB, dtype=jnp.int32))
    row_keys = jax.random.split(jax.random.fold_in(folded, 2), N_SEQ)
    owners = jax.vmap(lambda subkey: jax.random.permutation(subkey, N_SEQ))(row_keys).astype(jnp.int32)
    local_index = jax.random.randint(jax.random.fold_in(folded, 3), (N_SEQ, N_SEQ), 0, BLK_DEV).astype(jnp.int32)
    chosen = stored_block[owners * BLK_DEV + local_index]
    counts = jax.random.randint(jax.random.fold_in(folded, 4), (N_SEQ,), 1, N_SEQ + 1).astype(jnp.int32)
    fullest = jax.random.randint(jax.random.fold_in(folded, 6), (), 0, N_SEQ).astype(jnp.int32)
    counts = jnp.where(jnp.arange(N_SEQ, dtype=jnp.int32) == fullest, N_SEQ, counts).astype(jnp.int32)
    return (home_rows, chosen, counts)


def draw_block_home(key, part):
    return cache_tables(key)[0]


def draw_block_list(key, part):
    return cache_tables(key)[1]


def draw_list_len(key, part):
    return cache_tables(key)[2]


def block_scale(own_key, extent, cuts, least, top_value):
    def one(axis_at, blocks):
        heights = jax.random.uniform(jax.random.fold_in(jax.random.fold_in(own_key, 6), axis_at), (blocks,), jnp.float32, least / len(cuts), top_value / len(cuts))
        return jnp.repeat(jnp.exp(heights), extent[axis_at] // blocks).reshape((-1,) + (1,) * (len(extent) - axis_at - 1))

    gain = one(*cuts[0])
    for cut in cuts[1:]:
        gain = gain * one(*cut)
    return gain


def scatter_about(stream_key, shape, width, reach, cuts=(), held_as=jnp.bfloat16):
    entries = jax.random.normal(stream_key, shape, jnp.float32) * width
    if len(cuts) > 0:
        entries = block_scale(stream_key, shape, cuts, -0.22, 0.18) * entries
    return jnp.clip(entries, min=-reach, max=reach).astype(held_as)


def setup_inputs(seed: int = 0, part: int = 0) -> dict:
    streams_of = jax.random.split(jax.random.key(seed), 9)
    part_keys = jax.random.split(jax.random.fold_in(streams_of[8], part), 9)
    return {
        "queries": draw_queries(jax.random.fold_in(jax.random.fold_in(streams_of[8], part), 71), part),
        "own_kv": draw_own_kv(jax.random.fold_in(jax.random.fold_in(streams_of[8], part), 71), part),
        "past_kv": scatter_about(part_keys[2], (NB, BT, 2 * KV_HEADS * HEAD_DIM), 1.4, 8.0, ((0, 16),)),
        "block_home": draw_block_home(jax.random.fold_in(jax.random.fold_in(streams_of[8], part), 71), part),
        "block_list": draw_block_list(jax.random.fold_in(jax.random.fold_in(streams_of[8], part), 71), part),
        "list_len": draw_list_len(jax.random.fold_in(jax.random.fold_in(streams_of[8], part), 71), part),
        "final_weight": scatter_about(streams_of[6], (HEADS * HEAD_DIM, 4 * LAT), (HEADS * HEAD_DIM // 16) ** -0.5, 0.4375, ((0, 16),)),
        "decoder_weight": scatter_about(streams_of[7], (27 * LAT, CH), (27 * LAT) ** -0.5, 0.3125, ((1, 16),)),
    }


def attend(query_rows, own_rows, past_rows, past_listed):
    tokens = query_rows.shape[0]
    group_size = HEADS // KV_HEADS
    key_width = KV_HEADS * HEAD_DIM
    score_scale = 1.0 / math.sqrt(HEAD_DIM)
    query_heads = query_rows.astype(jnp.float32).reshape(tokens, KV_HEADS, group_size, HEAD_DIM)
    keys_own = own_rows[:, :key_width].astype(jnp.float32).reshape(tokens, KV_HEADS, HEAD_DIM)
    values_own = own_rows[:, key_width:].astype(jnp.float32).reshape(tokens, KV_HEADS, HEAD_DIM)
    past_count = past_rows.shape[0]
    keys_past = past_rows[:, :key_width].astype(jnp.float32).reshape(past_count, KV_HEADS, HEAD_DIM)
    values_past = past_rows[:, key_width:].astype(jnp.float32).reshape(past_count, KV_HEADS, HEAD_DIM)
    scores_own = jnp.einsum('tkgd,skd->kgts', query_heads, keys_own) * score_scale
    scores_past = jnp.einsum('tkgd,skd->kgts', query_heads, keys_past) * score_scale
    scores_past = jnp.where(past_listed[None, None, None, :], scores_past, -1e+30)
    row_top = jnp.maximum(lax.optimization_barrier(jnp.max(scores_own, axis=-1, keepdims=True)), lax.optimization_barrier(jnp.max(scores_past, axis=-1, keepdims=True)))
    exp_own = jnp.exp(scores_own - row_top)
    exp_past = jnp.where(past_listed[None, None, None, :], jnp.exp(scores_past - row_top), 0.0)
    denominator = lax.optimization_barrier(jnp.sum(exp_own, axis=-1, keepdims=True)) + lax.optimization_barrier(jnp.sum(exp_past, axis=-1, keepdims=True))
    weights_own = lax.optimization_barrier((exp_own / denominator).astype(jnp.bfloat16)).astype(jnp.float32)
    weights_past = lax.optimization_barrier((exp_past / denominator).astype(jnp.bfloat16)).astype(jnp.float32)
    mixed = jnp.einsum('kgts,skd->tkgd', weights_own, values_own) + jnp.einsum('kgts,skd->tkgd', weights_past, values_past)
    return mixed.reshape(tokens, HEADS * HEAD_DIM).astype(jnp.bfloat16)

def reference(queries, own_kv, past_kv, block_home, block_list, list_len, final_weight, decoder_weight):
    frames, rows_all, patches, width_query = queries.shape
    tiles = N_SEQ
    patch_rows = rows_all // tiles
    tokens = frames * patch_rows * patches
    pair_width = own_kv.shape[3]

    def one_tile(tile_index):
        query_rows = lax.dynamic_slice_in_dim(queries, tile_index * patch_rows, patch_rows, 1).reshape(tokens, width_query)
        own_rows = lax.dynamic_slice_in_dim(own_kv, tile_index * patch_rows, patch_rows, 1).reshape(tokens, pair_width)
        stored_at = block_home[block_list[tile_index]]
        past_rows = past_kv[stored_at].reshape(tiles * BT, pair_width)
        listed = jnp.arange(tiles, dtype=jnp.int32) < list_len[tile_index]
        past_listed = jnp.repeat(listed, BT)
        return attend(query_rows, own_rows, past_rows, past_listed)
    attended = lax.map(one_tile, jnp.arange(tiles, dtype=jnp.int32))
    predicted = jnp.dot(attended.reshape(tiles * tokens, width_query), final_weight, preferred_element_type=jnp.float32).astype(jnp.bfloat16)
    latent_width = final_weight.shape[1] // 4
    latent = predicted.reshape(tiles, frames, patch_rows, patches, 2, 2, latent_width)
    latent = latent.transpose(1, 0, 2, 4, 3, 5, 6).reshape(frames, 2 * rows_all, 2 * patches, latent_width)
    padded = jnp.pad(latent, ((2, 0), (1, 1), (1, 1), (0, 0)))
    tall = 2 * rows_all
    broad = 2 * patches
    tap_list = []
    for shift_t in range(3):
        for shift_y in range(3):
            for shift_x in range(3):
                tap_list.append(padded[shift_t:shift_t + frames, shift_y:shift_y + tall, shift_x:shift_x + broad, :])
    columns = jnp.concatenate(tap_list, axis=3).reshape(frames * tall * broad, 27 * latent_width)
    features = jnp.dot(columns, decoder_weight, preferred_element_type=jnp.float32).astype(jnp.bfloat16)
    return features.reshape(frames, tall, broad, decoder_weight.shape[1])
```

```python
import functools
import math

import jax
import jax.numpy as jnp
from jax import lax
from jax.experimental import pallas as pl
from jax.experimental.pallas import tpu as pltpu
from jax.sharding import PartitionSpec as P

HEADS = 24
KV_HEADS = 4
HEAD_DIM = 128
GROUP = HEADS // KV_HEADS
LOG2E = 1.4426950408889634
VMEM_LIMIT = 48 * 1024 * 1024


def attention_body(
    blocks_here, listed_max, table, home, blocks, lens, query, key_own, value_own, key_past,
    value_past, weight, out, keys, values, total
):
    step = pl.program_id(0)
    tokens = query.shape[0]
    block_tokens = key_past.shape[1]
    tile = table[0]
    count = lens[tile]

    @pl.when(step == 0)
    def _():
        values[:, HEAD_DIM:] = jnp.ones((values.shape[0], HEAD_DIM), jnp.bfloat16)
        total[...] = jnp.zeros_like(total)

    keys[:tokens] = key_own[...]
    values[:tokens, :HEAD_DIM] = value_own[...]

    def place(entry, carry):
        listed = entry < count
        stored = home[blocks[tile, jnp.where(listed, entry, 0)]]
        place_of = table[1 + ((stored // blocks_here) ^ tile)]
        slot = place_of * blocks_here + stored % blocks_here
        row = pl.multiple_of(tokens + entry * block_tokens, block_tokens)
        keys[pl.ds(row, block_tokens)] = key_past[slot]
        live = jnp.where(listed, 1.0, 0.0)
        values[pl.ds(row, block_tokens), :HEAD_DIM] = jnp.where(
            listed, value_past[slot], jnp.zeros((block_tokens, HEAD_DIM), jnp.bfloat16)
        )
        values[pl.ds(row, block_tokens), HEAD_DIM:] = jnp.full(
            (block_tokens, HEAD_DIM), live, jnp.float32
        ).astype(jnp.bfloat16)
        return carry

    lax.fori_loop(0, listed_max, place, 0, unroll=listed_max <= 16)

    scale = LOG2E / math.sqrt(HEAD_DIM)
    key_rows = keys[...]
    value_rows = values[...]
    part = total[...]
    for head in range(GROUP):
        score = lax.dot_general(
            query[:, head * HEAD_DIM : (head + 1) * HEAD_DIM],
            key_rows,
            (((1,), (1,)), ((), ())),
            preferred_element_type=jnp.float32,
        )
        top = jnp.max(score, axis=1, keepdims=True)
        weights = jnp.exp2((score - top) * scale).astype(jnp.bfloat16)
        mixed = jnp.dot(weights, value_rows, preferred_element_type=jnp.float32)
        attended = (mixed[:, :HEAD_DIM] / mixed[:, HEAD_DIM:]).astype(jnp.bfloat16)
        part += jnp.dot(
            attended,
            weight[head * HEAD_DIM : (head + 1) * HEAD_DIM],
            preferred_element_type=jnp.float32,
        )
    total[...] = part

    @pl.when(step == KV_HEADS - 1)
    def _():
        out[...] = part.astype(jnp.bfloat16)


def attention(tile, query_rows, own_rows, past, block_home, block_list, list_len, final_weight, blocks_here):
    tokens, width = query_rows.shape
    count, block_tokens, _ = past.shape
    listed_max = block_list.shape[1]
    rows = tokens + listed_max * block_tokens
    span = GROUP * HEAD_DIM
    columns = final_weight.shape[1]
    smem = pl.BlockSpec(memory_space=pltpu.SMEM)
    return pl.pallas_call(
        functools.partial(attention_body, blocks_here, listed_max),
        grid=(KV_HEADS,),
        in_specs=[
            smem,
            smem,
            smem,
            smem,
            pl.BlockSpec((tokens, span), lambda g: (0, g)),
            pl.BlockSpec((tokens, HEAD_DIM), lambda g: (0, g)),
            pl.BlockSpec((tokens, HEAD_DIM), lambda g: (0, KV_HEADS + g)),
            pl.BlockSpec((count, block_tokens, HEAD_DIM), lambda g: (0, 0, g)),
            pl.BlockSpec((count, block_tokens, HEAD_DIM), lambda g: (0, 0, KV_HEADS + g)),
            pl.BlockSpec((span, columns), lambda g: (g, 0)),
        ],
        out_specs=pl.BlockSpec((tokens, columns), lambda g: (0, 0)),
        out_shape=jax.ShapeDtypeStruct((tokens, columns), jnp.bfloat16),
        scratch_shapes=[
            pltpu.VMEM((rows, HEAD_DIM), jnp.bfloat16),
            pltpu.VMEM((rows, 2 * HEAD_DIM), jnp.bfloat16),
            pltpu.VMEM((tokens, columns), jnp.float32),
        ],
        compiler_params=pltpu.CompilerParams(vmem_limit_bytes=VMEM_LIMIT),
        cost_estimate=pl.CostEstimate(
            flops=6 * tokens * rows * width, bytes_accessed=4 * tokens * width, transcendentals=0
        ),
        name="attention",
    )(tile, block_home, block_list, list_len, query_rows, own_rows, own_rows, past, past, final_weight)


def decoder_body(lat, pred, above, below, kernel, out, wide, columns, panel):
    row = pl.program_id(0)
    frames, patch_rows, patches, _ = pred.shape
    broad = 2 * patches
    lanes = wide.shape[2]
    span = 3 * lanes

    @pl.when(row == 0)
    def _():
        wide[...] = jnp.zeros_like(wide)
        columns[...] = jnp.zeros_like(columns)
        panel[...] = jnp.zeros_like(panel)
        depth = (patch_rows + 2) * 4 * lat
        source = lax.broadcasted_iota(jnp.int32, (depth, lanes), 0)
        target = lax.broadcasted_iota(jnp.int32, (depth, lanes), 1)
        wanted = target == (source // (2 * lat) - 1) * lat + source % lat
        inside = (source >= 2 * lat) & (source < depth - 2 * lat)
        for frame in range(frames):
            cells = jnp.concatenate(
                [above[frame]] + [pred[frame, r] for r in range(patch_rows)] + [below[frame]], axis=1
            )
            for side in range(2):
                pick = wanted & inside & ((source // lat) % 2 == side)
                wide[frame, pl.ds(8 + side, patches, stride=2), :] = jnp.dot(
                    cells, pick.astype(jnp.float32).astype(jnp.bfloat16), preferred_element_type=jnp.float32
                )
        for frame in range(frames):
            for shift_t in range(3):
                source_frame = frame + shift_t - 2
                if source_frame < 0:
                    continue
                for shift_x in range(3):
                    columns[
                        frame * broad : (frame + 1) * broad,
                        shift_t * span + shift_x * lanes : shift_t * span + (shift_x + 1) * lanes,
                    ] = wide[source_frame, 7 + shift_x : 7 + shift_x + broad, :].astype(jnp.bfloat16)

    for shift_t in range(3):
        for shift_x in range(3):
            base = shift_t * span + shift_x * lanes

            @pl.when(row > 0)
            def _():
                before = pl.multiple_of(base + (row - 1) * lat, lat)
                panel[pl.ds(before, lat), :] = jnp.zeros((lat, panel.shape[1]), jnp.bfloat16)

            for shift_y in range(3):
                tap = ((3 * shift_t + shift_y) * 3 + shift_x) * lat
                start = pl.multiple_of(base + (row + shift_y) * lat, lat)
                panel[pl.ds(start, lat), :] = kernel[tap : tap + lat, :]
    features = jnp.dot(columns[...], panel[...], preferred_element_type=jnp.float32)
    out[...] = features.astype(jnp.bfloat16).reshape(out.shape)


def decoder(pred, above, below, kernel):
    frames, patch_rows, patches, values = pred.shape
    lat = values // 4
    lanes = 128
    tall, broad = 2 * patch_rows, 2 * patches
    channels = kernel.shape[1]
    depth = 9 * lanes
    assert (tall + 2) * lat <= lanes
    return pl.pallas_call(
        functools.partial(decoder_body, lat),
        grid=(tall,),
        in_specs=[
            pl.BlockSpec(pred.shape, lambda y: (0, 0, 0, 0)),
            pl.BlockSpec(above.shape, lambda y: (0, 0, 0)),
            pl.BlockSpec(below.shape, lambda y: (0, 0, 0)),
            pl.BlockSpec(kernel.shape, lambda y: (0, 0)),
        ],
        out_specs=pl.BlockSpec((frames, 1, broad, channels), lambda y: (0, y, 0, 0)),
        out_shape=jax.ShapeDtypeStruct((frames, tall, broad, channels), jnp.bfloat16),
        scratch_shapes=[
            pltpu.VMEM((frames, broad + 16, lanes), jnp.float32),
            pltpu.VMEM((frames * broad, depth), jnp.bfloat16),
            pltpu.VMEM((depth, channels), jnp.bfloat16),
        ],
        compiler_params=pltpu.CompilerParams(vmem_limit_bytes=VMEM_LIMIT),
        cost_estimate=pl.CostEstimate(
            flops=2 * frames * tall * broad * depth * channels,
            bytes_accessed=2 * frames * tall * broad * channels,
            transcendentals=0,
        ),
        name="decoder",
    )(pred, above, below, kernel)


def exchange(value, offset):
    count = lax.axis_size("seq")
    return lax.ppermute(value, "seq", [(i, i ^ offset) for i in range(count)])


def gather_relative(shard):
    count = lax.axis_size("seq")
    assert count & (count - 1) == 0
    bit = count // 2
    held = shard
    order = [0]
    while bit:
        held = jnp.concatenate([held, exchange(held, bit)], axis=0)
        order = order + [o ^ bit for o in order]
        bit //= 2
    return held, order


def local(queries, own_kv, past_kv, block_home, block_list, list_len, final_weight, decoder_weight):
    frames, patch_rows, patches, width = queries.shape
    tokens = frames * patch_rows * patches
    count = lax.axis_size("seq")
    blocks_here = past_kv.shape[0]
    tile = lax.axis_index("seq").astype(jnp.int32).reshape(1)
    held, order = gather_relative(past_kv)
    past = held
    places = jnp.array([order.index(k) for k in range(count)], jnp.int32)
    tile = jnp.concatenate([tile, places])
    fw = lax.all_gather(final_weight, "seq", axis=0, tiled=True)
    dw = lax.all_gather(decoder_weight, "seq", axis=1, tiled=True)
    predicted = attention(
        tile, queries.reshape(tokens, width), own_kv.reshape(tokens, own_kv.shape[3]), past,
        block_home, block_list, list_len, fw, blocks_here,
    )
    predicted = predicted.reshape(frames, patch_rows, patches, predicted.shape[1])
    above = lax.ppermute(predicted[:, -1], "seq", [(i, i + 1) for i in range(count - 1)])
    below = lax.ppermute(predicted[:, 0], "seq", [(i + 1, i) for i in range(count - 1)])
    return decoder(predicted, above, below, dw)


def solution(mesh):
    return jax.shard_map(
        local,
        mesh=mesh,
        in_specs=(
            P("groups", "seq", None, None),
            P("groups", "seq", None, None),
            P(("groups", "seq"), None, None),
            P("groups"),
            P("groups", None),
            P("groups"),
            P("seq", None),
            P(None, "seq"),
        ),
        out_specs=P("groups", "seq", None, None),
        check_vma=False,
    )
```

```python
import functools
import math

import jax
import jax.numpy as jnp
from jax import lax
from jax.experimental import pallas as pl
from jax.experimental.pallas import tpu as pltpu
from jax.sharding import PartitionSpec as P

HEADS = 24
KV_HEADS = 4
HEAD_DIM = 128
GROUP = HEADS // KV_HEADS
SCALE = math.log2(math.e) / math.sqrt(HEAD_DIM)
SAFE = 2.0**100
MIB = 1024 * 1024
WHOLE = pl.BlockSpec(memory_space=pltpu.VMEM)
SCALARS = pl.BlockSpec(memory_space=pltpu.SMEM)
BF16 = jnp.bfloat16
F32 = jnp.float32


def head_columns(index):
    return slice(index * HEAD_DIM, (index + 1) * HEAD_DIM)


def params(mib):
    return pltpu.CompilerParams(vmem_limit_bytes=mib * MIB)


def own_body(queries, own, packed, sums):
    tokens = queries.shape[0]

    def one(g, carry):
        def columns(index):
            return pl.ds(pl.multiple_of(index * HEAD_DIM, HEAD_DIM), HEAD_DIM)

        query = jnp.concatenate([queries[:, columns(g * GROUP + h)] for h in range(GROUP)], axis=0)
        value = jnp.concatenate(
            [own[:, columns(KV_HEADS + g)], jnp.ones((tokens, HEAD_DIM), BF16)], axis=1
        )
        score = lax.dot_general(
            query, own[:, columns(g)], (((1,), (1,)), ((), ())), preferred_element_type=F32
        )
        top = jnp.max(score, axis=1, keepdims=True)
        weights = jnp.exp2((score - top) * SCALE).astype(BF16)
        mixed = jnp.dot(weights, value, preferred_element_type=F32)
        total = mixed[:, HEAD_DIM:]
        sums[g] = mixed[:, :HEAD_DIM] / total
        level = top + jnp.log2(total) * (1.0 / SCALE)
        high = level.astype(BF16).astype(F32)
        middle = (level - high).astype(BF16).astype(F32)
        low = level - high - middle
        lane = lax.broadcasted_iota(jnp.int32, level.shape, 1)
        extra = jnp.where(lane == 0, high, jnp.where(lane == 1, middle, jnp.where(lane == 2, low, 0.0)))
        packed[g, :, :HEAD_DIM] = query
        packed[g, :, HEAD_DIM:] = extra.astype(BF16)
        return carry

    lax.fori_loop(0, KV_HEADS, one, 0)


def attend_own(query_rows, own_rows):
    tokens, width = query_rows.shape
    rows = GROUP * tokens
    return pl.pallas_call(
        own_body,
        in_specs=[WHOLE, WHOLE],
        out_specs=[WHOLE, WHOLE],
        out_shape=[
            jax.ShapeDtypeStruct((KV_HEADS, rows, 2 * HEAD_DIM), BF16),
            jax.ShapeDtypeStruct((KV_HEADS, rows, HEAD_DIM), F32),
        ],
        compiler_params=params(24),
        cost_estimate=pl.CostEstimate(
            flops=12 * tokens * tokens * width, bytes_accessed=10 * tokens * width, transcendentals=0
        ),
        name="attend_own",
    )(query_rows, own_rows)


def slots_body(blocks_here, table, home, blocks, lens, slots):
    tile = table[0]
    count = lens[tile]
    for entry in range(slots.shape[0]):
        listed = entry < count
        stored = home[blocks[tile, jnp.where(listed, entry, 0)]]
        place = table[1 + ((stored // blocks_here) ^ tile)]
        slots[entry] = jnp.where(listed, place * blocks_here + stored % blocks_here, -1)


def find_slots(table, block_home, block_list, list_len, blocks_here):
    return pl.pallas_call(
        functools.partial(slots_body, blocks_here),
        in_specs=[SCALARS] * 4,
        out_specs=SCALARS,
        out_shape=jax.ShapeDtypeStruct((block_list.shape[1],), jnp.int32),
        name="find_slots",
    )(table, block_home, block_list, list_len)


def past_body(slots, packed, past, sums, weight, out, keys, values, worst):
    entries = slots.shape[0]
    block_tokens = past.shape[1]
    tokens, columns = out.shape
    lane = lax.broadcasted_iota(jnp.int32, (block_tokens, HEAD_DIM), 1)
    minus = jnp.where(lane < 3, -1.0, 0.0)
    zero = jnp.zeros((block_tokens, HEAD_DIM), BF16)
    for entry in range(entries):
        listed = slots[entry] >= 0
        block = past[jnp.where(listed, slots[entry], slots[0])]
        live = jnp.where(listed, 1.0, 0.0)
        level = (minus * live).astype(BF16)
        counted = jnp.full((block_tokens, HEAD_DIM), live, F32).astype(BF16)
        rows = slice(entry * block_tokens, (entry + 1) * block_tokens)
        for g in range(KV_HEADS):
            keys[g, rows, :HEAD_DIM] = jnp.where(listed, block[:, head_columns(g)], zero)
            keys[g, rows, HEAD_DIM:] = level
            values[g, rows, :HEAD_DIM] = jnp.where(listed, block[:, head_columns(KV_HEADS + g)], zero)
            values[g, rows, HEAD_DIM:] = counted

    heads = GROUP if keys.shape[1] <= 512 else 1
    steps = KV_HEADS * GROUP // heads

    def over_steps(one, start):
        if heads == GROUP:
            for step in range(steps):
                start = one(step, start)
            return start
        return lax.fori_loop(0, steps, one, start)

    def place(step):
        if heads == GROUP:
            return step, slice(None), slice(step * GROUP * HEAD_DIM, (step + 1) * GROUP * HEAD_DIM)
        rows = pl.ds(pl.multiple_of((step % GROUP) * tokens, tokens), tokens)
        return step // GROUP, rows, pl.ds(pl.multiple_of(step * HEAD_DIM, HEAD_DIM), HEAD_DIM)

    def scores(g, rows):
        return SCALE * lax.dot_general(
            packed[g, rows], keys[g], (((1,), (1,)), ((), ())), preferred_element_type=F32
        )

    def projected(attended, weight_rows):
        panel = weight[weight_rows]
        part = jnp.zeros((tokens, columns), F32)
        for h in range(heads):
            part += jnp.dot(
                attended[h * tokens : (h + 1) * tokens], panel[head_columns(h)], preferred_element_type=F32
            )
        return part

    def quick(step, carry):
        total, largest = carry
        g, rows, weight_rows = place(step)
        weights = jnp.exp2(scores(g, rows)).astype(BF16)
        mixed = jnp.dot(weights, values[g], preferred_element_type=F32)
        below = mixed[:, HEAD_DIM:] + 1.0
        largest = jnp.maximum(largest, jnp.max(below.reshape((-1,) + largest.shape), axis=0))
        attended = ((mixed[:, :HEAD_DIM] + sums[g, rows]) / below).astype(BF16)
        return total + projected(attended, weight_rows), largest

    nothing = jnp.zeros((tokens, columns), F32)
    total, largest = over_steps(quick, (nothing, jnp.zeros(worst.shape, F32)))
    out[...] = total.astype(BF16)
    worst[...] = largest

    @pl.when(jnp.logical_not(jnp.max(worst[...]) < SAFE))
    def _():
        def careful(step, total):
            g, rows, weight_rows = place(step)
            score = scores(g, rows)
            top = jnp.maximum(jnp.max(score, axis=1, keepdims=True), 0.0)
            weights = jnp.exp2(score - top).astype(BF16)
            mixed = jnp.dot(weights, values[g], preferred_element_type=F32)
            share = jnp.exp2(-top)
            attended = (mixed[:, :HEAD_DIM] + share * sums[g, rows]) / (mixed[:, HEAD_DIM:] + share)
            return total + projected(attended.astype(BF16), weight_rows)

        out[...] = over_steps(careful, nothing).astype(BF16)


def attend_past(slots, packed, past, sums, weight):
    heads, rows, _ = packed.shape
    tokens = rows // GROUP
    keys = slots.shape[0] * past.shape[1]
    columns = weight.shape[1]
    return pl.pallas_call(
        past_body,
        in_specs=[SCALARS, WHOLE, WHOLE, WHOLE, WHOLE],
        out_specs=WHOLE,
        out_shape=jax.ShapeDtypeStruct((tokens, columns), BF16),
        scratch_shapes=[
            pltpu.VMEM((heads, keys, 2 * HEAD_DIM), BF16),
            pltpu.VMEM((heads, keys, 2 * HEAD_DIM), BF16),
            pltpu.VMEM((8, HEAD_DIM), F32),
        ],
        compiler_params=params(40 if keys > 256 else 24),
        cost_estimate=pl.CostEstimate(
            flops=8 * heads * rows * keys * HEAD_DIM, bytes_accessed=heads * rows * 1024, transcendentals=0
        ),
        name="attend_past",
    )(slots, packed, past, sums, weight)


def pack_body(final, decode, out):
    half = final.shape[0] // 2
    taps, width = decode.shape
    share = 128 // width
    tall = out.shape[0] - half
    out[:half] = jnp.concatenate([final[:half], final[half:]], axis=1)
    parts = []
    for part in range(share):
        rows = decode[part * tall : min((part + 1) * tall, taps)]
        missing = tall - rows.shape[0]
        if missing:
            rows = jnp.concatenate([rows, jnp.zeros((missing, width), BF16)], axis=0)
        parts.append(rows)
    out[half:] = jnp.concatenate(parts, axis=1)


def packed_rows(final, decode, lat):
    share = 128 // decode.shape[1]
    per_part = -(-(decode.shape[0] // lat) // share) * lat
    return final.shape[0] // 2 + per_part


def pack(final, decode, lat):
    return pl.pallas_call(
        pack_body,
        in_specs=[WHOLE, WHOLE],
        out_specs=WHOLE,
        out_shape=jax.ShapeDtypeStruct((packed_rows(final, decode, lat), 128), BF16),
        name="pack",
    )(final, decode)


def unpack_body(table, gathered, final, decode):
    count = gathered.shape[0]
    depth = final.shape[0] // count
    half = depth // 2
    width = decode.shape[1] // count
    share = 128 // width
    tall = gathered.shape[1] - half
    tile = table[0]
    for device in range(count):
        block = gathered[table[1 + (device ^ tile)], :half]
        final[device * depth : device * depth + half] = block[:, : final.shape[1]]
        final[device * depth + half : (device + 1) * depth] = block[:, final.shape[1] :]
    for column in range(count // share):
        blocks = [
            gathered[table[1 + ((column * share + k) ^ tile)], half:] for k in range(share)
        ]
        for part in range(share):
            rows = min((part + 1) * tall, decode.shape[0]) - part * tall
            decode[part * tall : part * tall + rows, column * 128 : (column + 1) * 128] = jnp.concatenate(
                [b[:rows, part * width : (part + 1) * width] for b in blocks], axis=1
            )


def unpack(table, gathered, final_shape, decode_shape):
    return pl.pallas_call(
        unpack_body,
        in_specs=[SCALARS, WHOLE],
        out_specs=[WHOLE, WHOLE],
        out_shape=[jax.ShapeDtypeStruct(final_shape, BF16), jax.ShapeDtypeStruct(decode_shape, BF16)],
        name="unpack",
    )(table, gathered)


def tap_rows(frames, cells, width):
    stacks = []
    for shift_t in range(3):
        rows = []
        for frame in range(frames):
            source = frame + shift_t - 2
            rows.append(cells[source] if source >= 0 else jnp.zeros((width, cells[0].shape[1]), BF16))
        stacks.append(jnp.concatenate(rows, axis=0))
    return stacks


def shifted(wide, frame, width, lat):
    chunks = []
    for chunk in range(wide.shape[1]):
        lane = lax.broadcasted_iota(jnp.int32, (width, 128), 1) + 128 * chunk
        shift = (lane // lat) % 3
        near = jnp.where(shift == 1, wide[frame, chunk, 8 : 8 + width], wide[frame, chunk, 9 : 9 + width])
        chunks.append(jnp.where(shift == 0, wide[frame, chunk, 7 : 7 + width], near).astype(BF16))
    return jnp.concatenate(chunks, axis=1)


def inner_body(lat, predicted, kernel, features, edges, wide, done, sems):
    frames, patch_rows, patches, values = predicted.shape
    tall, broad = 2 * patch_rows, 2 * patches
    span = 3 * lat
    chunks = wide.shape[1]
    lanes = 128 * chunks
    wide[:, :, 0:8] = jnp.zeros((frames, chunks, 8, 128), F32)
    wide[:, :, 8 + broad :] = jnp.zeros((frames, chunks, 8, 128), F32)
    source = lax.broadcasted_iota(jnp.int32, (values, lanes), 0)
    target = lax.broadcasted_iota(jnp.int32, (values, lanes), 1)
    for side in range(2):
        picks = []
        for r in range(patch_rows):
            upper = target // span - 2 * r
            wanted = (upper >= 0) & (upper < 2) & (source == upper * 2 * lat + side * lat + target % lat)
            picks.append(jnp.where(wanted, 1.0, 0.0).astype(BF16))
        for frame in range(frames):
            cells = jnp.zeros((patches, lanes), F32)
            for r in range(patch_rows):
                cells += jnp.dot(predicted[frame, r], picks[r], preferred_element_type=F32)
            for chunk in range(chunks):
                wide[frame, chunk, pl.ds(8 + side, patches, stride=2), :] = cells[:, 128 * chunk : 128 * (chunk + 1)]
    stacks = tap_rows(frames, [shifted(wide, f, broad, lat) for f in range(frames)], broad)
    copies = []
    for row in list(range(1, tall - 1)) + [0, tall - 1]:
        first, last = max(row - 1, 0), min(row + 1, tall - 1)
        total = jnp.zeros((frames * broad, kernel.shape[1]), F32)
        for shift_t in range(3):
            start = (3 * shift_t + first - (row - 1)) * span
            total += jnp.dot(
                stacks[shift_t][:, first * span : (last + 1) * span],
                kernel[start : start + (last + 1 - first) * span],
                preferred_element_type=F32,
            )
        if 0 < row < tall - 1:
            done[row - 1] = total.astype(BF16).reshape(done.shape[1:])
            copy = pltpu.make_async_copy(done.at[row - 1], features.at[:, row], sems.at[row - 1])
            copy.start()
            copies.append(copy)
        else:
            edges[0 if row == 0 else 1] = total
    for copy in copies:
        copy.wait()


def convolve_inner(predicted, kernel):
    frames, patch_rows, patches, values = predicted.shape
    lat = values // 4
    tall, broad = 2 * patch_rows, 2 * patches
    channels = kernel.shape[1]
    lanes = -(-tall * 3 * lat // 128) * 128
    return pl.pallas_call(
        functools.partial(inner_body, lat),
        in_specs=[WHOLE, WHOLE],
        out_specs=[pl.BlockSpec(memory_space=pl.ANY), WHOLE],
        out_shape=[
            jax.ShapeDtypeStruct((frames, tall, broad, channels), BF16),
            jax.ShapeDtypeStruct((2, frames * broad, channels), F32),
        ],
        scratch_shapes=[
            pltpu.VMEM((frames, lanes // 128, broad + 16, 128), F32),
            pltpu.VMEM((tall - 2, frames, broad, channels), BF16),
            pltpu.SemaphoreType.DMA((tall - 2,)),
        ],
        compiler_params=params(16),
        cost_estimate=pl.CostEstimate(
            flops=2 * frames * tall * broad * 27 * lat * channels,
            bytes_accessed=2 * frames * tall * broad * channels,
            transcendentals=0,
        ),
        name="convolve_inner",
    )(predicted, kernel)


def outer_body(lat, above, below, kernel, edges, given, features, wide, done, sems):
    frames, patches, values = above.shape
    broad = 2 * patches
    tall = features.shape[1]
    span = 3 * lat
    chunks = wide.shape[2]
    lanes = 128 * chunks
    source = lax.broadcasted_iota(jnp.int32, (values, lanes), 0)
    target = lax.broadcasted_iota(jnp.int32, (values, lanes), 1)
    lane = lax.broadcasted_iota(jnp.int32, (broad, lanes), 1)
    copies = []
    for edge, cells in enumerate((above, below)):
        wide[edge, :, :, 0:8] = jnp.zeros((frames, chunks, 8, 128), F32)
        wide[edge, :, :, 8 + broad :] = jnp.zeros((frames, chunks, 8, 128), F32)
        for side in range(2):
            wanted = (source == (1 - edge) * 2 * lat + side * lat + target % lat) & (target < 3 * span)
            pick = jnp.where(wanted, 1.0, 0.0).astype(BF16)
            for frame in range(frames):
                spread = jnp.dot(cells[frame], pick, preferred_element_type=F32)
                for chunk in range(chunks):
                    wide[edge, frame, chunk, pl.ds(8 + side, patches, stride=2), :] = spread[
                        :, 128 * chunk : 128 * (chunk + 1)
                    ]
        ready = [shifted(wide.at[edge], f, broad, lat) for f in range(frames)]
        rows = []
        for frame in range(frames):
            taps = jnp.zeros((broad, lanes), BF16)
            for shift_t in range(3):
                if frame + shift_t - 2 >= 0:
                    taps = jnp.where(lane // span == shift_t, ready[frame + shift_t - 2], taps)
            rows.append(taps)
        shift_y = 2 * edge
        panel = jnp.concatenate(
            [kernel[(3 * t + shift_y) * span : (3 * t + shift_y + 1) * span] for t in range(3)], axis=0
        )
        total = edges[edge] + jnp.dot(
            jnp.concatenate(rows, axis=0)[:, : 3 * span], panel, preferred_element_type=F32
        )
        done[edge] = total.astype(BF16).reshape(done.shape[1:])
        copy = pltpu.make_async_copy(done.at[edge], features.at[:, edge * (tall - 1)], sems.at[edge])
        copy.start()
        copies.append(copy)
    for copy in copies:
        copy.wait()


def convolve_outer(above, below, kernel, edges, features):
    frames, patches, values = above.shape
    lat = values // 4
    broad = 2 * patches
    channels = kernel.shape[1]
    lanes = -(-9 * lat // 128) * 128
    anywhere = pl.BlockSpec(memory_space=pl.ANY)
    return pl.pallas_call(
        functools.partial(outer_body, lat),
        in_specs=[WHOLE, WHOLE, WHOLE, WHOLE, anywhere],
        out_specs=anywhere,
        out_shape=jax.ShapeDtypeStruct(features.shape, BF16),
        input_output_aliases={4: 0},
        scratch_shapes=[
            pltpu.VMEM((2, frames, lanes // 128, broad + 16, 128), F32),
            pltpu.VMEM((2, frames, broad, channels), BF16),
            pltpu.SemaphoreType.DMA((2,)),
        ],
        compiler_params=params(16),
        name="convolve_outer",
    )(above, below, kernel, edges, features)


def exchange(value, offset):
    count = lax.axis_size("seq")
    return lax.ppermute(value, "seq", [(i, i ^ offset) for i in range(count)])


def places(order):
    return [order.index(k) for k in range(len(order))]


def gather_by_doubling(shard, bits):
    held, order = shard, [0]
    for bit in bits:
        held = jnp.concatenate([held, exchange(held, bit)], axis=0)
        order = order + [o ^ bit for o in order]
    return held, order


def local(queries, own_kv, past_kv, block_home, block_list, list_len, final_weight, decoder_weight):
    frames, patch_rows, patches, width = queries.shape
    tokens = frames * patch_rows * patches
    count = lax.axis_size("seq")
    assert count & (count - 1) == 0
    blocks_here = past_kv.shape[0]
    lat = final_weight.shape[1] // 4
    me = lax.axis_index("seq").astype(jnp.int32).reshape(1)
    bits = [1 << k for k in reversed(range(count.bit_length() - 1))]
    small = count == 16 and decoder_weight.shape[1] * 4 == 128 and final_weight.shape[0] % 32 == 0
    if small:
        far = [4, 8, 12]
        panels = pack(final_weight, decoder_weight, lat)[None]
        arrived = [exchange(past_kv, k) for k in far]
        panels = jnp.concatenate([panels, exchange(panels, 2)], axis=0)
        past = jnp.concatenate([past_kv] + arrived, axis=0)
        past = jnp.concatenate([past, exchange(past, 2)], axis=0)
        past = jnp.concatenate([past, exchange(past, 1)], axis=0)
        order = [0] + far
        order = order + [o ^ 2 for o in order]
        order = order + [o ^ 1 for o in order]
        panels = jnp.concatenate([panels] + [exchange(panels, k) for k in far], axis=0)
        panels = jnp.concatenate([panels, exchange(panels, 1)], axis=0)
        panel_order = [k ^ x for k in [0] + far for x in (0, 2)]
        panel_order = panel_order + [o ^ 1 for o in panel_order]
        panel_table = jnp.concatenate([me, jnp.array(places(panel_order), jnp.int32)])
        final, decode = unpack(
            panel_table,
            panels,
            (final_weight.shape[0] * count, final_weight.shape[1]),
            (decoder_weight.shape[0], decoder_weight.shape[1] * count),
        )
    else:
        past, order = gather_by_doubling(past_kv, bits)
        final = lax.all_gather(final_weight, "seq", axis=0, tiled=True)
        decode = lax.all_gather(decoder_weight, "seq", axis=1, tiled=True)
    table = jnp.concatenate([me, jnp.array(places(order), jnp.int32)])
    slots = find_slots(table, block_home, block_list, list_len, blocks_here)
    packed, sums = attend_own(queries.reshape(tokens, width), own_kv.reshape(tokens, own_kv.shape[3]))
    predicted = attend_past(slots, packed, past, sums, final)
    predicted = predicted.reshape(frames, patch_rows, patches, predicted.shape[1])
    above = lax.ppermute(predicted[:, -1], "seq", [(i, i + 1) for i in range(count - 1)])
    below = lax.ppermute(predicted[:, 0], "seq", [(i + 1, i) for i in range(count - 1)])
    features, edges = convolve_inner(predicted, decode)
    return convolve_outer(above, below, decode, edges, features)


def solution(mesh):
    return jax.shard_map(
        local,
        mesh=mesh,
        in_specs=(
            P("groups", "seq", None, None),
            P("groups", "seq", None, None),
            P(("groups", "seq"), None, None),
            P("groups"),
            P("groups", None),
            P("groups"),
            P("seq", None),
            P(None, "seq"),
        ),
        out_specs=P("groups", "seq", None, None),
        check_vma=False,
    )
```

```python
import functools
import math

import jax
import jax.numpy as jnp
from jax import lax
from jax.experimental import pallas as pl
from jax.experimental.pallas import tpu as pltpu
from jax.sharding import PartitionSpec as P

HEADS = 24
KV_HEADS = 4
HEAD_DIM = 128
GROUP = HEADS // KV_HEADS
SCALE = math.log2(math.e) / math.sqrt(HEAD_DIM)
SAFE = 2.0**100
MIB = 1024 * 1024
WHOLE = pl.BlockSpec(memory_space=pltpu.VMEM)
SCALARS = pl.BlockSpec(memory_space=pltpu.SMEM)
BF16 = jnp.bfloat16
F32 = jnp.float32


def head_columns(index):
    return slice(index * HEAD_DIM, (index + 1) * HEAD_DIM)


def params(mib):
    return pltpu.CompilerParams(vmem_limit_bytes=mib * MIB)


def place_of(offset, turns):
    return sum(((offset >> bit) & 1) << to for bit, to in turns)


def own_body(turns, blocks_here, tile_ref, home, blocks, lens, queries, own, packed, sums, slots):
    tokens = queries.shape[0]
    tile = tile_ref[0]
    for place in range(slots.shape[0]):
        slots[place] = -1

    def find(entry, carry):
        stored = home[blocks[tile, entry]]
        slots[place_of((stored // blocks_here) ^ tile, turns)] = stored % blocks_here
        return carry

    lax.fori_loop(0, lens[tile], find, 0)

    def one(g, carry):
        def columns(index):
            return pl.ds(pl.multiple_of(index * HEAD_DIM, HEAD_DIM), HEAD_DIM)

        query = jnp.concatenate([queries[:, columns(g * GROUP + h)] for h in range(GROUP)], axis=0)
        value = jnp.concatenate(
            [own[:, columns(KV_HEADS + g)], jnp.ones((tokens, HEAD_DIM), BF16)], axis=1
        )
        score = lax.dot_general(
            query, own[:, columns(g)], (((1,), (1,)), ((), ())), preferred_element_type=F32
        )
        top = jnp.max(score, axis=1, keepdims=True)
        weights = jnp.exp2((score - top) * SCALE).astype(BF16)
        mixed = jnp.dot(weights, value, preferred_element_type=F32)
        total = mixed[:, HEAD_DIM:]
        sums[g] = mixed[:, :HEAD_DIM] / total
        level = top + jnp.log2(total) * (1.0 / SCALE)
        high = level.astype(BF16).astype(F32)
        middle = (level - high).astype(BF16).astype(F32)
        low = level - high - middle
        lane = lax.broadcasted_iota(jnp.int32, level.shape, 1)
        extra = jnp.where(lane == 0, high, jnp.where(lane == 1, middle, jnp.where(lane == 2, low, 0.0)))
        packed[g, :, :HEAD_DIM] = query
        packed[g, :, HEAD_DIM:] = extra.astype(BF16)
        return carry

    lax.fori_loop(0, KV_HEADS, one, 0)


def attend_own(tile, block_home, block_list, list_len, query_rows, own_rows, turns, blocks_here):
    tokens, width = query_rows.shape
    rows = GROUP * tokens
    return pl.pallas_call(
        functools.partial(own_body, turns, blocks_here),
        in_specs=[SCALARS] * 4 + [WHOLE, WHOLE],
        out_specs=[WHOLE, WHOLE, SCALARS],
        out_shape=[
            jax.ShapeDtypeStruct((KV_HEADS, rows, 2 * HEAD_DIM), BF16),
            jax.ShapeDtypeStruct((KV_HEADS, rows, HEAD_DIM), F32),
            jax.ShapeDtypeStruct((1 << len(turns),), jnp.int32),
        ],
        compiler_params=params(24),
        cost_estimate=pl.CostEstimate(
            flops=12 * tokens * tokens * width, bytes_accessed=10 * tokens * width, transcendentals=0
        ),
        name="attend_own",
    )(tile, block_home, block_list, list_len, query_rows, own_rows)


def past_body(sizes, slots, packed, sums, *refs):
    gathered, (out, keys, values, worst) = refs[: len(sizes)], refs[len(sizes) :]
    blocks_here = sum(ref.shape[0] for ref in gathered) // sum(sizes)
    block_tokens = gathered[0].shape[1]
    tokens = out.shape[0]
    lane = lax.broadcasted_iota(jnp.int32, (block_tokens, HEAD_DIM), 1)
    minus = jnp.where(lane < 3, -1.0, 0.0)
    zero = jnp.zeros((block_tokens, HEAD_DIM), BF16)
    homes = [(ref, k) for ref, size in zip(gathered, sizes) for k in range(size)]
    for place, (ref, k) in enumerate(homes):
        slot = slots[place]
        listed = slot >= 0
        block = ref[k * blocks_here + jnp.maximum(slot, 0)]
        live = jnp.where(listed, 1.0, 0.0)
        level = (minus * live).astype(BF16)
        counted = jnp.full((block_tokens, HEAD_DIM), live, F32).astype(BF16)
        rows = slice(place * block_tokens, (place + 1) * block_tokens)
        for g in range(KV_HEADS):
            keys[g, rows, :HEAD_DIM] = jnp.where(listed, block[:, head_columns(g)], zero)
            keys[g, rows, HEAD_DIM:] = level
            values[g, rows, :HEAD_DIM] = jnp.where(listed, block[:, head_columns(KV_HEADS + g)], zero)
            values[g, rows, HEAD_DIM:] = counted

    heads = GROUP if keys.shape[1] <= 512 else 1
    steps = KV_HEADS * GROUP // heads

    def over_steps(one, start):
        if heads == GROUP:
            for step in range(steps):
                start = one(step, start)
            return start
        return lax.fori_loop(0, steps, one, start)

    def place(step):
        if heads == GROUP:
            return step, slice(None)
        return step // GROUP, pl.ds(pl.multiple_of((step % GROUP) * tokens, tokens), tokens)

    def scores(g, rows):
        return SCALE * lax.dot_general(
            packed[g, rows], keys[g], (((1,), (1,)), ((), ())), preferred_element_type=F32
        )

    def emit(step, attended):
        attended = attended.astype(BF16)
        for h in range(heads):
            columns = (step * heads + h) * HEAD_DIM
            if heads == 1:
                columns = pl.multiple_of(columns, HEAD_DIM)
            out[:, pl.ds(columns, HEAD_DIM)] = attended[h * tokens : (h + 1) * tokens]

    def quick(step, largest):
        g, rows = place(step)
        weights = jnp.exp2(scores(g, rows)).astype(BF16)
        mixed = jnp.dot(weights, values[g], preferred_element_type=F32)
        below = mixed[:, HEAD_DIM:] + 1.0
        emit(step, (mixed[:, :HEAD_DIM] + sums[g, rows]) / below)
        return jnp.maximum(largest, jnp.max(below.reshape((-1,) + largest.shape), axis=0))

    worst[...] = over_steps(quick, jnp.zeros(worst.shape, F32))

    @pl.when(jnp.logical_not(jnp.max(worst[...]) < SAFE))
    def _():
        def careful(step, carry):
            g, rows = place(step)
            score = scores(g, rows)
            top = jnp.maximum(jnp.max(score, axis=1, keepdims=True), 0.0)
            weights = jnp.exp2(score - top).astype(BF16)
            mixed = jnp.dot(weights, values[g], preferred_element_type=F32)
            share = jnp.exp2(-top)
            emit(step, (mixed[:, :HEAD_DIM] + share * sums[g, rows]) / (mixed[:, HEAD_DIM:] + share))
            return carry

        over_steps(careful, 0)


def attend_past(slots, packed, sums, gathered, blocks_here):
    heads, rows, _ = packed.shape
    tokens = rows // GROUP
    sizes = [array.shape[0] // blocks_here for array in gathered]
    keys = sum(sizes) * gathered[0].shape[1]
    return pl.pallas_call(
        functools.partial(past_body, sizes),
        in_specs=[SCALARS] + [WHOLE] * (2 + len(gathered)),
        out_specs=WHOLE,
        out_shape=jax.ShapeDtypeStruct((tokens, HEADS * HEAD_DIM), BF16),
        scratch_shapes=[
            pltpu.VMEM((heads, keys, 2 * HEAD_DIM), BF16),
            pltpu.VMEM((heads, keys, 2 * HEAD_DIM), BF16),
            pltpu.VMEM((8, HEAD_DIM), F32),
        ],
        compiler_params=params(40 if keys > 256 else 24),
        cost_estimate=pl.CostEstimate(
            flops=8 * heads * rows * keys * HEAD_DIM, bytes_accessed=heads * rows * 1024, transcendentals=0
        ),
        name="attend_past",
    )(slots, packed, sums, *gathered)


def join_body(*refs):
    *parts, out = refs
    row = 0
    for part in parts:
        out[row : row + part.shape[0]] = part[...]
        row += part.shape[0]


def join(parts, name):
    rows = sum(part.shape[0] for part in parts)
    return pl.pallas_call(
        join_body,
        in_specs=[WHOLE] * len(parts),
        out_specs=WHOLE,
        out_shape=jax.ShapeDtypeStruct((rows,) + parts[0].shape[1:], BF16),
        name=name,
    )(*parts)


def pack_body(final, decode, out):
    half, depth = final.shape[0] // 2, final.shape[1]
    taps = decode.shape[1]
    blank = out.shape[2] - 2 * depth - taps
    out[0] = jnp.concatenate(
        [final[:half], final[half:], decode[...], jnp.zeros((half, blank), BF16)], axis=1
    )


def pack(final, decode):
    lanes = -(-(2 * final.shape[1] + decode.shape[1]) // 128) * 128
    return pl.pallas_call(
        pack_body,
        in_specs=[WHOLE, WHOLE],
        out_specs=WHOLE,
        out_shape=jax.ShapeDtypeStruct((1, decode.shape[0], lanes), BF16),
        name="pack",
    )(final, decode)


def project_body(depth, order, tile_ref, attended, *refs):
    *panels, out, staged, whole = refs
    place = 0
    half = staged.shape[1]
    for panel in panels:
        for k in range(panel.shape[0]):
            staged[tile_ref[0] ^ order[place]] = panel[k, :, : staged.shape[2]]
            place += 1
    for device in range(len(order)):
        for part in range(2):
            whole[part * half : (part + 1) * half, device * depth : (device + 1) * depth] = staged[
                device, :, part * depth : (part + 1) * depth
            ]
    out[...] = lax.dot_general(
        attended[...], whole[...], (((1,), (1,)), ((), ())), preferred_element_type=F32
    ).astype(BF16)


def project(tile, attended, panels, order, depth, columns):
    tokens, width = attended.shape
    lanes = -(-2 * depth // 128) * 128
    return pl.pallas_call(
        functools.partial(project_body, depth, order),
        in_specs=[SCALARS] + [WHOLE] * (1 + len(panels)),
        out_specs=WHOLE,
        out_shape=jax.ShapeDtypeStruct((tokens, columns), BF16),
        scratch_shapes=[
            pltpu.VMEM((len(order), columns // 2, lanes), BF16),
            pltpu.VMEM((columns, width), BF16),
        ],
        compiler_params=params(16),
        name="project",
    )(tile, attended, *panels)


def unpack_body(depth, order, tile_ref, *refs):
    *panels, out, staged = refs
    place = 0
    width = staged.shape[1]
    taps = out.shape[0]
    for panel in panels:
        for k in range(panel.shape[0]):
            staged[tile_ref[0] ^ order[place]] = panel[k]
            place += 1
    whole = jnp.concatenate([staged[d, :, 2 * depth : 2 * depth + taps] for d in range(len(order))], axis=0)
    out[...] = whole.T


def unpack(tile, panels, order, depth, taps):
    width, lanes = panels[0].shape[1:]
    return pl.pallas_call(
        functools.partial(unpack_body, depth, order),
        in_specs=[SCALARS] + [WHOLE] * len(panels),
        out_specs=WHOLE,
        out_shape=jax.ShapeDtypeStruct((taps, width * len(order)), BF16),
        scratch_shapes=[pltpu.VMEM((len(order), width, lanes), BF16)],
        compiler_params=params(16),
        name="unpack",
    )(tile, *panels)


def tap_rows(frames, cells, width):
    stacks = []
    for shift_t in range(3):
        rows = []
        for frame in range(frames):
            source = frame + shift_t - 2
            rows.append(cells[source] if source >= 0 else jnp.zeros((width, cells[0].shape[1]), BF16))
        stacks.append(jnp.concatenate(rows, axis=0))
    return stacks


def shifted(wide, frame, width, lat):
    chunks = []
    for chunk in range(wide.shape[1]):
        lane = lax.broadcasted_iota(jnp.int32, (width, 128), 1) + 128 * chunk
        shift = (lane // lat) % 3
        near = jnp.where(shift == 1, wide[frame, chunk, 8 : 8 + width], wide[frame, chunk, 9 : 9 + width])
        chunks.append(jnp.where(shift == 0, wide[frame, chunk, 7 : 7 + width], near).astype(BF16))
    return jnp.concatenate(chunks, axis=1)


def inner_body(lat, predicted, kernel, features, edges, wide, done, sems):
    frames, patch_rows, patches, values = predicted.shape
    tall, broad = 2 * patch_rows, 2 * patches
    span = 3 * lat
    chunks = wide.shape[1]
    lanes = 128 * chunks
    wide[:, :, 0:8] = jnp.zeros((frames, chunks, 8, 128), F32)
    wide[:, :, 8 + broad :] = jnp.zeros((frames, chunks, 8, 128), F32)
    source = lax.broadcasted_iota(jnp.int32, (values, lanes), 0)
    target = lax.broadcasted_iota(jnp.int32, (values, lanes), 1)
    for side in range(2):
        picks = []
        for r in range(patch_rows):
            upper = target // span - 2 * r
            wanted = (upper >= 0) & (upper < 2) & (source == upper * 2 * lat + side * lat + target % lat)
            picks.append(jnp.where(wanted, 1.0, 0.0).astype(BF16))
        for frame in range(frames):
            cells = jnp.zeros((patches, lanes), F32)
            for r in range(patch_rows):
                cells += jnp.dot(predicted[frame, r], picks[r], preferred_element_type=F32)
            for chunk in range(chunks):
                wide[frame, chunk, pl.ds(8 + side, patches, stride=2), :] = cells[:, 128 * chunk : 128 * (chunk + 1)]
    stacks = tap_rows(frames, [shifted(wide, f, broad, lat) for f in range(frames)], broad)
    copies = []
    for row in list(range(1, tall - 1)) + [0, tall - 1]:
        first, last = max(row - 1, 0), min(row + 1, tall - 1)
        total = jnp.zeros((frames * broad, kernel.shape[1]), F32)
        for shift_t in range(3):
            start = (3 * shift_t + first - (row - 1)) * span
            total += jnp.dot(
                stacks[shift_t][:, first * span : (last + 1) * span],
                kernel[start : start + (last + 1 - first) * span],
                preferred_element_type=F32,
            )
        if 0 < row < tall - 1:
            done[row - 1] = total.astype(BF16).reshape(done.shape[1:])
            copy = pltpu.make_async_copy(done.at[row - 1], features.at[:, row], sems.at[row - 1])
            copy.start()
            copies.append(copy)
        else:
            edges[0 if row == 0 else 1] = total
    for copy in copies:
        copy.wait()


def convolve_inner(predicted, kernel):
    frames, patch_rows, patches, values = predicted.shape
    lat = values // 4
    tall, broad = 2 * patch_rows, 2 * patches
    channels = kernel.shape[1]
    lanes = -(-tall * 3 * lat // 128) * 128
    return pl.pallas_call(
        functools.partial(inner_body, lat),
        in_specs=[WHOLE, WHOLE],
        out_specs=[pl.BlockSpec(memory_space=pl.ANY), WHOLE],
        out_shape=[
            jax.ShapeDtypeStruct((frames, tall, broad, channels), BF16),
            jax.ShapeDtypeStruct((2, frames * broad, channels), F32),
        ],
        scratch_shapes=[
            pltpu.VMEM((frames, lanes // 128, broad + 16, 128), F32),
            pltpu.VMEM((tall - 2, frames, broad, channels), BF16),
            pltpu.SemaphoreType.DMA((tall - 2,)),
        ],
        compiler_params=params(16),
        cost_estimate=pl.CostEstimate(
            flops=2 * frames * tall * broad * 27 * lat * channels,
            bytes_accessed=2 * frames * tall * broad * channels,
            transcendentals=0,
        ),
        name="convolve_inner",
    )(predicted, kernel)


def outer_body(lat, above, below, kernel, edges, given, features, wide, done, sems):
    frames, patches, values = above.shape
    broad = 2 * patches
    tall = features.shape[1]
    span = 3 * lat
    chunks = wide.shape[2]
    lanes = 128 * chunks
    source = lax.broadcasted_iota(jnp.int32, (values, lanes), 0)
    target = lax.broadcasted_iota(jnp.int32, (values, lanes), 1)
    lane = lax.broadcasted_iota(jnp.int32, (broad, lanes), 1)
    copies = []
    for edge, cells in enumerate((above, below)):
        wide[edge, :, :, 0:8] = jnp.zeros((frames, chunks, 8, 128), F32)
        wide[edge, :, :, 8 + broad :] = jnp.zeros((frames, chunks, 8, 128), F32)
        for side in range(2):
            wanted = (source == (1 - edge) * 2 * lat + side * lat + target % lat) & (target < 3 * span)
            pick = jnp.where(wanted, 1.0, 0.0).astype(BF16)
            for frame in range(frames):
                spread = jnp.dot(cells[frame], pick, preferred_element_type=F32)
                for chunk in range(chunks):
                    wide[edge, frame, chunk, pl.ds(8 + side, patches, stride=2), :] = spread[
                        :, 128 * chunk : 128 * (chunk + 1)
                    ]
        ready = [shifted(wide.at[edge], f, broad, lat) for f in range(frames)]
        rows = []
        for frame in range(frames):
            taps = jnp.zeros((broad, lanes), BF16)
            for shift_t in range(3):
                if frame + shift_t - 2 >= 0:
                    taps = jnp.where(lane // span == shift_t, ready[frame + shift_t - 2], taps)
            rows.append(taps)
        shift_y = 2 * edge
        panel = jnp.concatenate(
            [kernel[(3 * t + shift_y) * span : (3 * t + shift_y + 1) * span] for t in range(3)], axis=0
        )
        total = edges[edge] + jnp.dot(
            jnp.concatenate(rows, axis=0)[:, : 3 * span], panel, preferred_element_type=F32
        )
        done[edge] = total.astype(BF16).reshape(done.shape[1:])
        copy = pltpu.make_async_copy(done.at[edge], features.at[:, edge * (tall - 1)], sems.at[edge])
        copy.start()
        copies.append(copy)
    for copy in copies:
        copy.wait()


def convolve_outer(above, below, kernel, edges, features):
    frames, patches, values = above.shape
    lat = values // 4
    broad = 2 * patches
    channels = kernel.shape[1]
    lanes = -(-9 * lat // 128) * 128
    anywhere = pl.BlockSpec(memory_space=pl.ANY)
    return pl.pallas_call(
        functools.partial(outer_body, lat),
        in_specs=[WHOLE, WHOLE, WHOLE, WHOLE, anywhere],
        out_specs=anywhere,
        out_shape=jax.ShapeDtypeStruct(features.shape, BF16),
        input_output_aliases={4: 0},
        scratch_shapes=[
            pltpu.VMEM((2, frames, lanes // 128, broad + 16, 128), F32),
            pltpu.VMEM((2, frames, broad, channels), BF16),
            pltpu.SemaphoreType.DMA((2,)),
        ],
        compiler_params=params(16),
        name="convolve_outer",
    )(above, below, kernel, edges, features)


def exchange(value, offset):
    count = lax.axis_size("seq")
    return lax.ppermute(value, "seq", [(i, i ^ offset) for i in range(count)])


def local(queries, own_kv, past_kv, block_home, block_list, list_len, final_weight, decoder_weight):
    frames, patch_rows, patches, width = queries.shape
    tokens = frames * patch_rows * patches
    count = lax.axis_size("seq")
    assert count & (count - 1) == 0
    bits = count.bit_length() - 1
    blocks_here = past_kv.shape[0]
    depth, columns = final_weight.shape
    taps, panel_width = decoder_weight.shape
    tile = lax.axis_index("seq").astype(jnp.int32).reshape(1)
    query_rows = queries.reshape(tokens, width)
    own_rows = own_kv.reshape(tokens, own_kv.shape[3])
    if count == 16 and panel_width == columns // 2:
        far = [4, 8, 12]
        turns = [(2, 0), (3, 1), (1, 2), (0, 3)]
        steps = [exchange(past_kv, k) for k in far]
        panel = pack(final_weight.T, decoder_weight.T)
        pair = join([panel, exchange(panel, 2)], "join_panels")
        packed, sums, slots = attend_own(
            tile, block_home, block_list, list_len, query_rows, own_rows, turns, blocks_here
        )
        line = join([past_kv] + steps, "join_past")
        across = exchange(line, 2)
        gathered = [line, across, exchange(line, 1), exchange(across, 1)]
        panels = [pair] + [exchange(pair, k) for k in far]
        panels = panels + [exchange(p, 1) for p in panels]
        order = [k ^ x ^ c for c in (0, 1) for k in [0] + far for x in (0, 2)]
        attended = attend_past(slots, packed, sums, gathered, blocks_here)
        predicted = project(tile, attended, panels, order, depth, columns)
        decode = unpack(tile, panels, order, depth, taps)
    else:
        turns = [(bit, bits - 1 - bit) for bit in range(bits)]
        held = past_kv
        for bit in reversed(range(bits)):
            held = jnp.concatenate([held, exchange(held, 1 << bit)], axis=0)
        packed, sums, slots = attend_own(
            tile, block_home, block_list, list_len, query_rows, own_rows, turns, blocks_here
        )
        attended = attend_past(slots, packed, sums, [held], blocks_here)
        final = lax.all_gather(final_weight, "seq", axis=0, tiled=True)
        decode = lax.all_gather(decoder_weight, "seq", axis=1, tiled=True)
        predicted = jnp.dot(attended, final, preferred_element_type=F32).astype(BF16)
    predicted = predicted.reshape(frames, patch_rows, patches, columns)
    above = lax.ppermute(predicted[:, -1], "seq", [(i, i + 1) for i in range(count - 1)])
    below = lax.ppermute(predicted[:, 0], "seq", [(i + 1, i) for i in range(count - 1)])
    features, edges = convolve_inner(predicted, decode)
    return convolve_outer(above, below, decode, edges, features)


def solution(mesh):
    return jax.shard_map(
        local,
        mesh=mesh,
        in_specs=(
            P("groups", "seq", None, None),
            P("groups", "seq", None, None),
            P(("groups", "seq"), None, None),
            P("groups"),
            P("groups", None),
            P("groups"),
            P("seq", None),
            P(None, "seq"),
        ),
        out_specs=P("groups", "seq", None, None),
        check_vma=False,
    )
```

```python
import functools
import math

import jax
import jax.numpy as jnp
from jax import lax
from jax.experimental import pallas as pl
from jax.experimental.pallas import tpu as pltpu
from jax.sharding import PartitionSpec as P

HEADS = 24
KV_HEADS = 4
HEAD_DIM = 128
GROUP = HEADS // KV_HEADS
SCALE = math.log2(math.e) / math.sqrt(HEAD_DIM)
SAFE = 2.0**100
MIB = 1024 * 1024
WHOLE = pl.BlockSpec(memory_space=pltpu.VMEM)
ANYWHERE = pl.BlockSpec(memory_space=pl.ANY)
SCALARS = pl.BlockSpec(memory_space=pltpu.SMEM)
BF16 = jnp.bfloat16
F32 = jnp.float32


def head_columns(index):
    return slice(index * HEAD_DIM, (index + 1) * HEAD_DIM)


def params(mib):
    return pltpu.CompilerParams(vmem_limit_bytes=mib * MIB)


def place_of(offset, turns):
    return sum(((offset >> bit) & 1) << to for bit, to in turns)


def own_body(
    turns, blocks_here, tile_ref, home, blocks, lens, queries_from, own_from, packed, sums, slots,
    queries, own, sems
):
    tokens = queries.shape[0]
    tile = tile_ref[0]
    span = GROUP * HEAD_DIM
    copies = [pltpu.make_async_copy(own_from, own, sems.at[KV_HEADS])]
    for g in range(KV_HEADS):
        part = pl.ds(g * span, span)
        copies.append(pltpu.make_async_copy(queries_from.at[:, part], queries.at[:, part], sems.at[g]))
    for copy in copies:
        copy.start()
    for place in range(slots.shape[0]):
        slots[place] = -1

    def find(entry, carry):
        stored = home[blocks[tile, entry]]
        slots[place_of((stored // blocks_here) ^ tile, turns)] = stored % blocks_here
        return carry

    lax.fori_loop(0, lens[tile], find, 0)

    copies[0].wait()
    for g in range(KV_HEADS):
        copies[1 + g].wait()
        query = jnp.concatenate([queries[:, head_columns(g * GROUP + h)] for h in range(GROUP)], axis=0)
        value = jnp.concatenate(
            [own[:, head_columns(KV_HEADS + g)], jnp.ones((tokens, HEAD_DIM), BF16)], axis=1
        )
        score = lax.dot_general(
            query, own[:, head_columns(g)], (((1,), (1,)), ((), ())), preferred_element_type=F32
        )
        top = jnp.max(score, axis=1, keepdims=True)
        weights = jnp.exp2((score - top) * SCALE).astype(BF16)
        mixed = jnp.dot(weights, value, preferred_element_type=F32)
        total = mixed[:, HEAD_DIM:]
        sums[g] = mixed[:, :HEAD_DIM] / total
        level = top + jnp.log2(total) * (1.0 / SCALE)
        high = level.astype(BF16).astype(F32)
        middle = (level - high).astype(BF16).astype(F32)
        low = level - high - middle
        lane = lax.broadcasted_iota(jnp.int32, level.shape, 1)
        extra = jnp.where(lane == 0, high, jnp.where(lane == 1, middle, jnp.where(lane == 2, low, 0.0)))
        packed[g, :, :HEAD_DIM] = query
        packed[g, :, HEAD_DIM:] = extra.astype(BF16)


def attend_own(tile, block_home, block_list, list_len, query_rows, own_rows, turns, blocks_here):
    tokens, width = query_rows.shape
    rows = GROUP * tokens
    return pl.pallas_call(
        functools.partial(own_body, turns, blocks_here),
        in_specs=[SCALARS] * 4 + [ANYWHERE] * 2,
        out_specs=[WHOLE, WHOLE, SCALARS],
        out_shape=[
            jax.ShapeDtypeStruct((KV_HEADS, rows, 2 * HEAD_DIM), BF16),
            jax.ShapeDtypeStruct((KV_HEADS, rows, HEAD_DIM), F32),
            jax.ShapeDtypeStruct((1 << len(turns),), jnp.int32),
        ],
        scratch_shapes=[
            pltpu.VMEM(query_rows.shape, BF16),
            pltpu.VMEM(own_rows.shape, BF16),
            pltpu.SemaphoreType.DMA((KV_HEADS + 1,)),
        ],
        compiler_params=params(24),
        cost_estimate=pl.CostEstimate(
            flops=12 * tokens * tokens * width, bytes_accessed=10 * tokens * width, transcendentals=0
        ),
        name="attend_own",
    )(tile, block_home, block_list, list_len, query_rows, own_rows)


def past_body(sizes, slots, packed, sums, *refs):
    gathered, (out, keys, values, worst) = refs[: len(sizes)], refs[len(sizes) :]
    blocks_here = sum(ref.shape[0] for ref in gathered) // sum(sizes)
    block_tokens = gathered[0].shape[1]
    tokens = out.shape[0]
    lane = lax.broadcasted_iota(jnp.int32, (block_tokens, HEAD_DIM), 1)
    minus = jnp.where(lane < 3, -1.0, 0.0)
    zero = jnp.zeros((block_tokens, HEAD_DIM), BF16)
    homes = [(ref, k) for ref, size in zip(gathered, sizes) for k in range(size)]
    for place, (ref, k) in enumerate(homes):
        slot = slots[place]
        listed = slot >= 0
        block = ref[k * blocks_here + jnp.maximum(slot, 0)]
        live = jnp.where(listed, 1.0, 0.0)
        level = (minus * live).astype(BF16)
        counted = jnp.full((block_tokens, HEAD_DIM), live, F32).astype(BF16)
        rows = slice(place * block_tokens, (place + 1) * block_tokens)
        for g in range(KV_HEADS):
            keys[g, rows, :HEAD_DIM] = jnp.where(listed, block[:, head_columns(g)], zero)
            keys[g, rows, HEAD_DIM:] = level
            values[g, rows, :HEAD_DIM] = jnp.where(listed, block[:, head_columns(KV_HEADS + g)], zero)
            values[g, rows, HEAD_DIM:] = counted

    heads = GROUP if keys.shape[1] <= 512 else 1
    steps = KV_HEADS * GROUP // heads

    def over_steps(one, start):
        if heads == GROUP:
            for step in range(steps):
                start = one(step, start)
            return start
        return lax.fori_loop(0, steps, one, start)

    def place(step):
        if heads == GROUP:
            return step, slice(None)
        return step // GROUP, pl.ds(pl.multiple_of((step % GROUP) * tokens, tokens), tokens)

    def scores(g, rows):
        return SCALE * lax.dot_general(
            packed[g, rows], keys[g], (((1,), (1,)), ((), ())), preferred_element_type=F32
        )

    def emit(step, attended):
        attended = attended.astype(BF16)
        for h in range(heads):
            columns = (step * heads + h) * HEAD_DIM
            if heads == 1:
                columns = pl.multiple_of(columns, HEAD_DIM)
            out[:, pl.ds(columns, HEAD_DIM)] = attended[h * tokens : (h + 1) * tokens]

    def quick(step, largest):
        g, rows = place(step)
        weights = jnp.exp2(scores(g, rows)).astype(BF16)
        mixed = jnp.dot(weights, values[g], preferred_element_type=F32)
        below = mixed[:, HEAD_DIM:] + 1.0
        emit(step, (mixed[:, :HEAD_DIM] + sums[g, rows]) / below)
        return jnp.maximum(largest, jnp.max(below.reshape((-1,) + largest.shape), axis=0))

    worst[...] = over_steps(quick, jnp.zeros(worst.shape, F32))

    @pl.when(jnp.logical_not(jnp.max(worst[...]) < SAFE))
    def _():
        def careful(step, carry):
            g, rows = place(step)
            score = scores(g, rows)
            top = jnp.maximum(jnp.max(score, axis=1, keepdims=True), 0.0)
            weights = jnp.exp2(score - top).astype(BF16)
            mixed = jnp.dot(weights, values[g], preferred_element_type=F32)
            share = jnp.exp2(-top)
            emit(step, (mixed[:, :HEAD_DIM] + share * sums[g, rows]) / (mixed[:, HEAD_DIM:] + share))
            return carry

        over_steps(careful, 0)


def attend_past(slots, packed, sums, gathered, blocks_here):
    heads, rows, _ = packed.shape
    tokens = rows // GROUP
    sizes = [array.shape[0] // blocks_here for array in gathered]
    keys = sum(sizes) * gathered[0].shape[1]
    return pl.pallas_call(
        functools.partial(past_body, sizes),
        in_specs=[SCALARS] + [WHOLE] * (2 + len(gathered)),
        out_specs=WHOLE,
        out_shape=jax.ShapeDtypeStruct((tokens, HEADS * HEAD_DIM), BF16),
        scratch_shapes=[
            pltpu.VMEM((heads, keys, 2 * HEAD_DIM), BF16),
            pltpu.VMEM((heads, keys, 2 * HEAD_DIM), BF16),
            pltpu.VMEM((8, HEAD_DIM), F32),
        ],
        compiler_params=params(40 if keys > 256 else 24),
        cost_estimate=pl.CostEstimate(
            flops=8 * heads * rows * keys * HEAD_DIM, bytes_accessed=heads * rows * 1024, transcendentals=0
        ),
        name="attend_past",
    )(slots, packed, sums, *gathered)


def join_body(*refs):
    *parts, out = refs
    row = 0
    for part in parts:
        out[row : row + part.shape[0]] = part[...]
        row += part.shape[0]


def join(parts, name):
    rows = sum(part.shape[0] for part in parts)
    return pl.pallas_call(
        join_body,
        in_specs=[WHOLE] * len(parts),
        out_specs=WHOLE,
        out_shape=jax.ShapeDtypeStruct((rows,) + parts[0].shape[1:], BF16),
        compiler_params=params(4),
        name=name,
    )(*parts)


def pack_body(final, decode, out):
    half = final.shape[0] // 2
    blank = out.shape[2] - 2 * final.shape[1] - decode.shape[1]
    out[0] = jnp.concatenate(
        [final[:half], final[half:], decode[...], jnp.zeros((half, blank), BF16)], axis=1
    )


def pack(final, decode):
    lanes = -(-(2 * final.shape[1] + decode.shape[1]) // 128) * 128
    return pl.pallas_call(
        pack_body,
        in_specs=[WHOLE, WHOLE],
        out_specs=WHOLE,
        out_shape=jax.ShapeDtypeStruct((1, decode.shape[0], lanes), BF16),
        compiler_params=params(4),
        cost_estimate=pl.CostEstimate(flops=5 * 10**9, bytes_accessed=0, transcendentals=0),
        name="pack",
    )(final, decode)


def project_body(order, shape, depth, tile_ref, attended, *refs):
    *panels, out, to_pair, to_next, staged, whole = refs
    frames, patch_rows, patches = shape
    place = 0
    half = staged.shape[1]
    for panel in panels:
        for k in range(panel.shape[0]):
            staged[tile_ref[0] ^ order[place]] = panel[k, :, : staged.shape[2]]
            place += 1
    for device in range(len(order)):
        for part in range(2):
            whole[part * half : (part + 1) * half, device * depth : (device + 1) * depth] = staged[
                device, :, part * depth : (part + 1) * depth
            ]
    predicted = lax.dot_general(
        attended[...], whole[...], (((1,), (1,)), ((), ())), preferred_element_type=F32
    ).astype(BF16)
    out[...] = predicted
    even = tile_ref[0] % 2 == 0
    for frame in range(frames):
        rows = predicted[frame * patch_rows * patches : (frame + 1) * patch_rows * patches]
        first, last = rows[:patches], rows[(patch_rows - 1) * patches :]
        to_pair[frame] = jnp.where(even, last, first)
        to_next[frame] = jnp.where(even, first, last)


def project(tile, attended, panels, order, shape):
    tokens, width = attended.shape
    half = panels[0].shape[1]
    depth = width // len(order)
    border = jax.ShapeDtypeStruct((shape[0], shape[2], 2 * half), BF16)
    return pl.pallas_call(
        functools.partial(project_body, order, shape, depth),
        in_specs=[SCALARS] + [WHOLE] * (1 + len(panels)),
        out_specs=[WHOLE] * 3,
        out_shape=[jax.ShapeDtypeStruct((tokens, 2 * half), BF16), border, border],
        scratch_shapes=[
            pltpu.VMEM((len(order), half, -(-2 * depth // 128) * 128), BF16),
            pltpu.VMEM((2 * half, width), BF16),
        ],
        compiler_params=params(16),
        name="project",
    )(tile, attended, *panels)


def unpack_body(order, skip, tile_ref, *refs):
    *panels, out, staged = refs
    taps = out.shape[0]
    place = 0
    for panel in panels:
        for k in range(panel.shape[0]):
            staged[tile_ref[0] ^ order[place]] = panel[k]
            place += 1
    whole = [staged[device, :, skip : skip + taps] for device in range(len(order))]
    out[...] = jnp.concatenate(whole, axis=0).T


def unpack(tile, panels, order, skip, taps):
    width, lanes = panels[0].shape[1:]
    return pl.pallas_call(
        functools.partial(unpack_body, order, skip),
        in_specs=[SCALARS] + [WHOLE] * len(panels),
        out_specs=WHOLE,
        out_shape=jax.ShapeDtypeStruct((taps, width * len(order)), BF16),
        scratch_shapes=[pltpu.VMEM((len(order), width, lanes), BF16)],
        compiler_params=params(16),
        name="unpack",
    )(tile, *panels)


def tap_rows(frames, cells, width):
    stacks = []
    for shift_t in range(3):
        rows = []
        for frame in range(frames):
            source = frame + shift_t - 2
            rows.append(cells[source] if source >= 0 else jnp.zeros((width, cells[0].shape[1]), BF16))
        stacks.append(jnp.concatenate(rows, axis=0))
    return stacks


def shifted(wide, frame, width, lat):
    chunks = []
    for chunk in range(wide.shape[1]):
        lane = lax.broadcasted_iota(jnp.int32, (width, 128), 1) + 128 * chunk
        shift = (lane // lat) % 3
        near = jnp.where(shift == 1, wide[frame, chunk, 8 : 8 + width], wide[frame, chunk, 9 : 9 + width])
        chunks.append(jnp.where(shift == 0, wide[frame, chunk, 7 : 7 + width], near).astype(BF16))
    return jnp.concatenate(chunks, axis=1)


def inner_body(lat, predicted, kernel, features, edges, wide, done, sems):
    frames, patch_rows, patches, values = predicted.shape
    tall, broad = 2 * patch_rows, 2 * patches
    span = 3 * lat
    chunks = wide.shape[1]
    lanes = 128 * chunks
    wide[:, :, 0:8] = jnp.zeros((frames, chunks, 8, 128), F32)
    wide[:, :, 8 + broad :] = jnp.zeros((frames, chunks, 8, 128), F32)
    source = lax.broadcasted_iota(jnp.int32, (values, lanes), 0)
    target = lax.broadcasted_iota(jnp.int32, (values, lanes), 1)
    for side in range(2):
        picks = []
        for r in range(patch_rows):
            upper = target // span - 2 * r
            wanted = (upper >= 0) & (upper < 2) & (source == upper * 2 * lat + side * lat + target % lat)
            picks.append(jnp.where(wanted, 1.0, 0.0).astype(BF16))
        for frame in range(frames):
            cells = jnp.zeros((patches, lanes), F32)
            for r in range(patch_rows):
                cells += jnp.dot(predicted[frame, r], picks[r], preferred_element_type=F32)
            for chunk in range(chunks):
                wide[frame, chunk, pl.ds(8 + side, patches, stride=2), :] = cells[:, 128 * chunk : 128 * (chunk + 1)]
    stacks = tap_rows(frames, [shifted(wide, f, broad, lat) for f in range(frames)], broad)
    copies = []
    for row in list(range(1, tall - 1)) + [0, tall - 1]:
        first, last = max(row - 1, 0), min(row + 1, tall - 1)
        total = jnp.zeros((frames * broad, kernel.shape[1]), F32)
        for shift_t in range(3):
            start = (3 * shift_t + first - (row - 1)) * span
            total += jnp.dot(
                stacks[shift_t][:, first * span : (last + 1) * span],
                kernel[start : start + (last + 1 - first) * span],
                preferred_element_type=F32,
            )
        if 0 < row < tall - 1:
            done[row - 1] = total.astype(BF16).reshape(done.shape[1:])
            copy = pltpu.make_async_copy(done.at[row - 1], features.at[:, row], sems.at[row - 1])
            copy.start()
            copies.append(copy)
        else:
            edges[0 if row == 0 else 1] = total
    for copy in copies:
        copy.wait()


def convolve_inner(predicted, kernel):
    frames, patch_rows, patches, values = predicted.shape
    lat = values // 4
    tall, broad = 2 * patch_rows, 2 * patches
    channels = kernel.shape[1]
    lanes = -(-tall * 3 * lat // 128) * 128
    return pl.pallas_call(
        functools.partial(inner_body, lat),
        in_specs=[WHOLE, WHOLE],
        out_specs=[ANYWHERE, WHOLE],
        out_shape=[
            jax.ShapeDtypeStruct((frames, tall, broad, channels), BF16),
            jax.ShapeDtypeStruct((2, frames * broad, channels), F32),
        ],
        scratch_shapes=[
            pltpu.VMEM((frames, lanes // 128, broad + 16, 128), F32),
            pltpu.VMEM((tall - 2, frames, broad, channels), BF16),
            pltpu.SemaphoreType.DMA((tall - 2,)),
        ],
        compiler_params=params(16),
        cost_estimate=pl.CostEstimate(
            flops=2 * frames * tall * broad * 27 * lat * channels,
            bytes_accessed=2 * frames * tall * broad * channels,
            transcendentals=0,
        ),
        name="convolve_inner",
    )(predicted, kernel)


def outer_body(lat, tile_ref, from_pair, from_next, kernel, edges, given, features, wide, done, sems):
    frames, patches, values = from_pair.shape
    even = tile_ref[0] % 2 == 0
    broad = 2 * patches
    tall = features.shape[1]
    span = 3 * lat
    chunks = wide.shape[2]
    lanes = 128 * chunks
    source = lax.broadcasted_iota(jnp.int32, (values, lanes), 0)
    target = lax.broadcasted_iota(jnp.int32, (values, lanes), 1)
    lane = lax.broadcasted_iota(jnp.int32, (broad, lanes), 1)
    copies = []
    for edge in range(2):
        cells = [
            jnp.where(even == (edge == 0), from_next[frame], from_pair[frame]) for frame in range(frames)
        ]
        wide[edge, :, :, 0:8] = jnp.zeros((frames, chunks, 8, 128), F32)
        wide[edge, :, :, 8 + broad :] = jnp.zeros((frames, chunks, 8, 128), F32)
        for side in range(2):
            wanted = (source == (1 - edge) * 2 * lat + side * lat + target % lat) & (target < 3 * span)
            pick = jnp.where(wanted, 1.0, 0.0).astype(BF16)
            for frame in range(frames):
                spread = jnp.dot(cells[frame], pick, preferred_element_type=F32)
                for chunk in range(chunks):
                    wide[edge, frame, chunk, pl.ds(8 + side, patches, stride=2), :] = spread[
                        :, 128 * chunk : 128 * (chunk + 1)
                    ]
        ready = [shifted(wide.at[edge], f, broad, lat) for f in range(frames)]
        rows = []
        for frame in range(frames):
            taps = jnp.zeros((broad, lanes), BF16)
            for shift_t in range(3):
                if frame + shift_t - 2 >= 0:
                    taps = jnp.where(lane // span == shift_t, ready[frame + shift_t - 2], taps)
            rows.append(taps)
        shift_y = 2 * edge
        panel = jnp.concatenate(
            [kernel[(3 * t + shift_y) * span : (3 * t + shift_y + 1) * span] for t in range(3)], axis=0
        )
        total = edges[edge] + jnp.dot(
            jnp.concatenate(rows, axis=0)[:, : 3 * span], panel, preferred_element_type=F32
        )
        done[edge] = total.astype(BF16).reshape(done.shape[1:])
        copy = pltpu.make_async_copy(done.at[edge], features.at[:, edge * (tall - 1)], sems.at[edge])
        copy.start()
        copies.append(copy)
    for copy in copies:
        copy.wait()


def convolve_outer(tile, from_pair, from_next, kernel, edges, features):
    frames, patches, values = from_pair.shape
    lat = values // 4
    broad = 2 * patches
    channels = kernel.shape[1]
    lanes = -(-9 * lat // 128) * 128
    return pl.pallas_call(
        functools.partial(outer_body, lat),
        in_specs=[SCALARS] + [WHOLE] * 4 + [ANYWHERE],
        out_specs=ANYWHERE,
        out_shape=jax.ShapeDtypeStruct(features.shape, BF16),
        input_output_aliases={5: 0},
        scratch_shapes=[
            pltpu.VMEM((2, frames, lanes // 128, broad + 16, 128), F32),
            pltpu.VMEM((2, frames, broad, channels), BF16),
            pltpu.SemaphoreType.DMA((2,)),
        ],
        compiler_params=params(16),
        name="convolve_outer",
    )(tile, from_pair, from_next, kernel, edges, features)


def exchange(value, offset):
    count = lax.axis_size("seq")
    return lax.ppermute(value, "seq", [(i, i ^ offset) for i in range(count)])


def local(queries, own_kv, past_kv, block_home, block_list, list_len, final_weight, decoder_weight):
    frames, patch_rows, patches, width = queries.shape
    tokens = frames * patch_rows * patches
    count = lax.axis_size("seq")
    assert count & (count - 1) == 0
    bits = count.bit_length() - 1
    blocks_here = past_kv.shape[0]
    columns = final_weight.shape[1]
    tile = lax.axis_index("seq").astype(jnp.int32).reshape(1)
    query_rows = queries.reshape(tokens, width)
    own_rows = own_kv.reshape(tokens, own_kv.shape[3])
    shape = (frames, patch_rows, patches)
    if count == 16 and columns == 2 * decoder_weight.shape[1]:
        far = [4, 8, 12]
        turns = [(2, 0), (3, 1), (1, 2), (0, 3)]
        line = [exchange(past_kv, k) for k in far]
        panel = pack(final_weight.T, decoder_weight.T)
        panel_across = exchange(panel, 2)
        packed, sums, slots = attend_own(
            tile, block_home, block_list, list_len, query_rows, own_rows, turns, blocks_here
        )
        *line, panel_across, slots = lax.optimization_barrier((*line, panel_across, slots))
        line = join([past_kv] + line, "join_line")
        across = exchange(line, 2)
        beside = exchange(line, 1)
        panels = join([panel, panel_across], "join_pair")
        order = [k ^ x for k in [0] + far for x in (0, 2)]
        order = order + [k ^ 1 for k in order]
        panels_far = [exchange(panels, far[0])]
        panels, across, beside = lax.optimization_barrier((panels, across, beside))
        panels_far = panels_far + [exchange(panels, k) for k in far[1:]]
        gathered = [line, across, beside, exchange(across, 1)]
        attended = attend_past(slots, packed, sums, gathered, blocks_here)
        *panels_far, attended = lax.optimization_barrier((*panels_far, attended))
        panels = join([panels] + panels_far, "join_panels")
        panels = [panels, exchange(panels, 1)]
        predicted, to_pair, to_next = project(tile, attended, panels, order, shape)
        decode = unpack(tile, panels, order, 2 * final_weight.shape[0], decoder_weight.shape[0])
    else:
        turns = [(bit, bits - 1 - bit) for bit in range(bits)]
        held = past_kv
        for bit in reversed(range(bits)):
            held = jnp.concatenate([held, exchange(held, 1 << bit)], axis=0)
        packed, sums, slots = attend_own(
            tile, block_home, block_list, list_len, query_rows, own_rows, turns, blocks_here
        )
        attended = attend_past(slots, packed, sums, [held], blocks_here)
        final = lax.all_gather(final_weight, "seq", axis=0, tiled=True)
        decode = lax.all_gather(decoder_weight, "seq", axis=1, tiled=True)
        predicted = jnp.dot(attended, final, preferred_element_type=F32).astype(BF16)
        rows = predicted.reshape(shape + (columns,))
        even = tile[0] % 2 == 0
        to_pair = jnp.where(even, rows[:, -1], rows[:, 0])
        to_next = jnp.where(even, rows[:, 0], rows[:, -1])
    predicted = predicted.reshape(shape + (columns,))
    from_pair = exchange(to_pair, 1)
    swaps = [(i, i + 1) for i in range(1, count - 1, 2)] + [(i + 1, i) for i in range(1, count - 1, 2)]
    from_next = lax.ppermute(to_next, "seq", swaps)
    features, edges = convolve_inner(predicted, decode)
    return convolve_outer(tile, from_pair, from_next, decode, edges, features)


def solution(mesh):
    return jax.shard_map(
        local,
        mesh=mesh,
        in_specs=(
            P("groups", "seq", None, None),
            P("groups", "seq", None, None),
            P(("groups", "seq"), None, None),
            P("groups"),
            P("groups", None),
            P("groups"),
            P("seq", None),
            P(None, "seq"),
        ),
        out_specs=P("groups", "seq", None, None),
        check_vma=False,
    )
```

```python
import functools
import math

import jax
import jax.numpy as jnp
from jax import lax
from jax.experimental import pallas as pl
from jax.experimental.pallas import tpu as pltpu
from jax.sharding import PartitionSpec as P

HEADS = 24
KV_HEADS = 4
HEAD_DIM = 128
GROUP = HEADS // KV_HEADS
SCALE = math.log2(math.e) / math.sqrt(HEAD_DIM)
SAFE = 2.0**100
MIB = 1024 * 1024
WHOLE = pl.BlockSpec(memory_space=pltpu.VMEM)
ANYWHERE = pl.BlockSpec(memory_space=pl.ANY)
SCALARS = pl.BlockSpec(memory_space=pltpu.SMEM)
BF16 = jnp.bfloat16
F32 = jnp.float32


def head_columns(index):
    return slice(index * HEAD_DIM, (index + 1) * HEAD_DIM)


def params(mib):
    return pltpu.CompilerParams(vmem_limit_bytes=mib * MIB)


def place_of(offset, turns):
    return sum(((offset >> bit) & 1) << to for bit, to in turns)


def own_body(turns, blocks_here, groups, tile_ref, home, blocks, lens, queries, own, packed, sums, slots):
    tokens = queries.shape[0]
    tile = tile_ref[0]
    for place in range(slots.shape[0]):
        slots[place] = -1

    def find(entry, carry):
        stored = home[blocks[tile, entry]]
        slots[place_of((stored // blocks_here) ^ tile, turns)] = stored % blocks_here
        return carry

    if groups[-1] == KV_HEADS - 1:
        lax.fori_loop(0, lens[tile], find, 0)
    for index, g in enumerate(groups):
        query = jnp.concatenate([queries[:, head_columns(g * GROUP + h)] for h in range(GROUP)], axis=0)
        value = jnp.concatenate(
            [own[:, head_columns(KV_HEADS + g)], jnp.ones((tokens, HEAD_DIM), BF16)], axis=1
        )
        score = lax.dot_general(
            query, own[:, head_columns(g)], (((1,), (1,)), ((), ())), preferred_element_type=F32
        )
        top = jnp.max(score, axis=1, keepdims=True)
        weights = jnp.exp2((score - top) * SCALE).astype(BF16)
        mixed = jnp.dot(weights, value, preferred_element_type=F32)
        total = mixed[:, HEAD_DIM:]
        sums[index] = mixed[:, :HEAD_DIM] / total
        level = top + jnp.log2(total) * (1.0 / SCALE)
        high = level.astype(BF16).astype(F32)
        middle = (level - high).astype(BF16).astype(F32)
        low = level - high - middle
        lane = lax.broadcasted_iota(jnp.int32, level.shape, 1)
        extra = jnp.where(lane == 0, high, jnp.where(lane == 1, middle, jnp.where(lane == 2, low, 0.0)))
        packed[index, :, :HEAD_DIM] = query
        packed[index, :, HEAD_DIM:] = extra.astype(BF16)


def attend_own(groups, tile, block_home, block_list, list_len, query_rows, own_rows, turns, blocks_here):
    tokens, width = query_rows.shape
    rows = GROUP * tokens
    return pl.pallas_call(
        functools.partial(own_body, turns, blocks_here, groups),
        in_specs=[SCALARS] * 4 + [WHOLE] * 2,
        out_specs=[WHOLE, WHOLE, SCALARS],
        out_shape=[
            jax.ShapeDtypeStruct((len(groups), rows, 2 * HEAD_DIM), BF16),
            jax.ShapeDtypeStruct((len(groups), rows, HEAD_DIM), F32),
            jax.ShapeDtypeStruct((1 << len(turns),), jnp.int32),
        ],
        compiler_params=params(20),
        cost_estimate=pl.CostEstimate(
            flops=3 * len(groups) * tokens * tokens * width, bytes_accessed=0, transcendentals=0
        ),
        name="attend_own",
    )(tile, block_home, block_list, list_len, query_rows, own_rows)


def past_body(sizes, split, slots, *refs):
    packed, sums, refs = refs[:split], refs[split : 2 * split], refs[2 * split :]
    gathered, (out, keys, values, worst) = refs[: len(sizes)], refs[len(sizes) :]
    groups = KV_HEADS // split
    blocks_here = sum(ref.shape[0] for ref in gathered) // sum(sizes)
    block_tokens = gathered[0].shape[1]
    tokens = out.shape[0]
    lane = lax.broadcasted_iota(jnp.int32, (block_tokens, HEAD_DIM), 1)
    minus = jnp.where(lane < 3, -1.0, 0.0)
    zero = jnp.zeros((block_tokens, HEAD_DIM), BF16)
    homes = [(ref, k) for ref, size in zip(gathered, sizes) for k in range(size)]
    for place, (ref, k) in enumerate(homes):
        slot = slots[place]
        listed = slot >= 0
        block = ref[k * blocks_here + jnp.maximum(slot, 0)]
        live = jnp.where(listed, 1.0, 0.0)
        level = (minus * live).astype(BF16)
        counted = jnp.full((block_tokens, HEAD_DIM), live, F32).astype(BF16)
        rows = slice(place * block_tokens, (place + 1) * block_tokens)
        for g in range(KV_HEADS):
            keys[g, rows, :HEAD_DIM] = jnp.where(listed, block[:, head_columns(g)], zero)
            keys[g, rows, HEAD_DIM:] = level
            values[g, rows, :HEAD_DIM] = jnp.where(listed, block[:, head_columns(KV_HEADS + g)], zero)
            values[g, rows, HEAD_DIM:] = counted

    heads = GROUP if keys.shape[1] <= 512 else 1
    steps = KV_HEADS * GROUP // heads

    def over_steps(one, start):
        if heads == GROUP:
            for step in range(steps):
                start = one(step, start)
            return start
        return lax.fori_loop(0, steps, one, start)

    def place(step):
        if heads == GROUP:
            return step, slice(None)
        return step // GROUP, pl.ds(pl.multiple_of((step % GROUP) * tokens, tokens), tokens)

    def own_part(arrays, g, rows):
        if split == 1:
            return arrays[0][g, rows]
        return arrays[g // groups][g % groups, rows]

    def scores(g, rows):
        return SCALE * lax.dot_general(
            own_part(packed, g, rows), keys[g], (((1,), (1,)), ((), ())), preferred_element_type=F32
        )

    def emit(step, attended):
        attended = attended.astype(BF16)
        for h in range(heads):
            columns = (step * heads + h) * HEAD_DIM
            if heads == 1:
                columns = pl.multiple_of(columns, HEAD_DIM)
            out[:, pl.ds(columns, HEAD_DIM)] = attended[h * tokens : (h + 1) * tokens]

    def quick(step, largest):
        g, rows = place(step)
        weights = jnp.exp2(scores(g, rows)).astype(BF16)
        mixed = jnp.dot(weights, values[g], preferred_element_type=F32)
        below = mixed[:, HEAD_DIM:] + 1.0
        emit(step, (mixed[:, :HEAD_DIM] + own_part(sums, g, rows)) / below)
        return jnp.maximum(largest, jnp.max(below.reshape((-1,) + largest.shape), axis=0))

    worst[...] = over_steps(quick, jnp.zeros(worst.shape, F32))

    @pl.when(jnp.logical_not(jnp.max(worst[...]) < SAFE))
    def _():
        def careful(step, carry):
            g, rows = place(step)
            score = scores(g, rows)
            top = jnp.maximum(jnp.max(score, axis=1, keepdims=True), 0.0)
            weights = jnp.exp2(score - top).astype(BF16)
            mixed = jnp.dot(weights, values[g], preferred_element_type=F32)
            share = jnp.exp2(-top)
            joined = mixed[:, :HEAD_DIM] + share * own_part(sums, g, rows)
            emit(step, joined / (mixed[:, HEAD_DIM:] + share))
            return carry

        over_steps(careful, 0)


def attend_past(slots, packed, sums, gathered, blocks_here):
    heads = KV_HEADS
    rows = packed[0].shape[1]
    tokens = rows // GROUP
    sizes = [array.shape[0] // blocks_here for array in gathered]
    keys = sum(sizes) * gathered[0].shape[1]
    return pl.pallas_call(
        functools.partial(past_body, sizes, len(packed)),
        in_specs=[SCALARS] + [WHOLE] * (2 * len(packed) + len(gathered)),
        out_specs=WHOLE,
        out_shape=jax.ShapeDtypeStruct((tokens, HEADS * HEAD_DIM), BF16),
        scratch_shapes=[
            pltpu.VMEM((heads, keys, 2 * HEAD_DIM), BF16),
            pltpu.VMEM((heads, keys, 2 * HEAD_DIM), BF16),
            pltpu.VMEM((8, HEAD_DIM), F32),
        ],
        compiler_params=params(40 if keys > 256 else 24),
        cost_estimate=pl.CostEstimate(
            flops=8 * heads * rows * keys * HEAD_DIM, bytes_accessed=heads * rows * 1024, transcendentals=0
        ),
        name="attend_past",
    )(slots, *packed, *sums, *gathered)


def join_body(*refs):
    *parts, out = refs
    row = 0
    for part in parts:
        out[row : row + part.shape[0]] = part[...]
        row += part.shape[0]


def join(parts, name):
    rows = sum(part.shape[0] for part in parts)
    return pl.pallas_call(
        join_body,
        in_specs=[WHOLE] * len(parts),
        out_specs=WHOLE,
        out_shape=jax.ShapeDtypeStruct((rows,) + parts[0].shape[1:], BF16),
        compiler_params=params(4),
        name=name,
    )(*parts)


def pack_body(final, decode, final_across, decode_across, out):
    half = final.shape[0] // 2
    blank = out.shape[2] - 2 * final.shape[1] - decode.shape[1]
    for k, (left, right) in enumerate(((final, decode), (final_across, decode_across))):
        out[k] = jnp.concatenate(
            [left[:half], left[half:], right[...], jnp.zeros((half, blank), BF16)], axis=1
        )


def pack(final, decode, final_across, decode_across):
    lanes = -(-(2 * final.shape[1] + decode.shape[1]) // 128) * 128
    return pl.pallas_call(
        pack_body,
        in_specs=[WHOLE] * 4,
        out_specs=WHOLE,
        out_shape=jax.ShapeDtypeStruct((2, decode.shape[0], lanes), BF16),
        compiler_params=params(4),
        name="pack",
    )(final, decode, final_across, decode_across)


def project_body(order, shape, depth, tile_ref, attended, *refs):
    *panels, out, to_pair, to_next, staged, whole = refs
    frames, patch_rows, patches = shape
    place = 0
    half = staged.shape[1]
    for panel in panels:
        for k in range(panel.shape[0]):
            staged[tile_ref[0] ^ order[place]] = panel[k, :, : staged.shape[2]]
            place += 1
    for device in range(len(order)):
        for part in range(2):
            whole[part * half : (part + 1) * half, device * depth : (device + 1) * depth] = staged[
                device, :, part * depth : (part + 1) * depth
            ]
    predicted = lax.dot_general(
        attended[...], whole[...], (((1,), (1,)), ((), ())), preferred_element_type=F32
    ).astype(BF16)
    out[...] = predicted
    even = tile_ref[0] % 2 == 0
    for frame in range(frames):
        rows = predicted[frame * patch_rows * patches : (frame + 1) * patch_rows * patches]
        first, last = rows[:patches], rows[(patch_rows - 1) * patches :]
        to_pair[frame] = jnp.where(even, last, first)
        to_next[frame] = jnp.where(even, first, last)


def project(tile, attended, panels, order, shape):
    tokens, width = attended.shape
    half = panels[0].shape[1]
    depth = width // len(order)
    border = jax.ShapeDtypeStruct((shape[0], shape[2], 2 * half), BF16)
    return pl.pallas_call(
        functools.partial(project_body, order, shape, depth),
        in_specs=[SCALARS] + [WHOLE] * (1 + len(panels)),
        out_specs=[WHOLE] * 3,
        out_shape=[jax.ShapeDtypeStruct((tokens, 2 * half), BF16), border, border],
        scratch_shapes=[
            pltpu.VMEM((len(order), half, -(-2 * depth // 128) * 128), BF16),
            pltpu.VMEM((2 * half, width), BF16),
        ],
        compiler_params=params(16),
        name="project",
    )(tile, attended, *panels)


def unpack_body(order, skip, tile_ref, *refs):
    *panels, out, staged = refs
    taps = out.shape[0]
    place = 0
    for panel in panels:
        for k in range(panel.shape[0]):
            staged[tile_ref[0] ^ order[place]] = panel[k]
            place += 1
    whole = [staged[device, :, skip : skip + taps] for device in range(len(order))]
    out[...] = jnp.concatenate(whole, axis=0).T


def unpack(tile, panels, order, skip, taps):
    width, lanes = panels[0].shape[1:]
    return pl.pallas_call(
        functools.partial(unpack_body, order, skip),
        in_specs=[SCALARS] + [WHOLE] * len(panels),
        out_specs=WHOLE,
        out_shape=jax.ShapeDtypeStruct((taps, width * len(order)), BF16),
        scratch_shapes=[pltpu.VMEM((len(order), width, lanes), BF16)],
        compiler_params=params(16),
        name="unpack",
    )(tile, *panels)


def tap_rows(frames, cells, width):
    stacks = []
    for shift_t in range(3):
        rows = []
        for frame in range(frames):
            source = frame + shift_t - 2
            rows.append(cells[source] if source >= 0 else jnp.zeros((width, cells[0].shape[1]), BF16))
        stacks.append(jnp.concatenate(rows, axis=0))
    return stacks


def shifted(wide, frame, width, lat):
    chunks = []
    for chunk in range(wide.shape[1]):
        lane = lax.broadcasted_iota(jnp.int32, (width, 128), 1) + 128 * chunk
        shift = (lane // lat) % 3
        near = jnp.where(shift == 1, wide[frame, chunk, 8 : 8 + width], wide[frame, chunk, 9 : 9 + width])
        chunks.append(jnp.where(shift == 0, wide[frame, chunk, 7 : 7 + width], near).astype(BF16))
    return jnp.concatenate(chunks, axis=1)


def spread_body(lat, patch_rows, inner, outer):
    span = 3 * lat
    for side in range(2):
        source = lax.broadcasted_iota(jnp.int32, inner.shape[2:], 0)
        target = lax.broadcasted_iota(jnp.int32, inner.shape[2:], 1)
        for r in range(patch_rows):
            upper = target // span - 2 * r
            wanted = (upper >= 0) & (upper < 2) & (source == upper * 2 * lat + side * lat + target % lat)
            inner[side, r] = jnp.where(wanted, 1.0, 0.0).astype(BF16)
        source = lax.broadcasted_iota(jnp.int32, outer.shape[2:], 0)
        target = lax.broadcasted_iota(jnp.int32, outer.shape[2:], 1)
        for edge in range(2):
            wanted = source == (1 - edge) * 2 * lat + side * lat + target % lat
            wanted = wanted & (target < 3 * span)
            outer[edge, side] = jnp.where(wanted, 1.0, 0.0).astype(BF16)


def spreads(lat, patch_rows):
    tall = 2 * patch_rows
    return pl.pallas_call(
        functools.partial(spread_body, lat, patch_rows),
        out_specs=[WHOLE, WHOLE],
        out_shape=[
            jax.ShapeDtypeStruct((2, patch_rows, 4 * lat, -(-tall * 3 * lat // 128) * 128), BF16),
            jax.ShapeDtypeStruct((2, 2, 4 * lat, -(-9 * lat // 128) * 128), BF16),
        ],
        compiler_params=params(4),
        cost_estimate=pl.CostEstimate(flops=5 * 10**9, bytes_accessed=0, transcendentals=0),
        name="spreads",
    )()


def inner_body(lat, predicted, picks, kernel, features, edges, wide, done, sems):
    frames, patch_rows, patches, values = predicted.shape
    tall, broad = 2 * patch_rows, 2 * patches
    span = 3 * lat
    chunks = wide.shape[1]
    lanes = 128 * chunks
    wide[:, :, 0:8] = jnp.zeros((frames, chunks, 8, 128), F32)
    wide[:, :, 8 + broad :] = jnp.zeros((frames, chunks, 8, 128), F32)
    for side in range(2):
        for frame in range(frames):
            cells = jnp.zeros((patches, lanes), F32)
            for r in range(patch_rows):
                cells += jnp.dot(predicted[frame, r], picks[side, r], preferred_element_type=F32)
            for chunk in range(chunks):
                wide[frame, chunk, pl.ds(8 + side, patches, stride=2), :] = cells[:, 128 * chunk : 128 * (chunk + 1)]
    stacks = tap_rows(frames, [shifted(wide, f, broad, lat) for f in range(frames)], broad)
    copies = []
    for row in list(range(1, tall - 1)) + [0, tall - 1]:
        first, last = max(row - 1, 0), min(row + 1, tall - 1)
        total = jnp.zeros((frames * broad, kernel.shape[1]), F32)
        for shift_t in range(3):
            start = (3 * shift_t + first - (row - 1)) * span
            total += jnp.dot(
                stacks[shift_t][:, first * span : (last + 1) * span],
                kernel[start : start + (last + 1 - first) * span],
                preferred_element_type=F32,
            )
        if 0 < row < tall - 1:
            done[row - 1] = total.astype(BF16).reshape(done.shape[1:])
            copy = pltpu.make_async_copy(done.at[row - 1], features.at[:, row], sems.at[row - 1])
            copy.start()
            copies.append(copy)
        else:
            edges[0 if row == 0 else 1] = total
    for copy in copies:
        copy.wait()


def convolve_inner(predicted, picks, kernel):
    frames, patch_rows, patches, values = predicted.shape
    lat = values // 4
    tall, broad = 2 * patch_rows, 2 * patches
    channels = kernel.shape[1]
    lanes = -(-tall * 3 * lat // 128) * 128
    return pl.pallas_call(
        functools.partial(inner_body, lat),
        in_specs=[WHOLE] * 3,
        out_specs=[ANYWHERE, WHOLE],
        out_shape=[
            jax.ShapeDtypeStruct((frames, tall, broad, channels), BF16),
            jax.ShapeDtypeStruct((2, frames * broad, channels), F32),
        ],
        scratch_shapes=[
            pltpu.VMEM((frames, lanes // 128, broad + 16, 128), F32),
            pltpu.VMEM((tall - 2, frames, broad, channels), BF16),
            pltpu.SemaphoreType.DMA((tall - 2,)),
        ],
        compiler_params=params(16),
        cost_estimate=pl.CostEstimate(
            flops=2 * frames * tall * broad * 27 * lat * channels,
            bytes_accessed=2 * frames * tall * broad * channels,
            transcendentals=0,
        ),
        name="convolve_inner",
    )(predicted, picks, kernel)


def outer_body(lat, tile_ref, from_pair, from_next, picks, kernel, edges, given, features, wide, done, sems):
    frames, patches, values = from_pair.shape
    even = tile_ref[0] % 2 == 0
    broad = 2 * patches
    tall = features.shape[1]
    span = 3 * lat
    chunks = wide.shape[2]
    lanes = 128 * chunks
    lane = lax.broadcasted_iota(jnp.int32, (broad, lanes), 1)
    copies = []
    for edge in range(2):
        cells = [
            jnp.where(even == (edge == 0), from_next[frame], from_pair[frame]) for frame in range(frames)
        ]
        wide[edge, :, :, 0:8] = jnp.zeros((frames, chunks, 8, 128), F32)
        wide[edge, :, :, 8 + broad :] = jnp.zeros((frames, chunks, 8, 128), F32)
        for side in range(2):
            for frame in range(frames):
                spread = jnp.dot(cells[frame], picks[edge, side], preferred_element_type=F32)
                for chunk in range(chunks):
                    wide[edge, frame, chunk, pl.ds(8 + side, patches, stride=2), :] = spread[
                        :, 128 * chunk : 128 * (chunk + 1)
                    ]
        ready = [shifted(wide.at[edge], f, broad, lat) for f in range(frames)]
        rows = []
        for frame in range(frames):
            taps = jnp.zeros((broad, lanes), BF16)
            for shift_t in range(3):
                if frame + shift_t - 2 >= 0:
                    taps = jnp.where(lane // span == shift_t, ready[frame + shift_t - 2], taps)
            rows.append(taps)
        shift_y = 2 * edge
        panel = jnp.concatenate(
            [kernel[(3 * t + shift_y) * span : (3 * t + shift_y + 1) * span] for t in range(3)], axis=0
        )
        total = edges[edge] + jnp.dot(
            jnp.concatenate(rows, axis=0)[:, : 3 * span], panel, preferred_element_type=F32
        )
        done[edge] = total.astype(BF16).reshape(done.shape[1:])
        copy = pltpu.make_async_copy(done.at[edge], features.at[:, edge * (tall - 1)], sems.at[edge])
        copy.start()
        copies.append(copy)
    for copy in copies:
        copy.wait()


def convolve_outer(tile, from_pair, from_next, picks, kernel, edges, features):
    frames, patches, values = from_pair.shape
    lat = values // 4
    broad = 2 * patches
    channels = kernel.shape[1]
    lanes = -(-9 * lat // 128) * 128
    return pl.pallas_call(
        functools.partial(outer_body, lat),
        in_specs=[SCALARS] + [WHOLE] * 5 + [ANYWHERE],
        out_specs=ANYWHERE,
        out_shape=jax.ShapeDtypeStruct(features.shape, BF16),
        input_output_aliases={6: 0},
        scratch_shapes=[
            pltpu.VMEM((2, frames, lanes // 128, broad + 16, 128), F32),
            pltpu.VMEM((2, frames, broad, channels), BF16),
            pltpu.SemaphoreType.DMA((2,)),
        ],
        compiler_params=params(16),
        name="convolve_outer",
    )(tile, from_pair, from_next, picks, kernel, edges, features)


def exchange(value, offset):
    count = lax.axis_size("seq")
    return lax.ppermute(value, "seq", [(i, i ^ offset) for i in range(count)])


def local(queries, own_kv, past_kv, block_home, block_list, list_len, final_weight, decoder_weight):
    frames, patch_rows, patches, width = queries.shape
    tokens = frames * patch_rows * patches
    count = lax.axis_size("seq")
    assert count & (count - 1) == 0
    bits = count.bit_length() - 1
    blocks_here = past_kv.shape[0]
    columns = final_weight.shape[1]
    tile = lax.axis_index("seq").astype(jnp.int32).reshape(1)
    query_rows = queries.reshape(tokens, width)
    own_rows = own_kv.reshape(tokens, own_kv.shape[3])
    shape = (frames, patch_rows, patches)
    inner_picks, outer_picks = spreads(columns // 4, patch_rows)
    half = KV_HEADS // 2
    lists = (tile, block_home, block_list, list_len)
    if count == 16 and columns == 2 * decoder_weight.shape[1]:
        far = [4, 8, 12]
        turns = [(2, 0), (3, 1), (1, 2), (0, 3)]
        line = [exchange(past_kv, k) for k in far]
        final, decode = final_weight.T, decoder_weight.T
        final_across, decode_across = exchange(final, 2), exchange(decode, 2)
        own_rows, inner_picks, outer_picks = lax.optimization_barrier((own_rows, inner_picks, outer_picks))
        packed, sums, _ = attend_own(range(half), *lists, query_rows, own_rows, turns, blocks_here)
        *line, final_across, decode_across, packed = lax.optimization_barrier(
            (*line, final_across, decode_across, packed)
        )
        near = join([past_kv] + line, "join_near")
        across = exchange(near, 2)
        beside = exchange(near, 1)
        panels = pack(final, decode, final_across, decode_across)
        panels_far, panels_near = exchange(panels, 8), exchange(panels, 4)
        own_rows, near = lax.optimization_barrier((own_rows, near))
        others = attend_own(range(half, KV_HEADS), *lists, query_rows, own_rows, turns, blocks_here)
        packed, sums, slots = [packed, others[0]], [sums, others[1]], others[2]
        across, beside, panels_far, panels_near, slots = lax.optimization_barrier(
            (across, beside, panels_far, panels_near, slots)
        )
        gathered = [near, across, beside, exchange(across, 1)]
        panels_last = exchange(panels_far, 4)
        panels = join([panels, panels_far, panels_near], "join_panels")
        panels_beside = exchange(panels, 1)
        attended = attend_past(slots, packed, sums, gathered, blocks_here)
        panels_last, panels_beside, attended = lax.optimization_barrier((panels_last, panels_beside, attended))
        panels = [panels, panels_last, panels_beside, exchange(panels_last, 1)]
        order = [k ^ x for k in (0, 8, 4, 12) for x in (0, 2)]
        order = order + [k ^ 1 for k in order]
        predicted, to_pair, to_next = project(tile, attended, panels, order, shape)
        decode = unpack(tile, panels, order, 2 * final_weight.shape[0], decoder_weight.shape[0])
    else:
        turns = [(bit, bits - 1 - bit) for bit in range(bits)]
        held = past_kv
        for bit in reversed(range(bits)):
            held = jnp.concatenate([held, exchange(held, 1 << bit)], axis=0)
        packed, sums, slots = attend_own(
            range(KV_HEADS), *lists, query_rows, own_rows, turns, blocks_here
        )
        attended = attend_past(slots, [packed], [sums], [held], blocks_here)
        final = lax.all_gather(final_weight, "seq", axis=0, tiled=True)
        decode = lax.all_gather(decoder_weight, "seq", axis=1, tiled=True)
        predicted = jnp.dot(attended, final, preferred_element_type=F32).astype(BF16)
        rows = predicted.reshape(shape + (columns,))
        even = tile[0] % 2 == 0
        to_pair = jnp.where(even, rows[:, -1], rows[:, 0])
        to_next = jnp.where(even, rows[:, 0], rows[:, -1])
    predicted = predicted.reshape(shape + (columns,))
    swaps = [(i, i + 1) for i in range(1, count - 1, 2)] + [(i + 1, i) for i in range(1, count - 1, 2)]
    from_next = lax.ppermute(to_next, "seq", swaps)
    from_pair = exchange(to_pair, 1)
    features, edges = convolve_inner(predicted, inner_picks, decode)
    return convolve_outer(tile, from_pair, from_next, outer_picks, decode, edges, features)


def solution(mesh):
    return jax.shard_map(
        local,
        mesh=mesh,
        in_specs=(
            P("groups", "seq", None, None),
            P("groups", "seq", None, None),
            P(("groups", "seq"), None, None),
            P("groups"),
            P("groups", None),
            P("groups"),
            P("seq", None),
            P(None, "seq"),
        ),
        out_specs=P("groups", "seq", None, None),
        check_vma=False,
    )
```

```python
import functools
import math

import jax
import jax.numpy as jnp
from jax import lax
from jax.experimental import pallas as pl
from jax.experimental.pallas import tpu as pltpu
from jax.sharding import PartitionSpec as P

HEADS = 24
KV_HEADS = 4
HEAD_DIM = 128
GROUP = HEADS // KV_HEADS
SCALE = math.log2(math.e) / math.sqrt(HEAD_DIM)
SAFE = 2.0**100
MIB = 1024 * 1024
WHOLE = pl.BlockSpec(memory_space=pltpu.VMEM)
ANYWHERE = pl.BlockSpec(memory_space=pl.ANY)
SCALARS = pl.BlockSpec(memory_space=pltpu.SMEM)
BF16 = jnp.bfloat16
F32 = jnp.float32


def head_columns(index):
    return slice(index * HEAD_DIM, (index + 1) * HEAD_DIM)


def params(mib):
    return pltpu.CompilerParams(vmem_limit_bytes=mib * MIB)


def place_of(offset, turns):
    return sum(((offset >> bit) & 1) << to for bit, to in turns)


def own_body(turns, blocks_here, groups, tile_ref, home, blocks, lens, queries, own, packed, sums, slots):
    tokens = queries.shape[0]
    tile = tile_ref[0]
    for place in range(slots.shape[0]):
        slots[place] = -1

    def find(entry, carry):
        stored = home[blocks[tile, entry]]
        slots[place_of((stored // blocks_here) ^ tile, turns)] = stored % blocks_here
        return carry

    if groups[-1] == KV_HEADS - 1:
        lax.fori_loop(0, lens[tile], find, 0)
    for index, g in enumerate(groups):
        query = jnp.concatenate([queries[:, head_columns(g * GROUP + h)] for h in range(GROUP)], axis=0)
        value = jnp.concatenate(
            [own[:, head_columns(KV_HEADS + g)], jnp.ones((tokens, HEAD_DIM), BF16)], axis=1
        )
        score = lax.dot_general(
            query, own[:, head_columns(g)], (((1,), (1,)), ((), ())), preferred_element_type=F32
        )
        top = jnp.max(score, axis=1, keepdims=True)
        weights = jnp.exp2((score - top) * SCALE).astype(BF16)
        mixed = jnp.dot(weights, value, preferred_element_type=F32)
        total = mixed[:, HEAD_DIM:]
        sums[index] = mixed[:, :HEAD_DIM] / total
        level = top + jnp.log2(total) * (1.0 / SCALE)
        high = level.astype(BF16).astype(F32)
        middle = (level - high).astype(BF16).astype(F32)
        low = level - high - middle
        lane = lax.broadcasted_iota(jnp.int32, level.shape, 1)
        extra = jnp.where(lane == 0, high, jnp.where(lane == 1, middle, jnp.where(lane == 2, low, 0.0)))
        packed[index, :, :HEAD_DIM] = query
        packed[index, :, HEAD_DIM:] = extra.astype(BF16)


def attend_own(groups, tile, block_home, block_list, list_len, query_rows, own_rows, turns, blocks_here):
    tokens, width = query_rows.shape
    rows = GROUP * tokens
    return pl.pallas_call(
        functools.partial(own_body, turns, blocks_here, groups),
        in_specs=[SCALARS] * 4 + [WHOLE] * 2,
        out_specs=[WHOLE, WHOLE, SCALARS],
        out_shape=[
            jax.ShapeDtypeStruct((len(groups), rows, 2 * HEAD_DIM), BF16),
            jax.ShapeDtypeStruct((len(groups), rows, HEAD_DIM), F32),
            jax.ShapeDtypeStruct((1 << len(turns),), jnp.int32),
        ],
        compiler_params=params(20),
        cost_estimate=pl.CostEstimate(
            flops=3 * len(groups) * tokens * tokens * width, bytes_accessed=0, transcendentals=0
        ),
        name="attend_own",
    )(tile, block_home, block_list, list_len, query_rows, own_rows)


def past_body(sizes, split, slots, *refs):
    packed, sums, refs = refs[:split], refs[split : 2 * split], refs[2 * split :]
    gathered, (out, keys, values, worst) = refs[: len(sizes)], refs[len(sizes) :]
    groups = KV_HEADS // split
    blocks_here = sum(ref.shape[0] for ref in gathered) // sum(sizes)
    block_tokens = gathered[0].shape[1]
    tokens = out.shape[0]
    lane = lax.broadcasted_iota(jnp.int32, (block_tokens, HEAD_DIM), 1)
    minus = jnp.where(lane < 3, -1.0, 0.0)
    zero = jnp.zeros((block_tokens, HEAD_DIM), BF16)
    homes = [(ref, k) for ref, size in zip(gathered, sizes) for k in range(size)]
    for place, (ref, k) in enumerate(homes):
        slot = slots[place]
        listed = slot >= 0
        block = ref[k * blocks_here + jnp.maximum(slot, 0)]
        live = jnp.where(listed, 1.0, 0.0)
        level = (minus * live).astype(BF16)
        counted = jnp.full((block_tokens, HEAD_DIM), live, F32).astype(BF16)
        rows = slice(place * block_tokens, (place + 1) * block_tokens)
        for g in range(KV_HEADS):
            keys[g, rows, :HEAD_DIM] = jnp.where(listed, block[:, head_columns(g)], zero)
            keys[g, rows, HEAD_DIM:] = level
            values[g, rows, :HEAD_DIM] = jnp.where(listed, block[:, head_columns(KV_HEADS + g)], zero)
            values[g, rows, HEAD_DIM:] = counted

    heads = GROUP if keys.shape[1] <= 512 else 1
    steps = KV_HEADS * GROUP // heads

    def over_steps(one, start):
        if heads == GROUP:
            for step in range(steps):
                start = one(step, start)
            return start
        return lax.fori_loop(0, steps, one, start)

    def place(step):
        if heads == GROUP:
            return step, slice(None)
        return step // GROUP, pl.ds(pl.multiple_of((step % GROUP) * tokens, tokens), tokens)

    def own_part(arrays, g, rows):
        if split == 1:
            return arrays[0][g, rows]
        return arrays[g // groups][g % groups, rows]

    def scores(g, rows):
        return SCALE * lax.dot_general(
            own_part(packed, g, rows), keys[g], (((1,), (1,)), ((), ())), preferred_element_type=F32
        )

    def emit(step, attended):
        attended = attended.astype(BF16)
        for h in range(heads):
            columns = (step * heads + h) * HEAD_DIM
            if heads == 1:
                columns = pl.multiple_of(columns, HEAD_DIM)
            out[:, pl.ds(columns, HEAD_DIM)] = attended[h * tokens : (h + 1) * tokens]

    def quick(step, largest):
        g, rows = place(step)
        weights = jnp.exp2(scores(g, rows)).astype(BF16)
        mixed = jnp.dot(weights, values[g], preferred_element_type=F32)
        below = mixed[:, HEAD_DIM:] + 1.0
        emit(step, (mixed[:, :HEAD_DIM] + own_part(sums, g, rows)) / below)
        return jnp.maximum(largest, jnp.max(below.reshape((-1,) + largest.shape), axis=0))

    worst[...] = over_steps(quick, jnp.zeros(worst.shape, F32))

    @pl.when(jnp.logical_not(jnp.max(worst[...]) < SAFE))
    def _():
        def careful(step, carry):
            g, rows = place(step)
            score = scores(g, rows)
            top = jnp.maximum(jnp.max(score, axis=1, keepdims=True), 0.0)
            weights = jnp.exp2(score - top).astype(BF16)
            mixed = jnp.dot(weights, values[g], preferred_element_type=F32)
            share = jnp.exp2(-top)
            joined = mixed[:, :HEAD_DIM] + share * own_part(sums, g, rows)
            emit(step, joined / (mixed[:, HEAD_DIM:] + share))
            return carry

        over_steps(careful, 0)


def attend_past(slots, packed, sums, gathered, blocks_here):
    heads = KV_HEADS
    rows = packed[0].shape[1]
    tokens = rows // GROUP
    sizes = [array.shape[0] // blocks_here for array in gathered]
    keys = sum(sizes) * gathered[0].shape[1]
    return pl.pallas_call(
        functools.partial(past_body, sizes, len(packed)),
        in_specs=[SCALARS] + [WHOLE] * (2 * len(packed) + len(gathered)),
        out_specs=WHOLE,
        out_shape=jax.ShapeDtypeStruct((tokens, HEADS * HEAD_DIM), BF16),
        scratch_shapes=[
            pltpu.VMEM((heads, keys, 2 * HEAD_DIM), BF16),
            pltpu.VMEM((heads, keys, 2 * HEAD_DIM), BF16),
            pltpu.VMEM((8, HEAD_DIM), F32),
        ],
        compiler_params=params(40 if keys > 256 else 24),
        cost_estimate=pl.CostEstimate(
            flops=8 * heads * rows * keys * HEAD_DIM, bytes_accessed=heads * rows * 1024, transcendentals=0
        ),
        name="attend_past",
    )(slots, *packed, *sums, *gathered)


def join_body(*refs):
    *parts, out = refs
    row = 0
    for part in parts:
        out[row : row + part.shape[0]] = part[...]
        row += part.shape[0]


def join(parts, name):
    rows = sum(part.shape[0] for part in parts)
    return pl.pallas_call(
        join_body,
        in_specs=[WHOLE] * len(parts),
        out_specs=WHOLE,
        out_shape=jax.ShapeDtypeStruct((rows,) + parts[0].shape[1:], BF16),
        compiler_params=params(4),
        name=name,
    )(*parts)


def pack_body(final, decode, final_across, decode_across, out):
    half = final.shape[0] // 2
    blank = out.shape[2] - 2 * final.shape[1] - decode.shape[1]
    for k, (left, right) in enumerate(((final, decode), (final_across, decode_across))):
        out[k] = jnp.concatenate(
            [left[:half], left[half:], right[...], jnp.zeros((half, blank), BF16)], axis=1
        )


def pack(final, decode, final_across, decode_across):
    lanes = -(-(2 * final.shape[1] + decode.shape[1]) // 128) * 128
    return pl.pallas_call(
        pack_body,
        in_specs=[WHOLE] * 4,
        out_specs=WHOLE,
        out_shape=jax.ShapeDtypeStruct((2, decode.shape[0], lanes), BF16),
        compiler_params=params(4),
        name="pack",
    )(final, decode, final_across, decode_across)


def project_pairs(offsets, depth, tile, attended, ours, theirs):
    even = tile % 2 == 0
    total = jnp.zeros((attended.shape[0], 2 * ours[0].shape[1]), F32)
    ours = [(ref, k) for ref in ours for k in range(ref.shape[0])]
    theirs = [(ref, k) for ref in theirs for k in range(ref.shape[0])]
    for offset, (our, i), (their, j) in zip(offsets, ours, theirs):
        left, right = our[i], their[j]
        left, right = jnp.where(even, left, right), jnp.where(even, right, left)
        rows = [
            jnp.concatenate([panel[:, part * depth : (part + 1) * depth] for panel in (left, right)], axis=1)
            for part in range(2)
        ]
        start = pl.multiple_of(((tile ^ offset) // 2) * (2 * depth), 128)
        total += lax.dot_general(
            attended[:, pl.ds(start, 2 * depth)],
            jnp.concatenate(rows, axis=0),
            (((1,), (1,)), ((), ())),
            preferred_element_type=F32,
        )
    return total


def project_body(offsets, depth, tile_ref, attended, ours, theirs, out):
    out[...] = project_pairs(offsets, depth, tile_ref[0], attended, [ours], [theirs])


def project(tile, attended, ours, theirs, offsets, depth):
    return pl.pallas_call(
        functools.partial(project_body, offsets, depth),
        in_specs=[SCALARS] + [WHOLE] * 3,
        out_specs=WHOLE,
        out_shape=jax.ShapeDtypeStruct((attended.shape[0], 2 * ours.shape[1]), F32),
        compiler_params=params(16),
        name="project",
    )(tile, attended, ours, theirs)


def finish_body(offsets, depth, shape, tile_ref, attended, ours, theirs, part, out, to_pair, to_next):
    frames, patch_rows, patches = shape
    tile = tile_ref[0]
    predicted = part[...] + project_pairs(offsets, depth, tile, attended, [ours], [theirs])
    predicted = predicted.astype(BF16)
    out[...] = predicted
    even = tile % 2 == 0
    values = predicted.shape[1] // 2
    folds = 128 // values
    count = patches // folds

    def folded(rows):
        return jnp.concatenate([rows[k * count : (k + 1) * count] for k in range(folds)], axis=1)

    for frame in range(frames):
        rows = predicted[frame * patch_rows * patches : (frame + 1) * patch_rows * patches]
        first, last = folded(rows[:patches, :values]), folded(rows[(patch_rows - 1) * patches :, values:])
        to_pair[frame] = jnp.where(even, last, first)
        to_next[frame] = jnp.where(even, first, last)


def finish(tile, attended, ours, theirs, part, offsets, depth, shape):
    tokens, columns = part.shape
    border = jax.ShapeDtypeStruct((shape[0], shape[2] * (columns // 2) // 128, 128), BF16)
    return pl.pallas_call(
        functools.partial(finish_body, offsets, depth, shape),
        in_specs=[SCALARS] + [WHOLE] * 4,
        out_specs=[WHOLE] * 3,
        out_shape=[jax.ShapeDtypeStruct((tokens, columns), BF16), border, border],
        compiler_params=params(16),
        name="finish",
    )(tile, attended, ours, theirs, part)


def unpack_body(order, skip, tile_ref, *refs):
    *panels, out, staged = refs
    taps = out.shape[0]
    place = 0
    for panel in panels:
        for k in range(panel.shape[0]):
            staged[tile_ref[0] ^ order[place]] = panel[k]
            place += 1
    whole = [staged[device, :, skip : skip + taps] for device in range(len(order))]
    out[...] = jnp.concatenate(whole, axis=0).T


def unpack(tile, panels, order, skip, taps):
    width, lanes = panels[0].shape[1:]
    return pl.pallas_call(
        functools.partial(unpack_body, order, skip),
        in_specs=[SCALARS] + [WHOLE] * len(panels),
        out_specs=WHOLE,
        out_shape=jax.ShapeDtypeStruct((taps, width * len(order)), BF16),
        scratch_shapes=[pltpu.VMEM((len(order), width, lanes), BF16)],
        compiler_params=params(16),
        name="unpack",
    )(tile, *panels)


def tap_rows(frames, cells, width):
    stacks = []
    for shift_t in range(3):
        rows = []
        for frame in range(frames):
            source = frame + shift_t - 2
            rows.append(cells[source] if source >= 0 else jnp.zeros((width, cells[0].shape[1]), BF16))
        stacks.append(jnp.concatenate(rows, axis=0))
    return stacks


def shifted(wide, frame, width, lat):
    chunks = []
    for chunk in range(wide.shape[1]):
        lane = lax.broadcasted_iota(jnp.int32, (width, 128), 1) + 128 * chunk
        shift = (lane // lat) % 3
        near = jnp.where(shift == 1, wide[frame, chunk, 8 : 8 + width], wide[frame, chunk, 9 : 9 + width])
        chunks.append(jnp.where(shift == 0, wide[frame, chunk, 7 : 7 + width], near).astype(BF16))
    return jnp.concatenate(chunks, axis=1)


def spread_body(lat, patch_rows, inner, outer):
    span = 3 * lat
    for side in range(2):
        source = lax.broadcasted_iota(jnp.int32, inner.shape[2:], 0)
        target = lax.broadcasted_iota(jnp.int32, inner.shape[2:], 1)
        for r in range(patch_rows):
            upper = target // span - 2 * r
            wanted = (upper >= 0) & (upper < 2) & (source == upper * 2 * lat + side * lat + target % lat)
            inner[side, r] = jnp.where(wanted, 1.0, 0.0).astype(BF16)
        source = lax.broadcasted_iota(jnp.int32, outer.shape[1:], 0)
        target = lax.broadcasted_iota(jnp.int32, outer.shape[1:], 1)
        wanted = (source == side * lat + target % lat) & (target < 3 * span)
        outer[side] = jnp.where(wanted, 1.0, 0.0).astype(BF16)


def spreads(lat, patch_rows):
    tall = 2 * patch_rows
    return pl.pallas_call(
        functools.partial(spread_body, lat, patch_rows),
        out_specs=[WHOLE, WHOLE],
        out_shape=[
            jax.ShapeDtypeStruct((2, patch_rows, 4 * lat, -(-tall * 3 * lat // 128) * 128), BF16),
            jax.ShapeDtypeStruct((2, 2 * lat, -(-9 * lat // 128) * 128), BF16),
        ],
        compiler_params=params(4),
        cost_estimate=pl.CostEstimate(flops=5 * 10**9, bytes_accessed=0, transcendentals=0),
        name="spreads",
    )()


def inner_body(lat, predicted, picks, kernel, features, edges, wide, done, sems):
    frames, patch_rows, patches, values = predicted.shape
    tall, broad = 2 * patch_rows, 2 * patches
    span = 3 * lat
    chunks = wide.shape[1]
    lanes = 128 * chunks
    wide[:, :, 0:8] = jnp.zeros((frames, chunks, 8, 128), F32)
    wide[:, :, 8 + broad :] = jnp.zeros((frames, chunks, 8, 128), F32)
    for side in range(2):
        for frame in range(frames):
            cells = jnp.zeros((patches, lanes), F32)
            for r in range(patch_rows):
                cells += jnp.dot(predicted[frame, r], picks[side, r], preferred_element_type=F32)
            for chunk in range(chunks):
                wide[frame, chunk, pl.ds(8 + side, patches, stride=2), :] = cells[:, 128 * chunk : 128 * (chunk + 1)]
    stacks = tap_rows(frames, [shifted(wide, f, broad, lat) for f in range(frames)], broad)
    copies = []
    for row in list(range(1, tall - 1)) + [0, tall - 1]:
        first, last = max(row - 1, 0), min(row + 1, tall - 1)
        total = jnp.zeros((frames * broad, kernel.shape[1]), F32)
        for shift_t in range(3):
            start = (3 * shift_t + first - (row - 1)) * span
            total += jnp.dot(
                stacks[shift_t][:, first * span : (last + 1) * span],
                kernel[start : start + (last + 1 - first) * span],
                preferred_element_type=F32,
            )
        if 0 < row < tall - 1:
            done[row - 1] = total.astype(BF16).reshape(done.shape[1:])
            copy = pltpu.make_async_copy(done.at[row - 1], features.at[:, row], sems.at[row - 1])
            copy.start()
            copies.append(copy)
        else:
            edges[0 if row == 0 else 1] = total
    for copy in copies:
        copy.wait()


def convolve_inner(predicted, picks, kernel):
    frames, patch_rows, patches, values = predicted.shape
    lat = values // 4
    tall, broad = 2 * patch_rows, 2 * patches
    channels = kernel.shape[1]
    lanes = -(-tall * 3 * lat // 128) * 128
    return pl.pallas_call(
        functools.partial(inner_body, lat),
        in_specs=[WHOLE] * 3,
        out_specs=[ANYWHERE, WHOLE],
        out_shape=[
            jax.ShapeDtypeStruct((frames, tall, broad, channels), BF16),
            jax.ShapeDtypeStruct((2, frames * broad, channels), F32),
        ],
        scratch_shapes=[
            pltpu.VMEM((frames, lanes // 128, broad + 16, 128), F32),
            pltpu.VMEM((tall - 2, frames, broad, channels), BF16),
            pltpu.SemaphoreType.DMA((tall - 2,)),
        ],
        compiler_params=params(16),
        cost_estimate=pl.CostEstimate(
            flops=2 * frames * tall * broad * 27 * lat * channels,
            bytes_accessed=2 * frames * tall * broad * channels,
            transcendentals=0,
        ),
        name="convolve_inner",
    )(predicted, picks, kernel)


def outer_body(lat, tile_ref, from_pair, from_next, picks, kernel, edges, given, features, wide, done, sems):
    frames, values = from_pair.shape[0], picks.shape[1]
    folds = 128 // values
    patches = from_pair.shape[1] * folds
    even = tile_ref[0] % 2 == 0
    broad = 2 * patches
    tall = features.shape[1]
    span = 3 * lat
    chunks = wide.shape[2]
    lanes = 128 * chunks
    lane = lax.broadcasted_iota(jnp.int32, (broad, lanes), 1)
    copies = []
    for edge in range(2):
        cells = []
        for frame in range(frames):
            rows = jnp.where(even == (edge == 0), from_next[frame], from_pair[frame])
            parts = [rows[:, k * values : (k + 1) * values] for k in range(folds)]
            cells.append(jnp.concatenate(parts, axis=0))
        wide[edge, :, :, 0:8] = jnp.zeros((frames, chunks, 8, 128), F32)
        wide[edge, :, :, 8 + broad :] = jnp.zeros((frames, chunks, 8, 128), F32)
        for side in range(2):
            for frame in range(frames):
                spread = jnp.dot(cells[frame], picks[side], preferred_element_type=F32)
                for chunk in range(chunks):
                    wide[edge, frame, chunk, pl.ds(8 + side, patches, stride=2), :] = spread[
                        :, 128 * chunk : 128 * (chunk + 1)
                    ]
        ready = [shifted(wide.at[edge], f, broad, lat) for f in range(frames)]
        rows = []
        for frame in range(frames):
            taps = jnp.zeros((broad, lanes), BF16)
            for shift_t in range(3):
                if frame + shift_t - 2 >= 0:
                    taps = jnp.where(lane // span == shift_t, ready[frame + shift_t - 2], taps)
            rows.append(taps)
        shift_y = 2 * edge
        panel = jnp.concatenate(
            [kernel[(3 * t + shift_y) * span : (3 * t + shift_y + 1) * span] for t in range(3)], axis=0
        )
        total = edges[edge] + jnp.dot(
            jnp.concatenate(rows, axis=0)[:, : 3 * span], panel, preferred_element_type=F32
        )
        done[edge] = total.astype(BF16).reshape(done.shape[1:])
        copy = pltpu.make_async_copy(done.at[edge], features.at[:, edge * (tall - 1)], sems.at[edge])
        copy.start()
        copies.append(copy)
    for copy in copies:
        copy.wait()


def convolve_outer(tile, from_pair, from_next, picks, kernel, edges, features):
    frames, tall, broad, _ = features.shape
    lat = picks.shape[1] // 2
    channels = kernel.shape[1]
    lanes = -(-9 * lat // 128) * 128
    return pl.pallas_call(
        functools.partial(outer_body, lat),
        in_specs=[SCALARS] + [WHOLE] * 5 + [ANYWHERE],
        out_specs=ANYWHERE,
        out_shape=jax.ShapeDtypeStruct(features.shape, BF16),
        input_output_aliases={6: 0},
        scratch_shapes=[
            pltpu.VMEM((2, frames, lanes // 128, broad + 16, 128), F32),
            pltpu.VMEM((2, frames, broad, channels), BF16),
            pltpu.SemaphoreType.DMA((2,)),
        ],
        compiler_params=params(16),
        name="convolve_outer",
    )(tile, from_pair, from_next, picks, kernel, edges, features)


def exchange(value, offset):
    count = lax.axis_size("seq")
    return lax.ppermute(value, "seq", [(i, i ^ offset) for i in range(count)])


def local(queries, own_kv, past_kv, block_home, block_list, list_len, final_weight, decoder_weight):
    frames, patch_rows, patches, width = queries.shape
    tokens = frames * patch_rows * patches
    count = lax.axis_size("seq")
    assert count & (count - 1) == 0
    bits = count.bit_length() - 1
    blocks_here = past_kv.shape[0]
    columns = final_weight.shape[1]
    tile = lax.axis_index("seq").astype(jnp.int32).reshape(1)
    query_rows = queries.reshape(tokens, width)
    own_rows = own_kv.reshape(tokens, own_kv.shape[3])
    shape = (frames, patch_rows, patches)
    inner_picks, outer_picks = spreads(columns // 4, patch_rows)
    half = KV_HEADS // 2
    lists = (tile, block_home, block_list, list_len)
    if count == 16 and columns == 2 * decoder_weight.shape[1]:
        far = [4, 8, 12]
        turns = [(2, 0), (3, 1), (1, 2), (0, 3)]
        line = [exchange(past_kv, k) for k in far]
        final, decode, own_rows, inner_picks, outer_picks = lax.optimization_barrier(
            (final_weight.T, decoder_weight.T, own_rows, inner_picks, outer_picks)
        )
        final_across, decode_across = exchange(final, 2), exchange(decode, 2)
        packed, sums, _ = attend_own(range(half), *lists, query_rows, own_rows, turns, blocks_here)
        *line, final_across, decode_across, packed = lax.optimization_barrier(
            (*line, final_across, decode_across, packed)
        )
        near = join([past_kv] + line, "join_near")
        across = exchange(near, 2)
        panels = pack(final, decode, final_across, decode_across)
        panels_far, panels_near = exchange(panels, 8), exchange(panels, 4)
        own_rows, near = lax.optimization_barrier((own_rows, near))
        others = attend_own(range(half, KV_HEADS), *lists, query_rows, own_rows, turns, blocks_here)
        packed, sums, slots = [packed, others[0]], [sums, others[1]], others[2]
        across, panels_far, panels_near, slots = lax.optimization_barrier((across, panels_far, panels_near, slots))
        gathered = join([near, across], "join_chip")
        gathered = [gathered, exchange(gathered, 1)]
        panels_last = exchange(panels_far, 4)
        panels = join([panels, panels_far, panels_near], "join_panels")
        panels_beside = exchange(panels, 1)
        attended = attend_past(slots, packed, sums, gathered, blocks_here)
        panels_last, panels_beside, attended = lax.optimization_barrier((panels_last, panels_beside, attended))
        panels = [panels, panels_last, panels_beside, exchange(panels_last, 1)]
        order = [k ^ x for k in (0, 8, 4, 12) for x in (0, 2)]
        order = order + [k ^ 1 for k in order]
        depth = final_weight.shape[0]
        part = project(tile, attended, panels[0], panels[2], order[:6], depth)
        predicted, to_pair, to_next = finish(
            tile, attended, panels[1], panels[3], part, order[6:8], depth, shape
        )
        decode = unpack(tile, panels, order, 2 * final_weight.shape[0], decoder_weight.shape[0])
    else:
        turns = [(bit, bits - 1 - bit) for bit in range(bits)]
        held = past_kv
        for bit in reversed(range(bits)):
            held = jnp.concatenate([held, exchange(held, 1 << bit)], axis=0)
        packed, sums, slots = attend_own(
            range(KV_HEADS), *lists, query_rows, own_rows, turns, blocks_here
        )
        attended = attend_past(slots, [packed], [sums], [held], blocks_here)
        final = lax.all_gather(final_weight, "seq", axis=0, tiled=True)
        decode = lax.all_gather(decoder_weight, "seq", axis=1, tiled=True)
        predicted = jnp.dot(attended, final, preferred_element_type=F32).astype(BF16)
        rows = predicted.reshape(shape + (columns,))
        values = columns // 2
        folds = 128 // values

        def folded(cells):
            parts = cells.reshape(frames, folds, patches // folds, values)
            return parts.transpose(0, 2, 1, 3).reshape(frames, patches // folds, 128)

        first, last = folded(rows[:, 0, :, :values]), folded(rows[:, -1, :, values:])
        even = tile[0] % 2 == 0
        to_pair, to_next = jnp.where(even, last, first), jnp.where(even, first, last)
    predicted = predicted.reshape(shape + (columns,))
    swaps = [(i, i + 1) for i in range(1, count - 1, 2)] + [(i + 1, i) for i in range(1, count - 1, 2)]
    from_next = lax.ppermute(to_next, "seq", swaps)
    from_pair = exchange(to_pair, 1)
    features, edges = convolve_inner(predicted, inner_picks, decode)
    return convolve_outer(tile, from_pair, from_next, outer_picks, decode, edges, features)


def solution(mesh):
    return jax.shard_map(
        local,
        mesh=mesh,
        in_specs=(
            P("groups", "seq", None, None),
            P("groups", "seq", None, None),
            P(("groups", "seq"), None, None),
            P("groups"),
            P("groups", None),
            P("groups"),
            P("seq", None),
            P(None, "seq"),
        ),
        out_specs=P("groups", "seq", None, None),
        check_vma=False,
    )
```

```python
import functools
import math

import jax
import jax.numpy as jnp
from jax import lax
from jax.experimental import pallas as pl
from jax.experimental.pallas import tpu as pltpu
from jax.sharding import PartitionSpec as P

HEADS = 24
KV_HEADS = 4
HEAD_DIM = 128
GROUP = HEADS // KV_HEADS
SCALE = math.log2(math.e) / math.sqrt(HEAD_DIM)
SAFE = 2.0**100
MIB = 1024 * 1024
PART = 16
WHOLE = pl.BlockSpec(memory_space=pltpu.VMEM)
ANYWHERE = pl.BlockSpec(memory_space=pl.ANY)
SCALARS = pl.BlockSpec(memory_space=pltpu.SMEM)
BF16 = jnp.bfloat16
F32 = jnp.float32


def head_columns(index):
    return slice(index * HEAD_DIM, (index + 1) * HEAD_DIM)


def params(mib):
    return pltpu.CompilerParams(vmem_limit_bytes=mib * MIB)


def place_of(offset, turns):
    return sum(((offset >> bit) & 1) << to for bit, to in turns)


def own_body(turns, blocks_here, groups, tile_ref, home, blocks, lens, queries, own, packed, sums, slots):
    tokens = queries.shape[0]
    tile = tile_ref[0]
    for place in range(slots.shape[0]):
        slots[place] = -1

    def find(entry, carry):
        stored = home[blocks[tile, entry]]
        slots[place_of((stored // blocks_here) ^ tile, turns)] = stored % blocks_here
        return carry

    if groups[-1] == KV_HEADS - 1:
        lax.fori_loop(0, lens[tile], find, 0)
    for index, g in enumerate(groups):
        query = jnp.concatenate([queries[:, head_columns(g * GROUP + h)] for h in range(GROUP)], axis=0)
        value = jnp.concatenate(
            [own[:, head_columns(KV_HEADS + g)], jnp.ones((tokens, HEAD_DIM), BF16)], axis=1
        )
        score = lax.dot_general(
            query, own[:, head_columns(g)], (((1,), (1,)), ((), ())), preferred_element_type=F32
        )
        top = jnp.max(score, axis=1, keepdims=True)
        weights = jnp.exp2((score - top) * SCALE).astype(BF16)
        mixed = jnp.dot(weights, value, preferred_element_type=F32)
        total = mixed[:, HEAD_DIM:]
        sums[index] = mixed[:, :HEAD_DIM] / total
        level = top + jnp.log2(total) * (1.0 / SCALE)
        high = level.astype(BF16).astype(F32)
        middle = (level - high).astype(BF16).astype(F32)
        low = level - high - middle
        lane = lax.broadcasted_iota(jnp.int32, level.shape, 1)
        extra = jnp.where(lane == 0, high, jnp.where(lane == 1, middle, jnp.where(lane == 2, low, 0.0)))
        packed[index, :, :HEAD_DIM] = query
        packed[index, :, HEAD_DIM:] = extra.astype(BF16)


def attend_own(groups, tile, block_home, block_list, list_len, query_rows, own_rows, turns, blocks_here):
    tokens, width = query_rows.shape
    rows = GROUP * tokens
    return pl.pallas_call(
        functools.partial(own_body, turns, blocks_here, groups),
        in_specs=[SCALARS] * 4 + [WHOLE] * 2,
        out_specs=[WHOLE, WHOLE, SCALARS],
        out_shape=[
            jax.ShapeDtypeStruct((len(groups), rows, 2 * HEAD_DIM), BF16),
            jax.ShapeDtypeStruct((len(groups), rows, HEAD_DIM), F32),
            jax.ShapeDtypeStruct((1 << len(turns),), jnp.int32),
        ],
        compiler_params=params(20),
        cost_estimate=pl.CostEstimate(
            flops=3 * len(groups) * tokens * tokens * width, bytes_accessed=0, transcendentals=0
        ),
        name="attend_own",
    )(tile, block_home, block_list, list_len, query_rows, own_rows)


def past_body(sizes, split, slots, *refs):
    packed, sums, refs = refs[:split], refs[split : 2 * split], refs[2 * split :]
    gathered, (out, keys, values, worst) = refs[: len(sizes)], refs[len(sizes) :]
    groups = KV_HEADS // split
    blocks_here = sum(ref.shape[0] for ref in gathered) // sum(sizes)
    block_tokens = gathered[0].shape[1]
    tokens = out.shape[0]
    lane = lax.broadcasted_iota(jnp.int32, (block_tokens, HEAD_DIM), 1)
    minus = jnp.where(lane < 3, -1.0, 0.0)
    zero = jnp.zeros((block_tokens, HEAD_DIM), BF16)
    homes = [(ref, k) for ref, size in zip(gathered, sizes) for k in range(size)]
    for place, (ref, k) in enumerate(homes):
        slot = slots[place]
        listed = slot >= 0
        block = ref[k * blocks_here + jnp.maximum(slot, 0)]
        live = jnp.where(listed, 1.0, 0.0)
        level = (minus * live).astype(BF16)
        counted = jnp.full((block_tokens, HEAD_DIM), live, F32).astype(BF16)
        rows = slice(place * block_tokens, (place + 1) * block_tokens)
        for g in range(KV_HEADS):
            keys[g, rows, :HEAD_DIM] = jnp.where(listed, block[:, head_columns(g)], zero)
            keys[g, rows, HEAD_DIM:] = level
            values[g, rows, :HEAD_DIM] = jnp.where(listed, block[:, head_columns(KV_HEADS + g)], zero)
            values[g, rows, HEAD_DIM:] = counted

    heads = GROUP if keys.shape[1] <= 512 else 1
    steps = KV_HEADS * GROUP // heads

    def over_steps(one, start):
        if heads == GROUP:
            for step in range(steps):
                start = one(step, start)
            return start
        return lax.fori_loop(0, steps, one, start)

    def place(step):
        if heads == GROUP:
            return step, slice(None)
        return step // GROUP, pl.ds(pl.multiple_of((step % GROUP) * tokens, tokens), tokens)

    def own_part(arrays, g, rows):
        if split == 1:
            return arrays[0][g, rows]
        return arrays[g // groups][g % groups, rows]

    def scores(g, rows):
        return SCALE * lax.dot_general(
            own_part(packed, g, rows), keys[g], (((1,), (1,)), ((), ())), preferred_element_type=F32
        )

    def emit(step, attended):
        attended = attended.astype(BF16)
        for h in range(heads):
            columns = (step * heads + h) * HEAD_DIM
            if heads == 1:
                columns = pl.multiple_of(columns, HEAD_DIM)
            out[:, pl.ds(columns, HEAD_DIM)] = attended[h * tokens : (h + 1) * tokens]

    def quick(step, score, largest):
        g, rows = place(step)
        weights = jnp.exp2(score).astype(BF16)
        mixed = jnp.dot(weights, values[g], preferred_element_type=F32)
        below = mixed[:, HEAD_DIM:] + 1.0
        emit(step, (mixed[:, :HEAD_DIM] + own_part(sums, g, rows)) / below)
        return jnp.maximum(largest, jnp.max(below.reshape((-1,) + largest.shape), axis=0))

    largest = jnp.zeros(worst.shape, F32)
    if heads == GROUP:
        score = scores(*place(0))
        for step in range(steps):
            ahead = scores(*place(step + 1)) if step + 1 < steps else None
            largest = quick(step, score, largest)
            score = ahead
    else:
        largest = over_steps(lambda step, seen: quick(step, scores(*place(step)), seen), largest)
    worst[...] = largest

    @pl.when(jnp.logical_not(jnp.max(worst[...]) < SAFE))
    def _():
        def careful(step, carry):
            g, rows = place(step)
            score = scores(g, rows)
            top = jnp.maximum(jnp.max(score, axis=1, keepdims=True), 0.0)
            weights = jnp.exp2(score - top).astype(BF16)
            mixed = jnp.dot(weights, values[g], preferred_element_type=F32)
            share = jnp.exp2(-top)
            joined = mixed[:, :HEAD_DIM] + share * own_part(sums, g, rows)
            emit(step, joined / (mixed[:, HEAD_DIM:] + share))
            return carry

        over_steps(careful, 0)


def attend_past(slots, packed, sums, gathered, blocks_here):
    heads = KV_HEADS
    rows = packed[0].shape[1]
    tokens = rows // GROUP
    sizes = [array.shape[0] // blocks_here for array in gathered]
    keys = sum(sizes) * gathered[0].shape[1]
    return pl.pallas_call(
        functools.partial(past_body, sizes, len(packed)),
        in_specs=[SCALARS] + [WHOLE] * (2 * len(packed) + len(gathered)),
        out_specs=WHOLE,
        out_shape=jax.ShapeDtypeStruct((tokens, HEADS * HEAD_DIM), BF16),
        scratch_shapes=[
            pltpu.VMEM((heads, keys, 2 * HEAD_DIM), BF16),
            pltpu.VMEM((heads, keys, 2 * HEAD_DIM), BF16),
            pltpu.VMEM((8, HEAD_DIM), F32),
        ],
        compiler_params=params(40 if keys > 256 else 24),
        cost_estimate=pl.CostEstimate(
            flops=10**10, bytes_accessed=0, transcendentals=0
        ),
        name="attend_past",
    )(slots, *packed, *sums, *gathered)


def join_body(*refs):
    *parts, out = refs
    row = 0
    for part in parts:
        out[row : row + part.shape[0]] = part[...]
        row += part.shape[0]


def join(parts, name):
    rows = sum(part.shape[0] for part in parts)
    return pl.pallas_call(
        join_body,
        in_specs=[WHOLE] * len(parts),
        out_specs=WHOLE,
        out_shape=jax.ShapeDtypeStruct((rows,) + parts[0].shape[1:], BF16),
        compiler_params=params(4),
        name=name,
    )(*parts)


def parts_of(panel):
    return [panel[row : row + PART] for row in range(0, panel.shape[0], PART)]


def pack_body(final, decode, final_across, decode_across, out):
    for k, (left, right) in enumerate(((final, decode), (final_across, decode_across))):
        parts = parts_of(left) + parts_of(right)
        blank = out.shape[2] - sum(part.shape[1] for part in parts)
        out[k] = jnp.concatenate(parts + [jnp.zeros((PART, blank), BF16)], axis=1)


def pack(final, decode, final_across, decode_across):
    lanes = (final.size + decode.size) // PART
    return pl.pallas_call(
        pack_body,
        in_specs=[WHOLE] * 4,
        out_specs=WHOLE,
        out_shape=jax.ShapeDtypeStruct((2, PART, -(-lanes // 128) * 128), BF16),
        compiler_params=params(4),
        name="pack",
    )(final, decode, final_across, decode_across)


def project_pairs(offsets, depth, columns, tile, attended, ours, theirs):
    even = tile % 2 == 0
    total = jnp.zeros((attended.shape[0], columns), F32)
    ours = [(ref, k) for ref in ours for k in range(ref.shape[0])]
    theirs = [(ref, k) for ref in theirs for k in range(ref.shape[0])]
    for offset, (our, i), (their, j) in zip(offsets, ours, theirs):
        left, right = our[i], their[j]
        left, right = jnp.where(even, left, right), jnp.where(even, right, left)
        rows = [
            jnp.concatenate([panel[:, part * depth : (part + 1) * depth] for panel in (left, right)], axis=1)
            for part in range(columns // PART)
        ]
        start = pl.multiple_of(((tile ^ offset) // 2) * (2 * depth), 128)
        total += lax.dot_general(
            attended[:, pl.ds(start, 2 * depth)],
            jnp.concatenate(rows, axis=0),
            (((1,), (1,)), ((), ())),
            preferred_element_type=F32,
        )
    return total


def project_body(offsets, depth, tile_ref, attended, ours, theirs, out):
    out[...] = project_pairs(offsets, depth, out.shape[1], tile_ref[0], attended, [ours], [theirs])


def project(tile, attended, ours, theirs, offsets, depth, columns):
    return pl.pallas_call(
        functools.partial(project_body, offsets, depth),
        in_specs=[SCALARS] + [WHOLE] * 3,
        out_specs=WHOLE,
        out_shape=jax.ShapeDtypeStruct((attended.shape[0], columns), F32),
        compiler_params=params(16),
        name="project",
    )(tile, attended, ours, theirs)


def finish_body(offsets, depth, shape, tile_ref, attended, ours, theirs, part, out, to_pair, to_next):
    frames, patch_rows, patches = shape
    tile = tile_ref[0]
    predicted = part[...] + project_pairs(offsets, depth, part.shape[1], tile, attended, [ours], [theirs])
    predicted = predicted.astype(BF16)
    out[...] = predicted
    even = tile % 2 == 0
    values = predicted.shape[1] // 2
    folds = 128 // values
    count = patches // folds

    def folded(rows):
        return jnp.concatenate([rows[k * count : (k + 1) * count] for k in range(folds)], axis=1)

    for frame in range(frames):
        rows = predicted[frame * patch_rows * patches : (frame + 1) * patch_rows * patches]
        first, last = folded(rows[:patches, :values]), folded(rows[(patch_rows - 1) * patches :, values:])
        to_pair[frame] = jnp.where(even, last, first)
        to_next[frame] = jnp.where(even, first, last)


def finish(tile, attended, ours, theirs, part, offsets, depth, shape):
    tokens, columns = part.shape
    border = jax.ShapeDtypeStruct((shape[0], shape[2] * (columns // 2) // 128, 128), BF16)
    return pl.pallas_call(
        functools.partial(finish_body, offsets, depth, shape),
        in_specs=[SCALARS] + [WHOLE] * 4,
        out_specs=[WHOLE] * 3,
        out_shape=[jax.ShapeDtypeStruct((tokens, columns), BF16), border, border],
        compiler_params=params(16),
        name="finish",
    )(tile, attended, ours, theirs, part)


def unpack_body(order, skip, tile_ref, *refs):
    *panels, out, staged = refs
    taps = out.shape[0]
    place = 0
    for panel in panels:
        for k in range(panel.shape[0]):
            staged[tile_ref[0] ^ order[place]] = panel[k]
            place += 1
    width = out.shape[1] // len(order)
    whole = [
        staged[device, :, skip + part * taps : skip + (part + 1) * taps]
        for device in range(len(order))
        for part in range(width // PART)
    ]
    out[...] = jnp.concatenate(whole, axis=0).T


def unpack(tile, panels, order, skip, taps, width):
    return pl.pallas_call(
        functools.partial(unpack_body, order, skip),
        in_specs=[SCALARS] + [WHOLE] * len(panels),
        out_specs=WHOLE,
        out_shape=jax.ShapeDtypeStruct((taps, width * len(order)), BF16),
        scratch_shapes=[pltpu.VMEM((len(order),) + panels[0].shape[1:], BF16)],
        compiler_params=params(16),
        name="unpack",
    )(tile, *panels)


def tap_rows(frames, cells, width):
    stacks = []
    for shift_t in range(3):
        rows = []
        for frame in range(frames):
            source = frame + shift_t - 2
            rows.append(cells[source] if source >= 0 else jnp.zeros((width, cells[0].shape[1]), BF16))
        stacks.append(jnp.concatenate(rows, axis=0))
    return stacks


def shifted(wide, frame, width, lat):
    chunks = []
    for chunk in range(wide.shape[1]):
        lane = lax.broadcasted_iota(jnp.int32, (width, 128), 1) + 128 * chunk
        shift = (lane // lat) % 3
        near = jnp.where(shift == 1, wide[frame, chunk, 8 : 8 + width], wide[frame, chunk, 9 : 9 + width])
        chunks.append(jnp.where(shift == 0, wide[frame, chunk, 7 : 7 + width], near).astype(BF16))
    return jnp.concatenate(chunks, axis=1)


def spread_body(lat, patch_rows, inner, outer):
    span = 3 * lat
    for side in range(2):
        source = lax.broadcasted_iota(jnp.int32, inner.shape[2:], 0)
        target = lax.broadcasted_iota(jnp.int32, inner.shape[2:], 1)
        for r in range(patch_rows):
            upper = target // span - 2 * r
            wanted = (upper >= 0) & (upper < 2) & (source == upper * 2 * lat + side * lat + target % lat)
            inner[side, r] = jnp.where(wanted, 1.0, 0.0).astype(BF16)
        source = lax.broadcasted_iota(jnp.int32, outer.shape[1:], 0)
        target = lax.broadcasted_iota(jnp.int32, outer.shape[1:], 1)
        wanted = (source == side * lat + target % lat) & (target < 3 * span)
        outer[side] = jnp.where(wanted, 1.0, 0.0).astype(BF16)


def spreads(lat, patch_rows):
    tall = 2 * patch_rows
    return pl.pallas_call(
        functools.partial(spread_body, lat, patch_rows),
        out_specs=[WHOLE, WHOLE],
        out_shape=[
            jax.ShapeDtypeStruct((2, patch_rows, 4 * lat, -(-tall * 3 * lat // 128) * 128), BF16),
            jax.ShapeDtypeStruct((2, 2 * lat, -(-9 * lat // 128) * 128), BF16),
        ],
        compiler_params=params(4),
        cost_estimate=pl.CostEstimate(flops=5 * 10**9, bytes_accessed=0, transcendentals=0),
        name="spreads",
    )()


def inner_body(lat, predicted, picks, kernel, features, edges, wide, done, sems):
    frames, patch_rows, patches, values = predicted.shape
    tall, broad = 2 * patch_rows, 2 * patches
    span = 3 * lat
    chunks = wide.shape[1]
    lanes = 128 * chunks
    wide[:, :, 0:8] = jnp.zeros((frames, chunks, 8, 128), F32)
    wide[:, :, 8 + broad :] = jnp.zeros((frames, chunks, 8, 128), F32)
    for side in range(2):
        for frame in range(frames):
            cells = jnp.zeros((patches, lanes), F32)
            for r in range(patch_rows):
                cells += jnp.dot(predicted[frame, r], picks[side, r], preferred_element_type=F32)
            for chunk in range(chunks):
                wide[frame, chunk, pl.ds(8 + side, patches, stride=2), :] = cells[:, 128 * chunk : 128 * (chunk + 1)]
    stacks = tap_rows(frames, [shifted(wide, f, broad, lat) for f in range(frames)], broad)
    copies = []
    for row in list(range(1, tall - 1)) + [0, tall - 1]:
        first, last = max(row - 1, 0), min(row + 1, tall - 1)
        total = jnp.zeros((frames * broad, kernel.shape[1]), F32)
        for shift_t in range(3):
            start = (3 * shift_t + first - (row - 1)) * span
            total += jnp.dot(
                stacks[shift_t][:, first * span : (last + 1) * span],
                kernel[start : start + (last + 1 - first) * span],
                preferred_element_type=F32,
            )
        if 0 < row < tall - 1:
            done[row - 1] = total.astype(BF16).reshape(done.shape[1:])
            copy = pltpu.make_async_copy(done.at[row - 1], features.at[:, row], sems.at[row - 1])
            copy.start()
            copies.append(copy)
        else:
            edges[0 if row == 0 else 1] = total
    for copy in copies:
        copy.wait()


def convolve_inner(predicted, picks, kernel):
    frames, patch_rows, patches, values = predicted.shape
    lat = values // 4
    tall, broad = 2 * patch_rows, 2 * patches
    channels = kernel.shape[1]
    lanes = -(-tall * 3 * lat // 128) * 128
    return pl.pallas_call(
        functools.partial(inner_body, lat),
        in_specs=[WHOLE] * 3,
        out_specs=[ANYWHERE, WHOLE],
        out_shape=[
            jax.ShapeDtypeStruct((frames, tall, broad, channels), BF16),
            jax.ShapeDtypeStruct((2, frames * broad, channels), F32),
        ],
        scratch_shapes=[
            pltpu.VMEM((frames, lanes // 128, broad + 16, 128), F32),
            pltpu.VMEM((tall - 2, frames, broad, channels), BF16),
            pltpu.SemaphoreType.DMA((tall - 2,)),
        ],
        compiler_params=params(16),
        cost_estimate=pl.CostEstimate(
            flops=2 * frames * tall * broad * 27 * lat * channels,
            bytes_accessed=2 * frames * tall * broad * channels,
            transcendentals=0,
        ),
        name="convolve_inner",
    )(predicted, picks, kernel)


def outer_body(lat, tile_ref, from_pair, from_next, picks, kernel, edges, given, features, wide, done, sems):
    frames, values = from_pair.shape[0], picks.shape[1]
    folds = 128 // values
    patches = from_pair.shape[1] * folds
    even = tile_ref[0] % 2 == 0
    broad = 2 * patches
    tall = features.shape[1]
    span = 3 * lat
    chunks = wide.shape[2]
    lanes = 128 * chunks
    lane = lax.broadcasted_iota(jnp.int32, (broad, lanes), 1)
    copies = []
    for edge in range(2):
        cells = []
        for frame in range(frames):
            rows = jnp.where(even == (edge == 0), from_next[frame], from_pair[frame])
            parts = [rows[:, k * values : (k + 1) * values] for k in range(folds)]
            cells.append(jnp.concatenate(parts, axis=0))
        wide[edge, :, :, 0:8] = jnp.zeros((frames, chunks, 8, 128), F32)
        wide[edge, :, :, 8 + broad :] = jnp.zeros((frames, chunks, 8, 128), F32)
        for side in range(2):
            for frame in range(frames):
                spread = jnp.dot(cells[frame], picks[side], preferred_element_type=F32)
                for chunk in range(chunks):
                    wide[edge, frame, chunk, pl.ds(8 + side, patches, stride=2), :] = spread[
                        :, 128 * chunk : 128 * (chunk + 1)
                    ]
        ready = [shifted(wide.at[edge], f, broad, lat) for f in range(frames)]
        rows = []
        for frame in range(frames):
            taps = jnp.zeros((broad, lanes), BF16)
            for shift_t in range(3):
                if frame + shift_t - 2 >= 0:
                    taps = jnp.where(lane // span == shift_t, ready[frame + shift_t - 2], taps)
            rows.append(taps)
        shift_y = 2 * edge
        panel = jnp.concatenate(
            [kernel[(3 * t + shift_y) * span : (3 * t + shift_y + 1) * span] for t in range(3)], axis=0
        )
        total = edges[edge] + jnp.dot(
            jnp.concatenate(rows, axis=0)[:, : 3 * span], panel, preferred_element_type=F32
        )
        done[edge] = total.astype(BF16).reshape(done.shape[1:])
        copy = pltpu.make_async_copy(done.at[edge], features.at[:, edge * (tall - 1)], sems.at[edge])
        copy.start()
        copies.append(copy)
    for copy in copies:
        copy.wait()


def convolve_outer(tile, from_pair, from_next, picks, kernel, edges, features):
    frames, tall, broad, _ = features.shape
    lat = picks.shape[1] // 2
    channels = kernel.shape[1]
    lanes = -(-9 * lat // 128) * 128
    return pl.pallas_call(
        functools.partial(outer_body, lat),
        in_specs=[SCALARS] + [WHOLE] * 5 + [ANYWHERE],
        out_specs=ANYWHERE,
        out_shape=jax.ShapeDtypeStruct(features.shape, BF16),
        input_output_aliases={6: 0},
        scratch_shapes=[
            pltpu.VMEM((2, frames, lanes // 128, broad + 16, 128), F32),
            pltpu.VMEM((2, frames, broad, channels), BF16),
            pltpu.SemaphoreType.DMA((2,)),
        ],
        compiler_params=params(16),
        name="convolve_outer",
    )(tile, from_pair, from_next, picks, kernel, edges, features)


def exchange(value, offset):
    count = lax.axis_size("seq")
    return lax.ppermute(value, "seq", [(i, i ^ offset) for i in range(count)])


def local(queries, own_kv, past_kv, block_home, block_list, list_len, final_weight, decoder_weight):
    frames, patch_rows, patches, width = queries.shape
    tokens = frames * patch_rows * patches
    count = lax.axis_size("seq")
    assert count & (count - 1) == 0
    bits = count.bit_length() - 1
    blocks_here = past_kv.shape[0]
    columns = final_weight.shape[1]
    tile = lax.axis_index("seq").astype(jnp.int32).reshape(1)
    query_rows = queries.reshape(tokens, width)
    own_rows = own_kv.reshape(tokens, own_kv.shape[3])
    shape = (frames, patch_rows, patches)
    inner_picks, outer_picks = spreads(columns // 4, patch_rows)
    half = KV_HEADS // 2
    lists = (tile, block_home, block_list, list_len)
    if count == 16 and columns % PART == 0 and decoder_weight.shape[1] % PART == 0:
        far = [4, 8, 12]
        turns = [(2, 0), (3, 1), (1, 2), (0, 3)]
        line = [exchange(past_kv, k) for k in reversed(far)][::-1]
        final, decode, own_rows, inner_picks, outer_picks = lax.optimization_barrier(
            (final_weight.T, decoder_weight.T, own_rows, inner_picks, outer_picks)
        )
        final_across, decode_across = exchange(final, 2), exchange(decode, 2)
        packed, sums, _ = attend_own(range(half), *lists, query_rows, own_rows, turns, blocks_here)
        *line, final_across, decode_across, packed = lax.optimization_barrier(
            (*line, final_across, decode_across, packed)
        )
        near = join([past_kv] + line, "join_near")
        across = exchange(near, 2)
        panels = pack(final, decode, final_across, decode_across)
        panels_far, panels_near = exchange(panels, 8), exchange(panels, 4)
        own_rows, near = lax.optimization_barrier((own_rows, near))
        others = attend_own(range(half, KV_HEADS), *lists, query_rows, own_rows, turns, blocks_here)
        packed, sums, slots = [packed, others[0]], [sums, others[1]], others[2]
        across, panels_far, panels_near, slots = lax.optimization_barrier((across, panels_far, panels_near, slots))
        gathered = join([near, across], "join_chip")
        gathered = [gathered, exchange(gathered, 1)]
        panels_last = exchange(panels_far, 4)
        panels = join([panels, panels_far, panels_near], "join_panels")
        panels_beside = exchange(panels, 1)
        attended = attend_past(slots, packed, sums, gathered, blocks_here)
        panels_last, panels_beside, attended = lax.optimization_barrier((panels_last, panels_beside, attended))
        panels = [panels, panels_last, panels_beside, exchange(panels_last, 1)]
        order = [k ^ x for k in (0, 8, 4, 12) for x in (0, 2)]
        order = order + [k ^ 1 for k in order]
        depth = final_weight.shape[0]
        part = project(tile, attended, panels[0], panels[2], order[:6], depth, columns)
        predicted, to_pair, to_next = finish(
            tile, attended, panels[1], panels[3], part, order[6:8], depth, shape
        )
        decode = unpack(tile, panels, order, final_weight.size // PART, *decoder_weight.shape)
    else:
        turns = [(bit, bits - 1 - bit) for bit in range(bits)]
        held = past_kv
        for bit in reversed(range(bits)):
            held = jnp.concatenate([held, exchange(held, 1 << bit)], axis=0)
        packed, sums, slots = attend_own(
            range(KV_HEADS), *lists, query_rows, own_rows, turns, blocks_here
        )
        attended = attend_past(slots, [packed], [sums], [held], blocks_here)
        final = lax.all_gather(final_weight, "seq", axis=0, tiled=True)
        decode = lax.all_gather(decoder_weight, "seq", axis=1, tiled=True)
        predicted = jnp.dot(attended, final, preferred_element_type=F32).astype(BF16)
        rows = predicted.reshape(shape + (columns,))
        values = columns // 2
        folds = 128 // values

        def folded(cells):
            parts = cells.reshape(frames, folds, patches // folds, values)
            return parts.transpose(0, 2, 1, 3).reshape(frames, patches // folds, 128)

        first, last = folded(rows[:, 0, :, :values]), folded(rows[:, -1, :, values:])
        even = tile[0] % 2 == 0
        to_pair, to_next = jnp.where(even, last, first), jnp.where(even, first, last)
    predicted = predicted.reshape(shape + (columns,))
    swaps = [(i, i + 1) for i in range(1, count - 1, 2)] + [(i + 1, i) for i in range(1, count - 1, 2)]
    from_next = lax.ppermute(to_next, "seq", swaps)
    from_pair = exchange(to_pair, 1)
    features, edges = convolve_inner(predicted, inner_picks, decode)
    return convolve_outer(tile, from_pair, from_next, outer_picks, decode, edges, features)


def solution(mesh):
    return jax.shard_map(
        local,
        mesh=mesh,
        in_specs=(
            P("groups", "seq", None, None),
            P("groups", "seq", None, None),
            P(("groups", "seq"), None, None),
            P("groups"),
            P("groups", None),
            P("groups"),
            P("seq", None),
            P(None, "seq"),
        ),
        out_specs=P("groups", "seq", None, None),
        check_vma=False,
    )
```

```python
import functools
import math

import jax
import jax.numpy as jnp
from jax import lax
from jax.experimental import pallas as pl
from jax.experimental.pallas import tpu as pltpu
from jax.sharding import PartitionSpec as P

HEADS = 24
KV_HEADS = 4
HEAD_DIM = 128
GROUP = HEADS // KV_HEADS
SCALE = math.log2(math.e) / math.sqrt(HEAD_DIM)
SAFE = 2.0**100
MIB = 1024 * 1024
PART = 16
WHOLE = pl.BlockSpec(memory_space=pltpu.VMEM)
ANYWHERE = pl.BlockSpec(memory_space=pl.ANY)
SCALARS = pl.BlockSpec(memory_space=pltpu.SMEM)
BF16 = jnp.bfloat16
F32 = jnp.float32


def head_columns(index):
    return slice(index * HEAD_DIM, (index + 1) * HEAD_DIM)


def params(mib):
    return pltpu.CompilerParams(vmem_limit_bytes=mib * MIB)


def place_of(offset, turns):
    return sum(((offset >> bit) & 1) << to for bit, to in turns)


def own_body(turns, blocks_here, groups, tile_ref, home, blocks, lens, queries, own, packed, sums, slots):
    tokens = queries.shape[0]
    tile = tile_ref[0]
    for place in range(slots.shape[0]):
        slots[place] = -1

    def find(entry, carry):
        stored = home[blocks[tile, entry]]
        slots[place_of((stored // blocks_here) ^ tile, turns)] = stored % blocks_here
        return carry

    if groups[-1] == KV_HEADS - 1:
        lax.fori_loop(0, lens[tile], find, 0)
    for index, g in enumerate(groups):
        query = jnp.concatenate([queries[:, head_columns(g * GROUP + h)] for h in range(GROUP)], axis=0)
        value = jnp.concatenate(
            [own[:, head_columns(KV_HEADS + g)], jnp.ones((tokens, HEAD_DIM), BF16)], axis=1
        )
        score = lax.dot_general(
            query, own[:, head_columns(g)], (((1,), (1,)), ((), ())), preferred_element_type=F32
        )
        top = jnp.max(score, axis=1, keepdims=True)
        weights = jnp.exp2((score - top) * SCALE).astype(BF16)
        mixed = jnp.dot(weights, value, preferred_element_type=F32)
        total = mixed[:, HEAD_DIM:]
        sums[index] = mixed[:, :HEAD_DIM] / total
        level = top + jnp.log2(total) * (1.0 / SCALE)
        high = level.astype(BF16).astype(F32)
        middle = (level - high).astype(BF16).astype(F32)
        low = level - high - middle
        lane = lax.broadcasted_iota(jnp.int32, level.shape, 1)
        extra = jnp.where(lane == 0, high, jnp.where(lane == 1, middle, jnp.where(lane == 2, low, 0.0)))
        packed[index, :, :HEAD_DIM] = query
        packed[index, :, HEAD_DIM:] = extra.astype(BF16)


def attend_own(groups, tile, block_home, block_list, list_len, query_rows, own_rows, turns, blocks_here):
    tokens, width = query_rows.shape
    rows = GROUP * tokens
    return pl.pallas_call(
        functools.partial(own_body, turns, blocks_here, groups),
        in_specs=[SCALARS] * 4 + [WHOLE] * 2,
        out_specs=[WHOLE, WHOLE, SCALARS],
        out_shape=[
            jax.ShapeDtypeStruct((len(groups), rows, 2 * HEAD_DIM), BF16),
            jax.ShapeDtypeStruct((len(groups), rows, HEAD_DIM), F32),
            jax.ShapeDtypeStruct((1 << len(turns),), jnp.int32),
        ],
        compiler_params=params(20),
        cost_estimate=pl.CostEstimate(
            flops=3 * len(groups) * tokens * tokens * width, bytes_accessed=0, transcendentals=0
        ),
        name="attend_own",
    )(tile, block_home, block_list, list_len, query_rows, own_rows)


def past_body(sizes, split, slots, *refs):
    packed, sums, refs = refs[:split], refs[split : 2 * split], refs[2 * split :]
    gathered, (out, keys, values, worst) = refs[: len(sizes)], refs[len(sizes) :]
    groups = KV_HEADS // split
    blocks_here = sum(ref.shape[0] for ref in gathered) // sum(sizes)
    block_tokens = gathered[0].shape[1]
    tokens = out.shape[0]
    lane = lax.broadcasted_iota(jnp.int32, (block_tokens, HEAD_DIM), 1)
    minus = jnp.where(lane < 3, -1.0, 0.0)
    zero = jnp.zeros((block_tokens, HEAD_DIM), BF16)
    homes = [(ref, k) for ref, size in zip(gathered, sizes) for k in range(size)]
    for place, (ref, k) in enumerate(homes):
        slot = slots[place]
        listed = slot >= 0
        block = ref[k * blocks_here + jnp.maximum(slot, 0)]
        live = jnp.where(listed, 1.0, 0.0)
        level = (minus * live).astype(BF16)
        counted = jnp.full((block_tokens, HEAD_DIM), live, F32).astype(BF16)
        rows = slice(place * block_tokens, (place + 1) * block_tokens)
        for g in range(KV_HEADS):
            keys[g, rows, :HEAD_DIM] = jnp.where(listed, block[:, head_columns(g)], zero)
            keys[g, rows, HEAD_DIM:] = level
            values[g, rows, :HEAD_DIM] = jnp.where(listed, block[:, head_columns(KV_HEADS + g)], zero)
            values[g, rows, HEAD_DIM:] = counted

    heads = GROUP if keys.shape[1] <= 512 else 1
    steps = KV_HEADS * GROUP // heads

    def over_steps(one, start):
        if heads == GROUP:
            for step in range(steps):
                start = one(step, start)
            return start
        return lax.fori_loop(0, steps, one, start)

    def place(step):
        if heads == GROUP:
            return step, slice(None)
        return step // GROUP, pl.ds(pl.multiple_of((step % GROUP) * tokens, tokens), tokens)

    def own_part(arrays, g, rows):
        if split == 1:
            return arrays[0][g, rows]
        return arrays[g // groups][g % groups, rows]

    def scores(g, rows):
        return SCALE * lax.dot_general(
            own_part(packed, g, rows), keys[g], (((1,), (1,)), ((), ())), preferred_element_type=F32
        )

    def emit(step, attended):
        attended = attended.astype(BF16)
        for h in range(heads):
            columns = (step * heads + h) * HEAD_DIM
            if heads == 1:
                columns = pl.multiple_of(columns, HEAD_DIM)
            out[:, pl.ds(columns, HEAD_DIM)] = attended[h * tokens : (h + 1) * tokens]

    def quick(step, score, largest):
        g, rows = place(step)
        weights = jnp.exp2(score).astype(BF16)
        mixed = jnp.dot(weights, values[g], preferred_element_type=F32)
        below = mixed[:, HEAD_DIM:] + 1.0
        emit(step, (mixed[:, :HEAD_DIM] + own_part(sums, g, rows)) / below)
        return jnp.maximum(largest, jnp.max(below.reshape((-1,) + largest.shape), axis=0))

    largest = jnp.zeros(worst.shape, F32)
    if heads == GROUP:
        score = scores(*place(0))
        for step in range(steps):
            ahead = scores(*place(step + 1)) if step + 1 < steps else None
            largest = quick(step, score, largest)
            score = ahead
    else:
        largest = over_steps(lambda step, seen: quick(step, scores(*place(step)), seen), largest)
    worst[...] = largest

    @pl.when(jnp.logical_not(jnp.max(worst[...]) < SAFE))
    def _():
        def careful(step, carry):
            g, rows = place(step)
            score = scores(g, rows)
            top = jnp.maximum(jnp.max(score, axis=1, keepdims=True), 0.0)
            weights = jnp.exp2(score - top).astype(BF16)
            mixed = jnp.dot(weights, values[g], preferred_element_type=F32)
            share = jnp.exp2(-top)
            joined = mixed[:, :HEAD_DIM] + share * own_part(sums, g, rows)
            emit(step, joined / (mixed[:, HEAD_DIM:] + share))
            return carry

        over_steps(careful, 0)


def attend_past(slots, packed, sums, gathered, blocks_here):
    heads = KV_HEADS
    rows = packed[0].shape[1]
    tokens = rows // GROUP
    sizes = [array.shape[0] // blocks_here for array in gathered]
    keys = sum(sizes) * gathered[0].shape[1]
    return pl.pallas_call(
        functools.partial(past_body, sizes, len(packed)),
        in_specs=[SCALARS] + [WHOLE] * (2 * len(packed) + len(gathered)),
        out_specs=WHOLE,
        out_shape=jax.ShapeDtypeStruct((tokens, HEADS * HEAD_DIM), BF16),
        scratch_shapes=[
            pltpu.VMEM((heads, keys, 2 * HEAD_DIM), BF16),
            pltpu.VMEM((heads, keys, 2 * HEAD_DIM), BF16),
            pltpu.VMEM((8, HEAD_DIM), F32),
        ],
        compiler_params=params(40 if keys > 256 else 24),
        cost_estimate=pl.CostEstimate(
            flops=10**10, bytes_accessed=0, transcendentals=0
        ),
        name="attend_past",
    )(slots, *packed, *sums, *gathered)


def join_body(*refs):
    *parts, out = refs
    row = 0
    for part in parts:
        out[row : row + part.shape[0]] = part[...]
        row += part.shape[0]


def join(parts, name):
    rows = sum(part.shape[0] for part in parts)
    return pl.pallas_call(
        join_body,
        in_specs=[WHOLE] * len(parts),
        out_specs=WHOLE,
        out_shape=jax.ShapeDtypeStruct((rows,) + parts[0].shape[1:], BF16),
        compiler_params=params(4),
        name=name,
    )(*parts)


def parts_of(panel):
    return [panel[row : row + PART] for row in range(0, panel.shape[0], PART)]


def pack_body(final, decode, final_across, decode_across, out):
    for k, (left, right) in enumerate(((final, decode), (final_across, decode_across))):
        parts = parts_of(left) + parts_of(right)
        blank = out.shape[2] - sum(part.shape[1] for part in parts)
        out[k] = jnp.concatenate(parts + [jnp.zeros((PART, blank), BF16)], axis=1)


def pack(final, decode, final_across, decode_across):
    lanes = (final.size + decode.size) // PART
    return pl.pallas_call(
        pack_body,
        in_specs=[WHOLE] * 4,
        out_specs=WHOLE,
        out_shape=jax.ShapeDtypeStruct((2, PART, -(-lanes // 128) * 128), BF16),
        compiler_params=params(4),
        name="pack",
    )(final, decode, final_across, decode_across)


def project_pairs(offsets, depth, columns, tile, attended, ours, theirs):
    even = tile % 2 == 0
    total = jnp.zeros((attended.shape[0], columns), F32)
    ours = [(ref, k) for ref in ours for k in range(ref.shape[0])]
    theirs = [(ref, k) for ref in theirs for k in range(ref.shape[0])]
    for offset, (our, i), (their, j) in zip(offsets, ours, theirs):
        left, right = our[i], their[j]
        left, right = jnp.where(even, left, right), jnp.where(even, right, left)
        rows = [
            jnp.concatenate([panel[:, part * depth : (part + 1) * depth] for panel in (left, right)], axis=1)
            for part in range(columns // PART)
        ]
        start = pl.multiple_of(((tile ^ offset) // 2) * (2 * depth), 128)
        total += lax.dot_general(
            attended[:, pl.ds(start, 2 * depth)],
            jnp.concatenate(rows, axis=0),
            (((1,), (1,)), ((), ())),
            preferred_element_type=F32,
        )
    return total


def project_body(offsets, depth, tile_ref, attended, ours, theirs, out):
    out[...] = project_pairs(offsets, depth, out.shape[1], tile_ref[0], attended, [ours], [theirs])


def project(tile, attended, ours, theirs, offsets, depth, columns):
    return pl.pallas_call(
        functools.partial(project_body, offsets, depth),
        in_specs=[SCALARS] + [WHOLE] * 3,
        out_specs=WHOLE,
        out_shape=jax.ShapeDtypeStruct((attended.shape[0], columns), F32),
        compiler_params=params(16),
        name="project",
    )(tile, attended, ours, theirs)


def finish_body(offsets, depth, shape, tile_ref, attended, ours, theirs, part, out, to_pair, to_next):
    frames, patch_rows, patches = shape
    tile = tile_ref[0]
    predicted = part[...] + project_pairs(offsets, depth, part.shape[1], tile, attended, [ours], [theirs])
    predicted = predicted.astype(BF16)
    out[...] = predicted
    even = tile % 2 == 0
    values = predicted.shape[1] // 2
    folds = 128 // values
    count = patches // folds

    def folded(rows):
        return jnp.concatenate([rows[k * count : (k + 1) * count] for k in range(folds)], axis=1)

    for frame in range(frames):
        rows = predicted[frame * patch_rows * patches : (frame + 1) * patch_rows * patches]
        first, last = folded(rows[:patches, :values]), folded(rows[(patch_rows - 1) * patches :, values:])
        to_pair[frame] = jnp.where(even, last, first)
        to_next[frame] = jnp.where(even, first, last)


def finish(tile, attended, ours, theirs, part, offsets, depth, shape):
    tokens, columns = part.shape
    border = jax.ShapeDtypeStruct((shape[0], shape[2] * (columns // 2) // 128, 128), BF16)
    return pl.pallas_call(
        functools.partial(finish_body, offsets, depth, shape),
        in_specs=[SCALARS] + [WHOLE] * 4,
        out_specs=[WHOLE] * 3,
        out_shape=[jax.ShapeDtypeStruct((tokens, columns), BF16), border, border],
        compiler_params=params(16),
        name="finish",
    )(tile, attended, ours, theirs, part)


def unpack_body(order, skip, tile_ref, *refs):
    *panels, out, staged = refs
    taps = out.shape[0]
    place = 0
    for panel in panels:
        for k in range(panel.shape[0]):
            staged[tile_ref[0] ^ order[place]] = panel[k]
            place += 1
    width = out.shape[1] // len(order)
    whole = [
        staged[device, :, skip + part * taps : skip + (part + 1) * taps]
        for device in range(len(order))
        for part in range(width // PART)
    ]
    out[...] = jnp.concatenate(whole, axis=0).T


def unpack(tile, panels, order, skip, taps, width):
    return pl.pallas_call(
        functools.partial(unpack_body, order, skip),
        in_specs=[SCALARS] + [WHOLE] * len(panels),
        out_specs=WHOLE,
        out_shape=jax.ShapeDtypeStruct((taps, width * len(order)), BF16),
        scratch_shapes=[pltpu.VMEM((len(order),) + panels[0].shape[1:], BF16)],
        compiler_params=params(16),
        name="unpack",
    )(tile, *panels)


def tap_rows(frames, cells, width):
    stacks = []
    for shift_t in range(3):
        rows = []
        for frame in range(frames):
            source = frame + shift_t - 2
            rows.append(cells[source] if source >= 0 else jnp.zeros((width, cells[0].shape[1]), BF16))
        stacks.append(jnp.concatenate(rows, axis=0))
    return stacks


def shifted(wide, frame, width, lat):
    chunks = []
    for chunk in range(wide.shape[1]):
        lane = lax.broadcasted_iota(jnp.int32, (width, 128), 1) + 128 * chunk
        shift = (lane // lat) % 3
        near = jnp.where(shift == 1, wide[frame, chunk, 8 : 8 + width], wide[frame, chunk, 9 : 9 + width])
        chunks.append(jnp.where(shift == 0, wide[frame, chunk, 7 : 7 + width], near).astype(BF16))
    return jnp.concatenate(chunks, axis=1)


def spread_body(lat, patch_rows, inner, outer):
    span = 3 * lat
    for side in range(2):
        source = lax.broadcasted_iota(jnp.int32, inner.shape[2:], 0)
        target = lax.broadcasted_iota(jnp.int32, inner.shape[2:], 1)
        for r in range(patch_rows):
            upper = target // span - 2 * r
            wanted = (upper >= 0) & (upper < 2) & (source == upper * 2 * lat + side * lat + target % lat)
            inner[side, r] = jnp.where(wanted, 1.0, 0.0).astype(BF16)
        source = lax.broadcasted_iota(jnp.int32, outer.shape[1:], 0)
        target = lax.broadcasted_iota(jnp.int32, outer.shape[1:], 1)
        wanted = (source == side * lat + target % lat) & (target < 3 * span)
        outer[side] = jnp.where(wanted, 1.0, 0.0).astype(BF16)


def spreads(lat, patch_rows):
    tall = 2 * patch_rows
    return pl.pallas_call(
        functools.partial(spread_body, lat, patch_rows),
        out_specs=[WHOLE, WHOLE],
        out_shape=[
            jax.ShapeDtypeStruct((2, patch_rows, 4 * lat, -(-tall * 3 * lat // 128) * 128), BF16),
            jax.ShapeDtypeStruct((2, 2 * lat, -(-9 * lat // 128) * 128), BF16),
        ],
        compiler_params=params(4),
        cost_estimate=pl.CostEstimate(flops=5 * 10**9, bytes_accessed=0, transcendentals=0),
        name="spreads",
    )()


def border_taps(lat, cells, picks, wide):
    frames, values = cells.shape[0], picks.shape[1]
    folds = 128 // values
    patches = cells.shape[1] * folds
    broad = 2 * patches
    chunks = wide.shape[1]
    span = 3 * lat
    wide[:, :, 0:8] = jnp.zeros((frames, chunks, 8, 128), F32)
    wide[:, :, 8 + broad :] = jnp.zeros((frames, chunks, 8, 128), F32)
    for frame in range(frames):
        folded = cells[frame]
        row = jnp.concatenate([folded[:, k * values : (k + 1) * values] for k in range(folds)], axis=0)
        for side in range(2):
            spread = jnp.dot(row, picks[side], preferred_element_type=F32)
            for chunk in range(chunks):
                wide[frame, chunk, pl.ds(8 + side, patches, stride=2), :] = spread[
                    :, 128 * chunk : 128 * (chunk + 1)
                ]
    ready = [shifted(wide, frame, broad, lat) for frame in range(frames)]
    lane = lax.broadcasted_iota(jnp.int32, ready[0].shape, 1)
    rows = []
    for frame in range(frames):
        taps = jnp.zeros(ready[0].shape, BF16)
        for shift_t in range(3):
            if frame + shift_t - 2 >= 0:
                taps = jnp.where(lane // span == shift_t, ready[frame + shift_t - 2], taps)
        rows.append(taps[:, : 3 * span])
    return rows


def border_panel(lat, kernel, edge):
    span = 3 * lat
    starts = [pl.multiple_of((3 * shift_t + 2 * edge) * span, lat) for shift_t in range(3)]
    return jnp.concatenate([kernel[pl.ds(start, span)] for start in starts], axis=0)


def inner_body(
    lat, tile_ref, predicted, from_pair, inner_picks, outer_picks, kernel, features, edge_sum,
    wide, border, done, sems
):
    frames, patch_rows, patches, _ = predicted.shape
    tall, broad = 2 * patch_rows, 2 * patches
    span = 3 * lat
    chunks = wide.shape[1]
    even = tile_ref[0] % 2 == 0
    pair_edge = jnp.where(even, 1, 0)
    wide[:, :, 0:8] = jnp.zeros((frames, chunks, 8, 128), F32)
    wide[:, :, 8 + broad :] = jnp.zeros((frames, chunks, 8, 128), F32)
    for side in range(2):
        for frame in range(frames):
            cells = jnp.zeros((patches, 128 * chunks), F32)
            for r in range(patch_rows):
                cells += jnp.dot(predicted[frame, r], inner_picks[side, r], preferred_element_type=F32)
            for chunk in range(chunks):
                wide[frame, chunk, pl.ds(8 + side, patches, stride=2), :] = cells[:, 128 * chunk : 128 * (chunk + 1)]
    stacks = tap_rows(frames, [shifted(wide, f, broad, lat) for f in range(frames)], broad)

    def own_sum(row):
        first, last = max(row - 1, 0), min(row + 1, tall - 1)
        total = jnp.zeros((frames * broad, kernel.shape[1]), F32)
        for shift_t in range(3):
            start = (3 * shift_t + first - (row - 1)) * span
            total += jnp.dot(
                stacks[shift_t][:, first * span : (last + 1) * span],
                kernel[start : start + (last + 1 - first) * span],
                preferred_element_type=F32,
            )
        return total

    copies = []

    def send(index, row, total):
        done[index] = total.astype(BF16).reshape(done.shape[1:])
        copy = pltpu.make_async_copy(done.at[index], features.at[:, row], sems.at[index])
        copy.start()
        copies.append(copy)

    for row in range(1, tall - 1):
        send(row - 1, row, own_sum(row))
    first, last = own_sum(0), own_sum(tall - 1)
    edge_sum[...] = jnp.where(even, first, last)
    taps = jnp.concatenate(border_taps(lat, from_pair, outer_picks, border), axis=0)
    total = jnp.where(even, last, first) + jnp.dot(
        taps, border_panel(lat, kernel, pair_edge), preferred_element_type=F32
    )
    send(tall - 2, pair_edge * (tall - 1), total)
    for copy in copies:
        copy.wait()


def border_lanes(lat):
    return -(-9 * lat // 128)


def convolve_inner(tile, predicted, from_pair, inner_picks, outer_picks, kernel):
    frames, patch_rows, patches, values = predicted.shape
    lat = values // 4
    tall, broad = 2 * patch_rows, 2 * patches
    channels = kernel.shape[1]
    lanes = -(-tall * 3 * lat // 128) * 128
    return pl.pallas_call(
        functools.partial(inner_body, lat),
        in_specs=[SCALARS] + [WHOLE] * 5,
        out_specs=[ANYWHERE, WHOLE],
        out_shape=[
            jax.ShapeDtypeStruct((frames, tall, broad, channels), BF16),
            jax.ShapeDtypeStruct((frames * broad, channels), F32),
        ],
        scratch_shapes=[
            pltpu.VMEM((frames, lanes // 128, broad + 16, 128), F32),
            pltpu.VMEM((frames, border_lanes(lat), broad + 16, 128), F32),
            pltpu.VMEM((tall - 1, frames, broad, channels), BF16),
            pltpu.SemaphoreType.DMA((tall - 1,)),
        ],
        compiler_params=params(16),
        cost_estimate=pl.CostEstimate(
            flops=2 * frames * tall * broad * 27 * lat * channels,
            bytes_accessed=2 * frames * tall * broad * channels,
            transcendentals=0,
        ),
        name="convolve_inner",
    )(tile, predicted, from_pair, inner_picks, outer_picks, kernel)


def outer_body(lat, tile_ref, from_next, picks, kernel, edge_sum, given, features, wide, done, sems):
    frames, tall, broad, _ = features.shape
    edge = jnp.where(tile_ref[0] % 2 == 0, 0, 1)
    panel = border_panel(lat, kernel, edge)
    copies = []
    for frame, taps in enumerate(border_taps(lat, from_next, picks, wide)):
        total = edge_sum[frame * broad : (frame + 1) * broad] + jnp.dot(
            taps, panel, preferred_element_type=F32
        )
        done[frame] = total.astype(BF16)
        copy = pltpu.make_async_copy(done.at[frame], features.at[frame, edge * (tall - 1)], sems.at[frame])
        copy.start()
        copies.append(copy)
    for copy in copies:
        copy.wait()


def convolve_outer(tile, from_next, picks, kernel, edge_sum, features):
    frames, tall, broad, channels = features.shape
    lat = picks.shape[1] // 2
    return pl.pallas_call(
        functools.partial(outer_body, lat),
        in_specs=[SCALARS] + [WHOLE] * 4 + [ANYWHERE],
        out_specs=ANYWHERE,
        out_shape=jax.ShapeDtypeStruct(features.shape, BF16),
        input_output_aliases={5: 0},
        scratch_shapes=[
            pltpu.VMEM((frames, border_lanes(lat), broad + 16, 128), F32),
            pltpu.VMEM((frames, broad, channels), BF16),
            pltpu.SemaphoreType.DMA((frames,)),
        ],
        compiler_params=params(16),
        name="convolve_outer",
    )(tile, from_next, picks, kernel, edge_sum, features)


def exchange(value, offset):
    count = lax.axis_size("seq")
    return lax.ppermute(value, "seq", [(i, i ^ offset) for i in range(count)])


def local(queries, own_kv, past_kv, block_home, block_list, list_len, final_weight, decoder_weight):
    frames, patch_rows, patches, width = queries.shape
    tokens = frames * patch_rows * patches
    count = lax.axis_size("seq")
    assert count & (count - 1) == 0
    bits = count.bit_length() - 1
    blocks_here = past_kv.shape[0]
    columns = final_weight.shape[1]
    tile = lax.axis_index("seq").astype(jnp.int32).reshape(1)
    query_rows = queries.reshape(tokens, width)
    own_rows = own_kv.reshape(tokens, own_kv.shape[3])
    shape = (frames, patch_rows, patches)
    inner_picks, outer_picks = spreads(columns // 4, patch_rows)
    half = KV_HEADS // 2
    lists = (tile, block_home, block_list, list_len)
    if count == 16 and columns % PART == 0 and decoder_weight.shape[1] % PART == 0:
        far = [4, 8, 12]
        turns = [(2, 0), (3, 1), (1, 2), (0, 3)]
        line = [exchange(past_kv, k) for k in reversed(far)][::-1]
        final, decode, own_rows, inner_picks, outer_picks = lax.optimization_barrier(
            (final_weight.T, decoder_weight.T, own_rows, inner_picks, outer_picks)
        )
        final_across, decode_across = exchange(final, 2), exchange(decode, 2)
        packed, sums, _ = attend_own(range(half), *lists, query_rows, own_rows, turns, blocks_here)
        *line, final_across, decode_across, packed = lax.optimization_barrier(
            (*line, final_across, decode_across, packed)
        )
        near = join([past_kv] + line, "join_near")
        across = exchange(near, 2)
        panels = pack(final, decode, final_across, decode_across)
        panels_far, panels_near = exchange(panels, 8), exchange(panels, 4)
        own_rows, near = lax.optimization_barrier((own_rows, near))
        others = attend_own(range(half, KV_HEADS), *lists, query_rows, own_rows, turns, blocks_here)
        packed, sums, slots = [packed, others[0]], [sums, others[1]], others[2]
        across, panels_far, panels_near, slots = lax.optimization_barrier((across, panels_far, panels_near, slots))
        gathered = join([near, across], "join_chip")
        gathered = [gathered, exchange(gathered, 1)]
        panels_last = exchange(panels_far, 4)
        panels = join([panels, panels_far, panels_near], "join_panels")
        panels_beside = exchange(panels, 1)
        attended = attend_past(slots, packed, sums, gathered, blocks_here)
        panels_last, panels_beside, attended = lax.optimization_barrier((panels_last, panels_beside, attended))
        panels = [panels, panels_last, panels_beside, exchange(panels_last, 1)]
        order = [k ^ x for k in (0, 8, 4, 12) for x in (0, 2)]
        order = order + [k ^ 1 for k in order]
        depth = final_weight.shape[0]
        part = project(tile, attended, panels[0], panels[2], order[:6], depth, columns)
        predicted, to_pair, to_next = finish(
            tile, attended, panels[1], panels[3], part, order[6:8], depth, shape
        )
        decode = unpack(tile, panels, order, final_weight.size // PART, *decoder_weight.shape)
    else:
        turns = [(bit, bits - 1 - bit) for bit in range(bits)]
        held = past_kv
        for bit in reversed(range(bits)):
            held = jnp.concatenate([held, exchange(held, 1 << bit)], axis=0)
        packed, sums, slots = attend_own(
            range(KV_HEADS), *lists, query_rows, own_rows, turns, blocks_here
        )
        attended = attend_past(slots, [packed], [sums], [held], blocks_here)
        final = lax.all_gather(final_weight, "seq", axis=0, tiled=True)
        decode = lax.all_gather(decoder_weight, "seq", axis=1, tiled=True)
        predicted = jnp.dot(attended, final, preferred_element_type=F32).astype(BF16)
        rows = predicted.reshape(shape + (columns,))
        values = columns // 2
        folds = 128 // values

        def folded(cells):
            parts = cells.reshape(frames, folds, patches // folds, values)
            return parts.transpose(0, 2, 1, 3).reshape(frames, patches // folds, 128)

        first, last = folded(rows[:, 0, :, :values]), folded(rows[:, -1, :, values:])
        even = tile[0] % 2 == 0
        to_pair, to_next = jnp.where(even, last, first), jnp.where(even, first, last)
    predicted = predicted.reshape(shape + (columns,))
    swaps = [(i, i + 1) for i in range(1, count - 1, 2)] + [(i + 1, i) for i in range(1, count - 1, 2)]
    from_next = lax.ppermute(to_next, "seq", swaps)
    from_pair = exchange(to_pair, 1)
    features, edge_sum = convolve_inner(tile, predicted, from_pair, inner_picks, outer_picks, decode)
    return convolve_outer(tile, from_next, outer_picks, decode, edge_sum, features)


def solution(mesh):
    return jax.shard_map(
        local,
        mesh=mesh,
        in_specs=(
            P("groups", "seq", None, None),
            P("groups", "seq", None, None),
            P(("groups", "seq"), None, None),
            P("groups"),
            P("groups", None),
            P("groups"),
            P("seq", None),
            P(None, "seq"),
        ),
        out_specs=P("groups", "seq", None, None),
        check_vma=False,
    )
```

```python
import functools
import math

import jax
import jax.numpy as jnp
from jax import lax
from jax.experimental import pallas as pl
from jax.experimental.pallas import tpu as pltpu
from jax.sharding import PartitionSpec as P

HEADS = 24
KV_HEADS = 4
HEAD_DIM = 128
GROUP = HEADS // KV_HEADS
SCALE = math.log2(math.e) / math.sqrt(HEAD_DIM)
SAFE = 2.0**100
MIB = 1024 * 1024
PART = 16
WHOLE = pl.BlockSpec(memory_space=pltpu.VMEM)
ANYWHERE = pl.BlockSpec(memory_space=pl.ANY)
SCALARS = pl.BlockSpec(memory_space=pltpu.SMEM)
BF16 = jnp.bfloat16
F32 = jnp.float32


def head_columns(index):
    return slice(index * HEAD_DIM, (index + 1) * HEAD_DIM)


def params(mib):
    return pltpu.CompilerParams(vmem_limit_bytes=mib * MIB)


def place_of(offset, turns):
    return sum(((offset >> bit) & 1) << to for bit, to in turns)


def own_body(turns, blocks_here, groups, tile_ref, home, blocks, lens, queries, own, packed, sums, slots):
    tokens = queries.shape[0]
    tile = tile_ref[0]
    for place in range(slots.shape[0]):
        slots[place] = -1

    def find(entry, carry):
        stored = home[blocks[tile, entry]]
        slots[place_of((stored // blocks_here) ^ tile, turns)] = stored % blocks_here
        return carry

    if groups[-1] == KV_HEADS - 1:
        lax.fori_loop(0, lens[tile], find, 0)
    for index, g in enumerate(groups):
        query = jnp.concatenate([queries[:, head_columns(g * GROUP + h)] for h in range(GROUP)], axis=0)
        value = jnp.concatenate(
            [own[:, head_columns(KV_HEADS + g)], jnp.ones((tokens, HEAD_DIM), BF16)], axis=1
        )
        score = lax.dot_general(
            query, own[:, head_columns(g)], (((1,), (1,)), ((), ())), preferred_element_type=F32
        )
        top = jnp.max(score, axis=1, keepdims=True)
        weights = jnp.exp2((score - top) * SCALE).astype(BF16)
        mixed = jnp.dot(weights, value, preferred_element_type=F32)
        total = mixed[:, HEAD_DIM:]
        sums[index] = mixed[:, :HEAD_DIM] / total
        level = top + jnp.log2(total) * (1.0 / SCALE)
        high = level.astype(BF16).astype(F32)
        middle = (level - high).astype(BF16).astype(F32)
        low = level - high - middle
        lane = lax.broadcasted_iota(jnp.int32, level.shape, 1)
        extra = jnp.where(lane == 0, high, jnp.where(lane == 1, middle, jnp.where(lane == 2, low, 0.0)))
        packed[index, :, :HEAD_DIM] = query
        packed[index, :, HEAD_DIM:] = extra.astype(BF16)


def attend_own(groups, tile, block_home, block_list, list_len, query_rows, own_rows, turns, blocks_here):
    tokens, width = query_rows.shape
    rows = GROUP * tokens
    return pl.pallas_call(
        functools.partial(own_body, turns, blocks_here, groups),
        in_specs=[SCALARS] * 4 + [WHOLE] * 2,
        out_specs=[WHOLE, WHOLE, SCALARS],
        out_shape=[
            jax.ShapeDtypeStruct((len(groups), rows, 2 * HEAD_DIM), BF16),
            jax.ShapeDtypeStruct((len(groups), rows, HEAD_DIM), F32),
            jax.ShapeDtypeStruct((1 << len(turns),), jnp.int32),
        ],
        compiler_params=params(20),
        cost_estimate=pl.CostEstimate(
            flops=3 * len(groups) * tokens * tokens * width, bytes_accessed=0, transcendentals=0
        ),
        name="attend_own",
    )(tile, block_home, block_list, list_len, query_rows, own_rows)


def past_body(sizes, split, slots, *refs):
    packed, sums, refs = refs[:split], refs[split : 2 * split], refs[2 * split :]
    gathered, (out, keys, values, worst) = refs[: len(sizes)], refs[len(sizes) :]
    groups = KV_HEADS // split
    blocks_here = sum(ref.shape[0] for ref in gathered) // sum(sizes)
    block_tokens = gathered[0].shape[1]
    tokens = out.shape[0]
    lane = lax.broadcasted_iota(jnp.int32, (block_tokens, HEAD_DIM), 1)
    minus = jnp.where(lane < 3, -1.0, 0.0)
    zero = jnp.zeros((block_tokens, HEAD_DIM), BF16)
    homes = [(ref, k) for ref, size in zip(gathered, sizes) for k in range(size)]
    for place, (ref, k) in enumerate(homes):
        slot = slots[place]
        listed = slot >= 0
        block = ref[k * blocks_here + jnp.maximum(slot, 0)]
        live = jnp.where(listed, 1.0, 0.0)
        level = (minus * live).astype(BF16)
        counted = jnp.full((block_tokens, HEAD_DIM), live, F32).astype(BF16)
        rows = slice(place * block_tokens, (place + 1) * block_tokens)
        for g in range(KV_HEADS):
            keys[g, rows, :HEAD_DIM] = jnp.where(listed, block[:, head_columns(g)], zero)
            keys[g, rows, HEAD_DIM:] = level
            values[g, rows, :HEAD_DIM] = jnp.where(listed, block[:, head_columns(KV_HEADS + g)], zero)
            values[g, rows, HEAD_DIM:] = counted

    heads = GROUP if keys.shape[1] <= 512 else 1
    steps = KV_HEADS * GROUP // heads

    def over_steps(one, start):
        if heads == GROUP:
            for step in range(steps):
                start = one(step, start)
            return start
        return lax.fori_loop(0, steps, one, start)

    def place(step):
        if heads == GROUP:
            return step, slice(None)
        return step // GROUP, pl.ds(pl.multiple_of((step % GROUP) * tokens, tokens), tokens)

    def own_part(arrays, g, rows):
        if split == 1:
            return arrays[0][g, rows]
        return arrays[g // groups][g % groups, rows]

    def scores(g, rows):
        return SCALE * lax.dot_general(
            own_part(packed, g, rows), keys[g], (((1,), (1,)), ((), ())), preferred_element_type=F32
        )

    def emit(step, attended):
        attended = attended.astype(BF16)
        for h in range(heads):
            columns = (step * heads + h) * HEAD_DIM
            if heads == 1:
                columns = pl.multiple_of(columns, HEAD_DIM)
            out[:, pl.ds(columns, HEAD_DIM)] = attended[h * tokens : (h + 1) * tokens]

    def quick(step, score, largest):
        g, rows = place(step)
        weights = jnp.exp2(score).astype(BF16)
        mixed = jnp.dot(weights, values[g], preferred_element_type=F32)
        below = mixed[:, HEAD_DIM:] + 1.0
        emit(step, (mixed[:, :HEAD_DIM] + own_part(sums, g, rows)) / below)
        return jnp.maximum(largest, jnp.max(below.reshape((-1,) + largest.shape), axis=0))

    largest = jnp.zeros(worst.shape, F32)
    if heads == GROUP:
        score = scores(*place(0))
        for step in range(steps):
            ahead = scores(*place(step + 1)) if step + 1 < steps else None
            largest = quick(step, score, largest)
            score = ahead
    else:
        largest = over_steps(lambda step, seen: quick(step, scores(*place(step)), seen), largest)
    worst[...] = largest

    @pl.when(jnp.logical_not(jnp.max(worst[...]) < SAFE))
    def _():
        def careful(step, carry):
            g, rows = place(step)
            score = scores(g, rows)
            top = jnp.maximum(jnp.max(score, axis=1, keepdims=True), 0.0)
            weights = jnp.exp2(score - top).astype(BF16)
            mixed = jnp.dot(weights, values[g], preferred_element_type=F32)
            share = jnp.exp2(-top)
            joined = mixed[:, :HEAD_DIM] + share * own_part(sums, g, rows)
            emit(step, joined / (mixed[:, HEAD_DIM:] + share))
            return carry

        over_steps(careful, 0)


def attend_past(slots, packed, sums, gathered, blocks_here):
    heads = KV_HEADS
    rows = packed[0].shape[1]
    tokens = rows // GROUP
    sizes = [array.shape[0] // blocks_here for array in gathered]
    keys = sum(sizes) * gathered[0].shape[1]
    return pl.pallas_call(
        functools.partial(past_body, sizes, len(packed)),
        in_specs=[SCALARS] + [WHOLE] * (2 * len(packed) + len(gathered)),
        out_specs=WHOLE,
        out_shape=jax.ShapeDtypeStruct((tokens, HEADS * HEAD_DIM), BF16),
        scratch_shapes=[
            pltpu.VMEM((heads, keys, 2 * HEAD_DIM), BF16),
            pltpu.VMEM((heads, keys, 2 * HEAD_DIM), BF16),
            pltpu.VMEM((8, HEAD_DIM), F32),
        ],
        compiler_params=params(40 if keys > 256 else 24),
        cost_estimate=pl.CostEstimate(
            flops=10**10, bytes_accessed=0, transcendentals=0
        ),
        name="attend_past",
    )(slots, *packed, *sums, *gathered)


def join_body(*refs):
    *parts, out = refs
    row = 0
    for part in parts:
        out[row : row + part.shape[0]] = part[...]
        row += part.shape[0]


def join(parts, name):
    rows = sum(part.shape[0] for part in parts)
    return pl.pallas_call(
        join_body,
        in_specs=[WHOLE] * len(parts),
        out_specs=WHOLE,
        out_shape=jax.ShapeDtypeStruct((rows,) + parts[0].shape[1:], BF16),
        compiler_params=params(4),
        name=name,
    )(*parts)


def parts_of(panel):
    return [panel[row : row + PART] for row in range(0, panel.shape[0], PART)]


def pack_body(final, decode, final_across, decode_across, out):
    for k, (left, right) in enumerate(((final, decode), (final_across, decode_across))):
        parts = parts_of(left) + parts_of(right)
        blank = out.shape[2] - sum(part.shape[1] for part in parts)
        out[k] = jnp.concatenate(parts + [jnp.zeros((PART, blank), BF16)], axis=1)


def pack(final, decode, final_across, decode_across):
    lanes = (final.size + decode.size) // PART
    return pl.pallas_call(
        pack_body,
        in_specs=[WHOLE] * 4,
        out_specs=WHOLE,
        out_shape=jax.ShapeDtypeStruct((2, PART, -(-lanes // 128) * 128), BF16),
        compiler_params=params(4),
        name="pack",
    )(final, decode, final_across, decode_across)


def project_pairs(offsets, depth, columns, tile, attended, ours, theirs):
    even = tile % 2 == 0
    total = jnp.zeros((attended.shape[0], columns), F32)
    ours = [(ref, k) for ref in ours for k in range(ref.shape[0])]
    theirs = [(ref, k) for ref in theirs for k in range(ref.shape[0])]
    for offset, (our, i), (their, j) in zip(offsets, ours, theirs):
        left, right = our[i], their[j]
        left, right = jnp.where(even, left, right), jnp.where(even, right, left)
        rows = [
            jnp.concatenate([panel[:, part * depth : (part + 1) * depth] for panel in (left, right)], axis=1)
            for part in range(columns // PART)
        ]
        start = pl.multiple_of(((tile ^ offset) // 2) * (2 * depth), 128)
        total += lax.dot_general(
            attended[:, pl.ds(start, 2 * depth)],
            jnp.concatenate(rows, axis=0),
            (((1,), (1,)), ((), ())),
            preferred_element_type=F32,
        )
    return total


def project_body(offsets, depth, tile_ref, attended, ours, theirs, out):
    out[...] = project_pairs(offsets, depth, out.shape[1], tile_ref[0], attended, [ours], [theirs])


def project(tile, attended, ours, theirs, offsets, depth, columns):
    return pl.pallas_call(
        functools.partial(project_body, offsets, depth),
        in_specs=[SCALARS] + [WHOLE] * 3,
        out_specs=WHOLE,
        out_shape=jax.ShapeDtypeStruct((attended.shape[0], columns), F32),
        compiler_params=params(16),
        name="project",
    )(tile, attended, ours, theirs)


def finish_body(offsets, depth, shape, tile_ref, attended, ours, theirs, part, out, to_pair, to_next):
    frames, patch_rows, patches = shape
    tile = tile_ref[0]
    predicted = part[...] + project_pairs(offsets, depth, part.shape[1], tile, attended, [ours], [theirs])
    predicted = predicted.astype(BF16)
    out[...] = predicted
    even = tile % 2 == 0
    values = predicted.shape[1] // 2
    folds = 128 // values
    count = patches // folds

    def folded(rows):
        return jnp.concatenate([rows[k * count : (k + 1) * count] for k in range(folds)], axis=1)

    for frame in range(frames):
        rows = predicted[frame * patch_rows * patches : (frame + 1) * patch_rows * patches]
        first, last = folded(rows[:patches, :values]), folded(rows[(patch_rows - 1) * patches :, values:])
        to_pair[frame] = jnp.where(even, last, first)
        to_next[frame] = jnp.where(even, first, last)


def finish(tile, attended, ours, theirs, part, offsets, depth, shape):
    tokens, columns = part.shape
    border = jax.ShapeDtypeStruct((shape[0], shape[2] * (columns // 2) // 128, 128), BF16)
    return pl.pallas_call(
        functools.partial(finish_body, offsets, depth, shape),
        in_specs=[SCALARS] + [WHOLE] * 4,
        out_specs=[WHOLE] * 3,
        out_shape=[jax.ShapeDtypeStruct((tokens, columns), BF16), border, border],
        compiler_params=params(16),
        name="finish",
    )(tile, attended, ours, theirs, part)


def unpack_body(order, skip, tile_ref, *refs):
    *panels, out, staged = refs
    taps = out.shape[0]
    place = 0
    for panel in panels:
        for k in range(panel.shape[0]):
            staged[tile_ref[0] ^ order[place]] = panel[k]
            place += 1
    width = out.shape[1] // len(order)
    whole = [
        staged[device, :, skip + part * taps : skip + (part + 1) * taps]
        for device in range(len(order))
        for part in range(width // PART)
    ]
    out[...] = jnp.concatenate(whole, axis=0).T


def unpack(tile, panels, order, skip, taps, width):
    return pl.pallas_call(
        functools.partial(unpack_body, order, skip),
        in_specs=[SCALARS] + [WHOLE] * len(panels),
        out_specs=WHOLE,
        out_shape=jax.ShapeDtypeStruct((taps, width * len(order)), BF16),
        scratch_shapes=[pltpu.VMEM((len(order),) + panels[0].shape[1:], BF16)],
        compiler_params=params(16),
        name="unpack",
    )(tile, *panels)


def tap_rows(frames, cells, width):
    stacks = []
    for shift_t in range(3):
        rows = []
        for frame in range(frames):
            source = frame + shift_t - 2
            rows.append(cells[source] if source >= 0 else jnp.zeros((width, cells[0].shape[1]), BF16))
        stacks.append(jnp.concatenate(rows, axis=0))
    return stacks


def shifted(wide, frame, width, lat):
    chunks = []
    for chunk in range(wide.shape[1]):
        lane = lax.broadcasted_iota(jnp.int32, (width, 128), 1) + 128 * chunk
        shift = (lane // lat) % 3
        near = jnp.where(shift == 1, wide[frame, chunk, 8 : 8 + width], wide[frame, chunk, 9 : 9 + width])
        chunks.append(jnp.where(shift == 0, wide[frame, chunk, 7 : 7 + width], near).astype(BF16))
    return jnp.concatenate(chunks, axis=1)


def spread_body(lat, patch_rows, inner, outer):
    span = 3 * lat
    for side in range(2):
        source = lax.broadcasted_iota(jnp.int32, inner.shape[2:], 0)
        target = lax.broadcasted_iota(jnp.int32, inner.shape[2:], 1)
        for r in range(patch_rows):
            upper = target // span - 2 * r
            wanted = (upper >= 0) & (upper < 2) & (source == upper * 2 * lat + side * lat + target % lat)
            inner[side, r] = jnp.where(wanted, 1.0, 0.0).astype(BF16)
        source = lax.broadcasted_iota(jnp.int32, outer.shape[1:], 0)
        target = lax.broadcasted_iota(jnp.int32, outer.shape[1:], 1)
        wanted = (source == side * lat + target % lat) & (target < 3 * span)
        outer[side] = jnp.where(wanted, 1.0, 0.0).astype(BF16)


def spreads(lat, patch_rows):
    tall = 2 * patch_rows
    return pl.pallas_call(
        functools.partial(spread_body, lat, patch_rows),
        out_specs=[WHOLE, WHOLE],
        out_shape=[
            jax.ShapeDtypeStruct((2, patch_rows, 4 * lat, -(-tall * 3 * lat // 128) * 128), BF16),
            jax.ShapeDtypeStruct((2, 2 * lat, -(-9 * lat // 128) * 128), BF16),
        ],
        compiler_params=params(4),
        cost_estimate=pl.CostEstimate(flops=5 * 10**9, bytes_accessed=0, transcendentals=0),
        name="spreads",
    )()


def border_taps(lat, cells, picks, wide):
    frames, values = cells.shape[0], picks.shape[1]
    folds = 128 // values
    patches = cells.shape[1] * folds
    broad = 2 * patches
    chunks = wide.shape[1]
    span = 3 * lat
    wide[:, :, 0:8] = jnp.zeros((frames, chunks, 8, 128), F32)
    wide[:, :, 8 + broad :] = jnp.zeros((frames, chunks, 8, 128), F32)
    for frame in range(frames):
        folded = cells[frame]
        row = jnp.concatenate([folded[:, k * values : (k + 1) * values] for k in range(folds)], axis=0)
        for side in range(2):
            spread = jnp.dot(row, picks[side], preferred_element_type=F32)
            for chunk in range(chunks):
                wide[frame, chunk, pl.ds(8 + side, patches, stride=2), :] = spread[
                    :, 128 * chunk : 128 * (chunk + 1)
                ]
    ready = [shifted(wide, frame, broad, lat) for frame in range(frames)]
    lane = lax.broadcasted_iota(jnp.int32, ready[0].shape, 1)
    rows = []
    for frame in range(frames):
        taps = jnp.zeros(ready[0].shape, BF16)
        for shift_t in range(3):
            if frame + shift_t - 2 >= 0:
                taps = jnp.where(lane // span == shift_t, ready[frame + shift_t - 2], taps)
        rows.append(taps[:, : 3 * span])
    return rows


def border_panel(lat, kernel, edge):
    span = 3 * lat
    starts = [pl.multiple_of((3 * shift_t + 2 * edge) * span, lat) for shift_t in range(3)]
    return jnp.concatenate([kernel[pl.ds(start, span)] for start in starts], axis=0)


def inner_body(
    lat, tile_ref, predicted, from_pair, inner_picks, outer_picks, kernel, features, edge_sum, pair_row,
    wide, border, done, sems
):
    frames, patch_rows, patches, _ = predicted.shape
    tall, broad = 2 * patch_rows, 2 * patches
    span = 3 * lat
    chunks = wide.shape[1]
    even = tile_ref[0] % 2 == 0
    pair_edge = jnp.where(even, 1, 0)
    wide[:, :, 0:8] = jnp.zeros((frames, chunks, 8, 128), F32)
    wide[:, :, 8 + broad :] = jnp.zeros((frames, chunks, 8, 128), F32)
    for side in range(2):
        for frame in range(frames):
            cells = jnp.zeros((patches, 128 * chunks), F32)
            for r in range(patch_rows):
                cells += jnp.dot(predicted[frame, r], inner_picks[side, r], preferred_element_type=F32)
            for chunk in range(chunks):
                wide[frame, chunk, pl.ds(8 + side, patches, stride=2), :] = cells[:, 128 * chunk : 128 * (chunk + 1)]
    stacks = tap_rows(frames, [shifted(wide, f, broad, lat) for f in range(frames)], broad)

    def own_sum(row):
        first, last = max(row - 1, 0), min(row + 1, tall - 1)
        total = jnp.zeros((frames * broad, kernel.shape[1]), F32)
        for shift_t in range(3):
            start = (3 * shift_t + first - (row - 1)) * span
            total += jnp.dot(
                stacks[shift_t][:, first * span : (last + 1) * span],
                kernel[start : start + (last + 1 - first) * span],
                preferred_element_type=F32,
            )
        return total

    copies = []

    def send(index, row, total):
        done[index] = total.astype(BF16).reshape(done.shape[1:])
        copy = pltpu.make_async_copy(done.at[index], features.at[:, row], sems.at[index])
        copy.start()
        copies.append(copy)

    for row in range(1, tall - 1):
        send(row - 1, row, own_sum(row))
    first, last = own_sum(0), own_sum(tall - 1)
    edge_sum[...] = jnp.where(even, first, last)
    taps = jnp.concatenate(border_taps(lat, from_pair, outer_picks, border), axis=0)
    total = jnp.where(even, last, first) + jnp.dot(
        taps, border_panel(lat, kernel, pair_edge), preferred_element_type=F32
    )
    pair_row[...] = total.astype(BF16).reshape(pair_row.shape)
    for copy in copies:
        copy.wait()


def border_lanes(lat):
    return -(-9 * lat // 128)


def convolve_inner(tile, predicted, from_pair, inner_picks, outer_picks, kernel):
    frames, patch_rows, patches, values = predicted.shape
    lat = values // 4
    tall, broad = 2 * patch_rows, 2 * patches
    channels = kernel.shape[1]
    lanes = -(-tall * 3 * lat // 128) * 128
    return pl.pallas_call(
        functools.partial(inner_body, lat),
        in_specs=[SCALARS] + [WHOLE] * 5,
        out_specs=[ANYWHERE, WHOLE, WHOLE],
        out_shape=[
            jax.ShapeDtypeStruct((frames, tall, broad, channels), BF16),
            jax.ShapeDtypeStruct((frames * broad, channels), F32),
            jax.ShapeDtypeStruct((frames, broad, channels), BF16),
        ],
        scratch_shapes=[
            pltpu.VMEM((frames, lanes // 128, broad + 16, 128), F32),
            pltpu.VMEM((frames, border_lanes(lat), broad + 16, 128), F32),
            pltpu.VMEM((tall - 2, frames, broad, channels), BF16),
            pltpu.SemaphoreType.DMA((tall - 2,)),
        ],
        compiler_params=params(16),
        cost_estimate=pl.CostEstimate(
            flops=2 * frames * tall * broad * 27 * lat * channels,
            bytes_accessed=2 * frames * tall * broad * channels,
            transcendentals=0,
        ),
        name="convolve_inner",
    )(tile, predicted, from_pair, inner_picks, outer_picks, kernel)


def outer_body(lat, tile_ref, from_next, picks, kernel, edge_sum, pair_row, given, features, wide, done, sems):
    frames, tall, broad, _ = features.shape
    edge = jnp.where(tile_ref[0] % 2 == 0, 0, 1)
    panel = border_panel(lat, kernel, edge)
    copies = [pltpu.make_async_copy(pair_row, features.at[:, (1 - edge) * (tall - 1)], sems.at[frames])]
    copies[0].start()
    for frame, taps in enumerate(border_taps(lat, from_next, picks, wide)):
        total = edge_sum[frame * broad : (frame + 1) * broad] + jnp.dot(
            taps, panel, preferred_element_type=F32
        )
        done[frame] = total.astype(BF16)
        copy = pltpu.make_async_copy(done.at[frame], features.at[frame, edge * (tall - 1)], sems.at[frame])
        copy.start()
        copies.append(copy)
    for copy in copies:
        copy.wait()


def convolve_outer(tile, from_next, picks, kernel, edge_sum, pair_row, features):
    frames, tall, broad, channels = features.shape
    lat = picks.shape[1] // 2
    return pl.pallas_call(
        functools.partial(outer_body, lat),
        in_specs=[SCALARS] + [WHOLE] * 5 + [ANYWHERE],
        out_specs=ANYWHERE,
        out_shape=jax.ShapeDtypeStruct(features.shape, BF16),
        input_output_aliases={6: 0},
        scratch_shapes=[
            pltpu.VMEM((frames, border_lanes(lat), broad + 16, 128), F32),
            pltpu.VMEM((frames, broad, channels), BF16),
            pltpu.SemaphoreType.DMA((frames + 1,)),
        ],
        compiler_params=params(16),
        name="convolve_outer",
    )(tile, from_next, picks, kernel, edge_sum, pair_row, features)


def exchange(value, offset):
    count = lax.axis_size("seq")
    return lax.ppermute(value, "seq", [(i, i ^ offset) for i in range(count)])


def local(queries, own_kv, past_kv, block_home, block_list, list_len, final_weight, decoder_weight):
    frames, patch_rows, patches, width = queries.shape
    tokens = frames * patch_rows * patches
    count = lax.axis_size("seq")
    assert count & (count - 1) == 0
    bits = count.bit_length() - 1
    blocks_here = past_kv.shape[0]
    columns = final_weight.shape[1]
    tile = lax.axis_index("seq").astype(jnp.int32).reshape(1)
    query_rows = queries.reshape(tokens, width)
    own_rows = own_kv.reshape(tokens, own_kv.shape[3])
    shape = (frames, patch_rows, patches)
    inner_picks, outer_picks = spreads(columns // 4, patch_rows)
    half = KV_HEADS // 2
    lists = (tile, block_home, block_list, list_len)
    if count == 16 and columns % PART == 0 and decoder_weight.shape[1] % PART == 0:
        far = [4, 8, 12]
        turns = [(2, 0), (3, 1), (1, 2), (0, 3)]
        line = [exchange(past_kv, k) for k in reversed(far)][::-1]
        final, decode, own_rows, inner_picks, outer_picks = lax.optimization_barrier(
            (final_weight.T, decoder_weight.T, own_rows, inner_picks, outer_picks)
        )
        final_across, decode_across = exchange(final, 2), exchange(decode, 2)
        packed, sums, _ = attend_own(range(half), *lists, query_rows, own_rows, turns, blocks_here)
        *line, final_across, decode_across, packed = lax.optimization_barrier(
            (*line, final_across, decode_across, packed)
        )
        near = join([past_kv] + line, "join_near")
        across = exchange(near, 2)
        panels = pack(final, decode, final_across, decode_across)
        panels_far, panels_near = exchange(panels, 8), exchange(panels, 4)
        own_rows, near = lax.optimization_barrier((own_rows, near))
        others = attend_own(range(half, KV_HEADS), *lists, query_rows, own_rows, turns, blocks_here)
        packed, sums, slots = [packed, others[0]], [sums, others[1]], others[2]
        across, panels_far, panels_near, slots = lax.optimization_barrier((across, panels_far, panels_near, slots))
        gathered = join([near, across], "join_chip")
        gathered = [gathered, exchange(gathered, 1)]
        panels_last = exchange(panels_far, 4)
        panels = join([panels, panels_far, panels_near], "join_panels")
        panels_beside = exchange(panels, 1)
        attended = attend_past(slots, packed, sums, gathered, blocks_here)
        panels_last, panels_beside, attended = lax.optimization_barrier((panels_last, panels_beside, attended))
        panels = [panels, panels_last, panels_beside, exchange(panels_last, 1)]
        order = [k ^ x for k in (0, 8, 4, 12) for x in (0, 2)]
        order = order + [k ^ 1 for k in order]
        depth = final_weight.shape[0]
        part = project(tile, attended, panels[0], panels[2], order[:6], depth, columns)
        predicted, to_pair, to_next = finish(
            tile, attended, panels[1], panels[3], part, order[6:8], depth, shape
        )
        decode = unpack(tile, panels, order, final_weight.size // PART, *decoder_weight.shape)
    else:
        turns = [(bit, bits - 1 - bit) for bit in range(bits)]
        held = past_kv
        for bit in reversed(range(bits)):
            held = jnp.concatenate([held, exchange(held, 1 << bit)], axis=0)
        packed, sums, slots = attend_own(
            range(KV_HEADS), *lists, query_rows, own_rows, turns, blocks_here
        )
        attended = attend_past(slots, [packed], [sums], [held], blocks_here)
        final = lax.all_gather(final_weight, "seq", axis=0, tiled=True)
        decode = lax.all_gather(decoder_weight, "seq", axis=1, tiled=True)
        predicted = jnp.dot(attended, final, preferred_element_type=F32).astype(BF16)
        rows = predicted.reshape(shape + (columns,))
        values = columns // 2
        folds = 128 // values

        def folded(cells):
            parts = cells.reshape(frames, folds, patches // folds, values)
            return parts.transpose(0, 2, 1, 3).reshape(frames, patches // folds, 128)

        first, last = folded(rows[:, 0, :, :values]), folded(rows[:, -1, :, values:])
        even = tile[0] % 2 == 0
        to_pair, to_next = jnp.where(even, last, first), jnp.where(even, first, last)
    predicted = predicted.reshape(shape + (columns,))
    swaps = [(i, i + 1) for i in range(1, count - 1, 2)] + [(i + 1, i) for i in range(1, count - 1, 2)]
    from_next = lax.ppermute(to_next, "seq", swaps)
    from_pair = exchange(to_pair, 1)
    features, edge_sum, pair_row = convolve_inner(tile, predicted, from_pair, inner_picks, outer_picks, decode)
    return convolve_outer(tile, from_next, outer_picks, decode, edge_sum, pair_row, features)


def solution(mesh):
    return jax.shard_map(
        local,
        mesh=mesh,
        in_specs=(
            P("groups", "seq", None, None),
            P("groups", "seq", None, None),
            P(("groups", "seq"), None, None),
            P("groups"),
            P("groups", None),
            P("groups"),
            P("seq", None),
            P(None, "seq"),
        ),
        out_specs=P("groups", "seq", None, None),
        check_vma=False,
    )
```

```python
import functools
import math

import jax
import jax.numpy as jnp
from jax import lax
from jax.experimental import pallas as pl
from jax.experimental.pallas import tpu as pltpu
from jax.sharding import PartitionSpec as P

HEADS = 24
KV_HEADS = 4
HEAD_DIM = 128
GROUP = HEADS // KV_HEADS
SCALE = math.log2(math.e) / math.sqrt(HEAD_DIM)
SAFE = 2.0**100
MIB = 1024 * 1024
PART = 16
WHOLE = pl.BlockSpec(memory_space=pltpu.VMEM)
ANYWHERE = pl.BlockSpec(memory_space=pl.ANY)
SCALARS = pl.BlockSpec(memory_space=pltpu.SMEM)
BF16 = jnp.bfloat16
F32 = jnp.float32


def head_columns(index):
    return slice(index * HEAD_DIM, (index + 1) * HEAD_DIM)


def params(mib):
    return pltpu.CompilerParams(vmem_limit_bytes=mib * MIB)


def place_of(offset, turns):
    return sum(((offset >> bit) & 1) << to for bit, to in turns)


def own_body(turns, blocks_here, groups, tile_ref, home, blocks, lens, queries, own, packed, sums, slots):
    tokens = queries.shape[0]
    tile = tile_ref[0]
    for place in range(slots.shape[0]):
        slots[place] = -1

    def find(entry, carry):
        stored = home[blocks[tile, entry]]
        slots[place_of((stored // blocks_here) ^ tile, turns)] = stored % blocks_here
        return carry

    if groups[-1] == KV_HEADS - 1:
        lax.fori_loop(0, lens[tile], find, 0)
    for index, g in enumerate(groups):
        query = jnp.concatenate([queries[:, head_columns(g * GROUP + h)] for h in range(GROUP)], axis=0)
        value = jnp.concatenate(
            [own[:, head_columns(KV_HEADS + g)], jnp.ones((tokens, HEAD_DIM), BF16)], axis=1
        )
        score = lax.dot_general(
            query, own[:, head_columns(g)], (((1,), (1,)), ((), ())), preferred_element_type=F32
        )
        top = jnp.max(score, axis=1, keepdims=True)
        weights = jnp.exp2((score - top) * SCALE).astype(BF16)
        mixed = jnp.dot(weights, value, preferred_element_type=F32)
        total = mixed[:, HEAD_DIM:]
        sums[index] = mixed[:, :HEAD_DIM] / total
        level = top + jnp.log2(total) * (1.0 / SCALE)
        high = level.astype(BF16).astype(F32)
        middle = (level - high).astype(BF16).astype(F32)
        low = level - high - middle
        lane = lax.broadcasted_iota(jnp.int32, level.shape, 1)
        extra = jnp.where(lane == 0, high, jnp.where(lane == 1, middle, jnp.where(lane == 2, low, 0.0)))
        packed[index, :, :HEAD_DIM] = query
        packed[index, :, HEAD_DIM:] = extra.astype(BF16)


def attend_own(groups, tile, block_home, block_list, list_len, query_rows, own_rows, turns, blocks_here):
    tokens, width = query_rows.shape
    rows = GROUP * tokens
    return pl.pallas_call(
        functools.partial(own_body, turns, blocks_here, groups),
        in_specs=[SCALARS] * 4 + [WHOLE] * 2,
        out_specs=[WHOLE, WHOLE, SCALARS],
        out_shape=[
            jax.ShapeDtypeStruct((len(groups), rows, 2 * HEAD_DIM), BF16),
            jax.ShapeDtypeStruct((len(groups), rows, HEAD_DIM), F32),
            jax.ShapeDtypeStruct((1 << len(turns),), jnp.int32),
        ],
        compiler_params=params(20),
        cost_estimate=pl.CostEstimate(
            flops=3 * len(groups) * tokens * tokens * width, bytes_accessed=0, transcendentals=0
        ),
        name="attend_own",
    )(tile, block_home, block_list, list_len, query_rows, own_rows)


def past_body(sizes, split, slots, *refs):
    packed, sums, refs = refs[:split], refs[split : 2 * split], refs[2 * split :]
    gathered, (out, keys, values, worst) = refs[: len(sizes)], refs[len(sizes) :]
    groups = KV_HEADS // split
    blocks_here = sum(ref.shape[0] for ref in gathered) // sum(sizes)
    block_tokens = gathered[0].shape[1]
    tokens = out.shape[0]
    lane = lax.broadcasted_iota(jnp.int32, (block_tokens, HEAD_DIM), 1)
    minus = jnp.where(lane < 3, -1.0, 0.0)
    zero = jnp.zeros((block_tokens, HEAD_DIM), BF16)
    homes = [(ref, k) for ref, size in zip(gathered, sizes) for k in range(size)]
    found = []
    for place, (ref, k) in enumerate(homes):
        slot = slots[place]
        found.append((ref, k * blocks_here + jnp.maximum(slot, 0), slot >= 0))

    def fill(g):
        for place, (ref, index, listed) in enumerate(found):
            live = jnp.where(listed, 1.0, 0.0)
            rows = slice(place * block_tokens, (place + 1) * block_tokens)
            keys[g, rows, :HEAD_DIM] = jnp.where(listed, ref[index, :, head_columns(g)], zero)
            keys[g, rows, HEAD_DIM:] = (minus * live).astype(BF16)
            values[g, rows, :HEAD_DIM] = jnp.where(listed, ref[index, :, head_columns(KV_HEADS + g)], zero)
            values[g, rows, HEAD_DIM:] = jnp.full((block_tokens, HEAD_DIM), live, F32).astype(BF16)

    heads = GROUP if keys.shape[1] <= 512 else 1
    steps = KV_HEADS * GROUP // heads

    def over_steps(one, start):
        if heads == GROUP:
            for step in range(steps):
                start = one(step, start)
            return start
        return lax.fori_loop(0, steps, one, start)

    def place(step):
        if heads == GROUP:
            return step, slice(None)
        return step // GROUP, pl.ds(pl.multiple_of((step % GROUP) * tokens, tokens), tokens)

    def own_part(arrays, g, rows):
        if split == 1:
            return arrays[0][g, rows]
        return arrays[g // groups][g % groups, rows]

    def scores(g, rows):
        return SCALE * lax.dot_general(
            own_part(packed, g, rows), keys[g], (((1,), (1,)), ((), ())), preferred_element_type=F32
        )

    def emit(step, attended):
        attended = attended.astype(BF16)
        for h in range(heads):
            columns = (step * heads + h) * HEAD_DIM
            if heads == 1:
                columns = pl.multiple_of(columns, HEAD_DIM)
            out[:, pl.ds(columns, HEAD_DIM)] = attended[h * tokens : (h + 1) * tokens]

    def quick(step, score, largest):
        g, rows = place(step)
        weights = jnp.exp2(score).astype(BF16)
        mixed = jnp.dot(weights, values[g], preferred_element_type=F32)
        below = mixed[:, HEAD_DIM:] + 1.0
        emit(step, (mixed[:, :HEAD_DIM] + own_part(sums, g, rows)) / below)
        return jnp.maximum(largest, jnp.max(below.reshape((-1,) + largest.shape), axis=0))

    largest = jnp.zeros(worst.shape, F32)
    if heads == GROUP:
        fill(0)
        score = scores(*place(0))
        for step in range(steps):
            ahead = None
            if step + 1 < steps:
                fill(step + 1)
                ahead = scores(*place(step + 1))
            largest = quick(step, score, largest)
            score = ahead
    else:
        for g in range(KV_HEADS):
            fill(g)
        largest = over_steps(lambda step, seen: quick(step, scores(*place(step)), seen), largest)
    worst[...] = largest

    @pl.when(jnp.logical_not(jnp.max(worst[...]) < SAFE))
    def _():
        def careful(step, carry):
            g, rows = place(step)
            score = scores(g, rows)
            top = jnp.maximum(jnp.max(score, axis=1, keepdims=True), 0.0)
            weights = jnp.exp2(score - top).astype(BF16)
            mixed = jnp.dot(weights, values[g], preferred_element_type=F32)
            share = jnp.exp2(-top)
            joined = mixed[:, :HEAD_DIM] + share * own_part(sums, g, rows)
            emit(step, joined / (mixed[:, HEAD_DIM:] + share))
            return carry

        over_steps(careful, 0)


def attend_past(slots, packed, sums, gathered, blocks_here):
    heads = KV_HEADS
    rows = packed[0].shape[1]
    tokens = rows // GROUP
    sizes = [array.shape[0] // blocks_here for array in gathered]
    keys = sum(sizes) * gathered[0].shape[1]
    return pl.pallas_call(
        functools.partial(past_body, sizes, len(packed)),
        in_specs=[SCALARS] + [WHOLE] * (2 * len(packed) + len(gathered)),
        out_specs=WHOLE,
        out_shape=jax.ShapeDtypeStruct((tokens, HEADS * HEAD_DIM), BF16),
        scratch_shapes=[
            pltpu.VMEM((heads, keys, 2 * HEAD_DIM), BF16),
            pltpu.VMEM((heads, keys, 2 * HEAD_DIM), BF16),
            pltpu.VMEM((8, HEAD_DIM), F32),
        ],
        compiler_params=params(40 if keys > 256 else 24),
        cost_estimate=pl.CostEstimate(
            flops=10**10, bytes_accessed=0, transcendentals=0
        ),
        name="attend_past",
    )(slots, *packed, *sums, *gathered)


def join_body(*refs):
    *parts, out = refs
    row = 0
    for part in parts:
        out[row : row + part.shape[0]] = part[...]
        row += part.shape[0]


def join(parts, name):
    rows = sum(part.shape[0] for part in parts)
    return pl.pallas_call(
        join_body,
        in_specs=[WHOLE] * len(parts),
        out_specs=WHOLE,
        out_shape=jax.ShapeDtypeStruct((rows,) + parts[0].shape[1:], BF16),
        compiler_params=params(4),
        name=name,
    )(*parts)


def parts_of(panel):
    return [panel[row : row + PART] for row in range(0, panel.shape[0], PART)]


def pack_body(final, decode, final_across, decode_across, out):
    for k, (left, right) in enumerate(((final, decode), (final_across, decode_across))):
        parts = parts_of(left) + parts_of(right)
        blank = out.shape[2] - sum(part.shape[1] for part in parts)
        out[k] = jnp.concatenate(parts + [jnp.zeros((PART, blank), BF16)], axis=1)


def pack(final, decode, final_across, decode_across):
    lanes = (final.size + decode.size) // PART
    return pl.pallas_call(
        pack_body,
        in_specs=[WHOLE] * 4,
        out_specs=WHOLE,
        out_shape=jax.ShapeDtypeStruct((2, PART, -(-lanes // 128) * 128), BF16),
        compiler_params=params(4),
        name="pack",
    )(final, decode, final_across, decode_across)


def project_pairs(offsets, depth, columns, tile, attended, ours, theirs):
    even = tile % 2 == 0
    total = jnp.zeros((attended.shape[0], columns), F32)
    ours = [(ref, k) for ref in ours for k in range(ref.shape[0])]
    theirs = [(ref, k) for ref in theirs for k in range(ref.shape[0])]
    for offset, (our, i), (their, j) in zip(offsets, ours, theirs):
        left, right = our[i], their[j]
        left, right = jnp.where(even, left, right), jnp.where(even, right, left)
        rows = [
            jnp.concatenate([panel[:, part * depth : (part + 1) * depth] for panel in (left, right)], axis=1)
            for part in range(columns // PART)
        ]
        start = pl.multiple_of(((tile ^ offset) // 2) * (2 * depth), 128)
        total += lax.dot_general(
            attended[:, pl.ds(start, 2 * depth)],
            jnp.concatenate(rows, axis=0),
            (((1,), (1,)), ((), ())),
            preferred_element_type=F32,
        )
    return total


def project_body(offsets, depth, tile_ref, attended, ours, theirs, out):
    out[...] = project_pairs(offsets, depth, out.shape[1], tile_ref[0], attended, [ours], [theirs])


def project(tile, attended, ours, theirs, offsets, depth, columns):
    return pl.pallas_call(
        functools.partial(project_body, offsets, depth),
        in_specs=[SCALARS] + [WHOLE] * 3,
        out_specs=WHOLE,
        out_shape=jax.ShapeDtypeStruct((attended.shape[0], columns), F32),
        compiler_params=params(16),
        name="project",
    )(tile, attended, ours, theirs)


def finish_body(offsets, depth, shape, tile_ref, attended, ours, theirs, part, out, to_pair, to_next):
    frames, patch_rows, patches = shape
    tile = tile_ref[0]
    predicted = part[...] + project_pairs(offsets, depth, part.shape[1], tile, attended, [ours], [theirs])
    predicted = predicted.astype(BF16)
    out[...] = predicted
    even = tile % 2 == 0
    values = predicted.shape[1] // 2
    folds = 128 // values
    count = patches // folds

    def folded(rows):
        return jnp.concatenate([rows[k * count : (k + 1) * count] for k in range(folds)], axis=1)

    for frame in range(frames):
        rows = predicted[frame * patch_rows * patches : (frame + 1) * patch_rows * patches]
        first, last = folded(rows[:patches, :values]), folded(rows[(patch_rows - 1) * patches :, values:])
        to_pair[frame] = jnp.where(even, last, first)
        to_next[frame] = jnp.where(even, first, last)


def finish(tile, attended, ours, theirs, part, offsets, depth, shape):
    tokens, columns = part.shape
    border = jax.ShapeDtypeStruct((shape[0], shape[2] * (columns // 2) // 128, 128), BF16)
    return pl.pallas_call(
        functools.partial(finish_body, offsets, depth, shape),
        in_specs=[SCALARS] + [WHOLE] * 4,
        out_specs=[WHOLE] * 3,
        out_shape=[jax.ShapeDtypeStruct((tokens, columns), BF16), border, border],
        compiler_params=params(16),
        name="finish",
    )(tile, attended, ours, theirs, part)


def unpack_body(order, skip, tile_ref, *refs):
    *panels, out, staged = refs
    taps = out.shape[0]
    place = 0
    for panel in panels:
        for k in range(panel.shape[0]):
            staged[tile_ref[0] ^ order[place]] = panel[k]
            place += 1
    width = out.shape[1] // len(order)
    whole = [
        staged[device, :, skip + part * taps : skip + (part + 1) * taps]
        for device in range(len(order))
        for part in range(width // PART)
    ]
    out[...] = jnp.concatenate(whole, axis=0).T


def unpack(tile, panels, order, skip, taps, width):
    return pl.pallas_call(
        functools.partial(unpack_body, order, skip),
        in_specs=[SCALARS] + [WHOLE] * len(panels),
        out_specs=WHOLE,
        out_shape=jax.ShapeDtypeStruct((taps, width * len(order)), BF16),
        scratch_shapes=[pltpu.VMEM((len(order),) + panels[0].shape[1:], BF16)],
        compiler_params=params(16),
        name="unpack",
    )(tile, *panels)


def tap_rows(frames, cells, width):
    stacks = []
    for shift_t in range(3):
        rows = []
        for frame in range(frames):
            source = frame + shift_t - 2
            rows.append(cells[source] if source >= 0 else jnp.zeros((width, cells[0].shape[1]), BF16))
        stacks.append(jnp.concatenate(rows, axis=0))
    return stacks


def shifted(wide, frame, width, lat):
    chunks = []
    for chunk in range(wide.shape[1]):
        lane = lax.broadcasted_iota(jnp.int32, (width, 128), 1) + 128 * chunk
        shift = (lane // lat) % 3
        near = jnp.where(shift == 1, wide[frame, chunk, 8 : 8 + width], wide[frame, chunk, 9 : 9 + width])
        chunks.append(jnp.where(shift == 0, wide[frame, chunk, 7 : 7 + width], near).astype(BF16))
    return jnp.concatenate(chunks, axis=1)


def spread_body(lat, patch_rows, inner, outer):
    span = 3 * lat
    for side in range(2):
        source = lax.broadcasted_iota(jnp.int32, inner.shape[2:], 0)
        target = lax.broadcasted_iota(jnp.int32, inner.shape[2:], 1)
        for r in range(patch_rows):
            upper = target // span - 2 * r
            wanted = (upper >= 0) & (upper < 2) & (source == upper * 2 * lat + side * lat + target % lat)
            inner[side, r] = jnp.where(wanted, 1.0, 0.0).astype(BF16)
        source = lax.broadcasted_iota(jnp.int32, outer.shape[1:], 0)
        target = lax.broadcasted_iota(jnp.int32, outer.shape[1:], 1)
        wanted = (source == side * lat + target % lat) & (target < 3 * span)
        outer[side] = jnp.where(wanted, 1.0, 0.0).astype(BF16)


def spreads(lat, patch_rows):
    tall = 2 * patch_rows
    return pl.pallas_call(
        functools.partial(spread_body, lat, patch_rows),
        out_specs=[WHOLE, WHOLE],
        out_shape=[
            jax.ShapeDtypeStruct((2, patch_rows, 4 * lat, -(-tall * 3 * lat // 128) * 128), BF16),
            jax.ShapeDtypeStruct((2, 2 * lat, -(-9 * lat // 128) * 128), BF16),
        ],
        compiler_params=params(4),
        cost_estimate=pl.CostEstimate(flops=5 * 10**9, bytes_accessed=0, transcendentals=0),
        name="spreads",
    )()


def border_taps(lat, cells, picks, wide):
    frames, values = cells.shape[0], picks.shape[1]
    folds = 128 // values
    patches = cells.shape[1] * folds
    broad = 2 * patches
    chunks = wide.shape[1]
    span = 3 * lat
    wide[:, :, 0:8] = jnp.zeros((frames, chunks, 8, 128), F32)
    wide[:, :, 8 + broad :] = jnp.zeros((frames, chunks, 8, 128), F32)
    for frame in range(frames):
        folded = cells[frame]
        row = jnp.concatenate([folded[:, k * values : (k + 1) * values] for k in range(folds)], axis=0)
        for side in range(2):
            spread = jnp.dot(row, picks[side], preferred_element_type=F32)
            for chunk in range(chunks):
                wide[frame, chunk, pl.ds(8 + side, patches, stride=2), :] = spread[
                    :, 128 * chunk : 128 * (chunk + 1)
                ]
    ready = [shifted(wide, frame, broad, lat) for frame in range(frames)]
    lane = lax.broadcasted_iota(jnp.int32, ready[0].shape, 1)
    rows = []
    for frame in range(frames):
        taps = jnp.zeros(ready[0].shape, BF16)
        for shift_t in range(3):
            if frame + shift_t - 2 >= 0:
                taps = jnp.where(lane // span == shift_t, ready[frame + shift_t - 2], taps)
        rows.append(taps[:, : 3 * span])
    return rows


def border_panel(lat, kernel, edge):
    span = 3 * lat
    starts = [pl.multiple_of((3 * shift_t + 2 * edge) * span, lat) for shift_t in range(3)]
    return jnp.concatenate([kernel[pl.ds(start, span)] for start in starts], axis=0)


def inner_body(
    lat, tile_ref, predicted, from_pair, inner_picks, outer_picks, kernel, features, edge_sum, pair_row,
    wide, border, done, sems
):
    frames, patch_rows, patches, _ = predicted.shape
    tall, broad = 2 * patch_rows, 2 * patches
    span = 3 * lat
    chunks = wide.shape[1]
    even = tile_ref[0] % 2 == 0
    pair_edge = jnp.where(even, 1, 0)
    wide[:, :, 0:8] = jnp.zeros((frames, chunks, 8, 128), F32)
    wide[:, :, 8 + broad :] = jnp.zeros((frames, chunks, 8, 128), F32)
    for side in range(2):
        for frame in range(frames):
            cells = jnp.zeros((patches, 128 * chunks), F32)
            for r in range(patch_rows):
                cells += jnp.dot(predicted[frame, r], inner_picks[side, r], preferred_element_type=F32)
            for chunk in range(chunks):
                wide[frame, chunk, pl.ds(8 + side, patches, stride=2), :] = cells[:, 128 * chunk : 128 * (chunk + 1)]
    stacks = tap_rows(frames, [shifted(wide, f, broad, lat) for f in range(frames)], broad)

    def own_sum(row):
        first, last = max(row - 1, 0), min(row + 1, tall - 1)
        total = jnp.zeros((frames * broad, kernel.shape[1]), F32)
        for shift_t in range(3):
            start = (3 * shift_t + first - (row - 1)) * span
            total += jnp.dot(
                stacks[shift_t][:, first * span : (last + 1) * span],
                kernel[start : start + (last + 1 - first) * span],
                preferred_element_type=F32,
            )
        return total

    copies = []

    def send(index, row, total):
        done[index] = total.astype(BF16).reshape(done.shape[1:])
        copy = pltpu.make_async_copy(done.at[index], features.at[:, row], sems.at[index])
        copy.start()
        copies.append(copy)

    for row in range(1, tall - 1):
        send(row - 1, row, own_sum(row))
    first, last = own_sum(0), own_sum(tall - 1)
    edge_sum[...] = jnp.where(even, first, last)
    taps = jnp.concatenate(border_taps(lat, from_pair, outer_picks, border), axis=0)
    total = jnp.where(even, last, first) + jnp.dot(
        taps, border_panel(lat, kernel, pair_edge), preferred_element_type=F32
    )
    pair_row[...] = total.astype(BF16).reshape(pair_row.shape)
    for copy in copies:
        copy.wait()


def border_lanes(lat):
    return -(-9 * lat // 128)


def convolve_inner(tile, predicted, from_pair, inner_picks, outer_picks, kernel):
    frames, patch_rows, patches, values = predicted.shape
    lat = values // 4
    tall, broad = 2 * patch_rows, 2 * patches
    channels = kernel.shape[1]
    lanes = -(-tall * 3 * lat // 128) * 128
    return pl.pallas_call(
        functools.partial(inner_body, lat),
        in_specs=[SCALARS] + [WHOLE] * 5,
        out_specs=[ANYWHERE, WHOLE, WHOLE],
        out_shape=[
            jax.ShapeDtypeStruct((frames, tall, broad, channels), BF16),
            jax.ShapeDtypeStruct((frames * broad, channels), F32),
            jax.ShapeDtypeStruct((frames, broad, channels), BF16),
        ],
        scratch_shapes=[
            pltpu.VMEM((frames, lanes // 128, broad + 16, 128), F32),
            pltpu.VMEM((frames, border_lanes(lat), broad + 16, 128), F32),
            pltpu.VMEM((tall - 2, frames, broad, channels), BF16),
            pltpu.SemaphoreType.DMA((tall - 2,)),
        ],
        compiler_params=params(16),
        cost_estimate=pl.CostEstimate(
            flops=2 * frames * tall * broad * 27 * lat * channels,
            bytes_accessed=2 * frames * tall * broad * channels,
            transcendentals=0,
        ),
        name="convolve_inner",
    )(tile, predicted, from_pair, inner_picks, outer_picks, kernel)


def outer_body(lat, tile_ref, from_next, picks, kernel, edge_sum, pair_row, given, features, wide, done, sems):
    frames, tall, broad, _ = features.shape
    edge = jnp.where(tile_ref[0] % 2 == 0, 0, 1)
    panel = border_panel(lat, kernel, edge)
    copies = [pltpu.make_async_copy(pair_row, features.at[:, (1 - edge) * (tall - 1)], sems.at[frames])]
    copies[0].start()
    for frame, taps in enumerate(border_taps(lat, from_next, picks, wide)):
        total = edge_sum[frame * broad : (frame + 1) * broad] + jnp.dot(
            taps, panel, preferred_element_type=F32
        )
        done[frame] = total.astype(BF16)
        copy = pltpu.make_async_copy(done.at[frame], features.at[frame, edge * (tall - 1)], sems.at[frame])
        copy.start()
        copies.append(copy)
    for copy in copies:
        copy.wait()


def convolve_outer(tile, from_next, picks, kernel, edge_sum, pair_row, features):
    frames, tall, broad, channels = features.shape
    lat = picks.shape[1] // 2
    return pl.pallas_call(
        functools.partial(outer_body, lat),
        in_specs=[SCALARS] + [WHOLE] * 5 + [ANYWHERE],
        out_specs=ANYWHERE,
        out_shape=jax.ShapeDtypeStruct(features.shape, BF16),
        input_output_aliases={6: 0},
        scratch_shapes=[
            pltpu.VMEM((frames, border_lanes(lat), broad + 16, 128), F32),
            pltpu.VMEM((frames, broad, channels), BF16),
            pltpu.SemaphoreType.DMA((frames + 1,)),
        ],
        compiler_params=params(16),
        name="convolve_outer",
    )(tile, from_next, picks, kernel, edge_sum, pair_row, features)


def exchange(value, offset):
    count = lax.axis_size("seq")
    return lax.ppermute(value, "seq", [(i, i ^ offset) for i in range(count)])


def local(queries, own_kv, past_kv, block_home, block_list, list_len, final_weight, decoder_weight):
    frames, patch_rows, patches, width = queries.shape
    tokens = frames * patch_rows * patches
    count = lax.axis_size("seq")
    assert count & (count - 1) == 0
    bits = count.bit_length() - 1
    blocks_here = past_kv.shape[0]
    columns = final_weight.shape[1]
    tile = lax.axis_index("seq").astype(jnp.int32).reshape(1)
    query_rows = queries.reshape(tokens, width)
    own_rows = own_kv.reshape(tokens, own_kv.shape[3])
    shape = (frames, patch_rows, patches)
    inner_picks, outer_picks = spreads(columns // 4, patch_rows)
    half = KV_HEADS // 2
    lists = (tile, block_home, block_list, list_len)
    if count == 16 and columns % PART == 0 and decoder_weight.shape[1] % PART == 0:
        far = [4, 8, 12]
        turns = [(2, 0), (3, 1), (1, 2), (0, 3)]
        line = [exchange(past_kv, k) for k in reversed(far)][::-1]
        final, decode, own_rows, inner_picks, outer_picks = lax.optimization_barrier(
            (final_weight.T, decoder_weight.T, own_rows, inner_picks, outer_picks)
        )
        final_across, decode_across = exchange(final, 2), exchange(decode, 2)
        packed, sums, _ = attend_own(range(half), *lists, query_rows, own_rows, turns, blocks_here)
        *line, final_across, decode_across, packed = lax.optimization_barrier(
            (*line, final_across, decode_across, packed)
        )
        near = join([past_kv] + line, "join_near")
        across = exchange(near, 2)
        panels = pack(final, decode, final_across, decode_across)
        panels_far, panels_near = exchange(panels, 8), exchange(panels, 4)
        own_rows, near = lax.optimization_barrier((own_rows, near))
        others = attend_own(range(half, KV_HEADS), *lists, query_rows, own_rows, turns, blocks_here)
        packed, sums, slots = [packed, others[0]], [sums, others[1]], others[2]
        across, panels_far, panels_near, slots = lax.optimization_barrier((across, panels_far, panels_near, slots))
        gathered = join([near, across], "join_chip")
        gathered = [gathered, exchange(gathered, 1)]
        panels_last = exchange(panels_far, 4)
        panels = join([panels, panels_far, panels_near], "join_panels")
        panels_beside = exchange(panels, 1)
        attended = attend_past(slots, packed, sums, gathered, blocks_here)
        panels_last, panels_beside, attended = lax.optimization_barrier((panels_last, panels_beside, attended))
        panels = [panels, panels_last, panels_beside, exchange(panels_last, 1)]
        order = [k ^ x for k in (0, 8, 4, 12) for x in (0, 2)]
        order = order + [k ^ 1 for k in order]
        depth = final_weight.shape[0]
        part = project(tile, attended, panels[0], panels[2], order[:6], depth, columns)
        predicted, to_pair, to_next = finish(
            tile, attended, panels[1], panels[3], part, order[6:8], depth, shape
        )
        decode = unpack(tile, panels, order, final_weight.size // PART, *decoder_weight.shape)
    else:
        turns = [(bit, bits - 1 - bit) for bit in range(bits)]
        held = past_kv
        for bit in reversed(range(bits)):
            held = jnp.concatenate([held, exchange(held, 1 << bit)], axis=0)
        packed, sums, slots = attend_own(
            range(KV_HEADS), *lists, query_rows, own_rows, turns, blocks_here
        )
        attended = attend_past(slots, [packed], [sums], [held], blocks_here)
        final = lax.all_gather(final_weight, "seq", axis=0, tiled=True)
        decode = lax.all_gather(decoder_weight, "seq", axis=1, tiled=True)
        predicted = jnp.dot(attended, final, preferred_element_type=F32).astype(BF16)
        rows = predicted.reshape(shape + (columns,))
        values = columns // 2
        folds = 128 // values

        def folded(cells):
            parts = cells.reshape(frames, folds, patches // folds, values)
            return parts.transpose(0, 2, 1, 3).reshape(frames, patches // folds, 128)

        first, last = folded(rows[:, 0, :, :values]), folded(rows[:, -1, :, values:])
        even = tile[0] % 2 == 0
        to_pair, to_next = jnp.where(even, last, first), jnp.where(even, first, last)
    predicted = predicted.reshape(shape + (columns,))
    swaps = [(i, i + 1) for i in range(1, count - 1, 2)] + [(i + 1, i) for i in range(1, count - 1, 2)]
    from_next = lax.ppermute(to_next, "seq", swaps)
    from_pair = exchange(to_pair, 1)
    features, edge_sum, pair_row = convolve_inner(tile, predicted, from_pair, inner_picks, outer_picks, decode)
    return convolve_outer(tile, from_next, outer_picks, decode, edge_sum, pair_row, features)


def solution(mesh):
    return jax.shard_map(
        local,
        mesh=mesh,
        in_specs=(
            P("groups", "seq", None, None),
            P("groups", "seq", None, None),
            P(("groups", "seq"), None, None),
            P("groups"),
            P("groups", None),
            P("groups"),
            P("seq", None),
            P(None, "seq"),
        ),
        out_specs=P("groups", "seq", None, None),
        check_vma=False,
    )
```

```python
import functools
import math

import jax
import jax.numpy as jnp
from jax import lax
from jax.experimental import pallas as pl
from jax.experimental.pallas import tpu as pltpu
from jax.sharding import PartitionSpec as P

HEADS = 24
KV_HEADS = 4
HEAD_DIM = 128
GROUP = HEADS // KV_HEADS
SCALE = math.log2(math.e) / math.sqrt(HEAD_DIM)
SAFE = 2.0**100
MIB = 1024 * 1024
PART = 16
WHOLE = pl.BlockSpec(memory_space=pltpu.VMEM)
ANYWHERE = pl.BlockSpec(memory_space=pl.ANY)
SCALARS = pl.BlockSpec(memory_space=pltpu.SMEM)
BF16 = jnp.bfloat16
F32 = jnp.float32


def head_columns(index):
    return slice(index * HEAD_DIM, (index + 1) * HEAD_DIM)


def params(mib):
    return pltpu.CompilerParams(vmem_limit_bytes=mib * MIB)


def place_of(offset, turns):
    return sum(((offset >> bit) & 1) << to for bit, to in turns)


def own_body(turns, blocks_here, groups, tile_ref, home, blocks, lens, queries, own, packed, sums, slots):
    tokens = queries.shape[0]
    tile = tile_ref[0]
    for place in range(slots.shape[0]):
        slots[place] = -1

    def find(entry, carry):
        stored = home[blocks[tile, entry]]
        slots[place_of((stored // blocks_here) ^ tile, turns)] = stored % blocks_here
        return carry

    if groups[-1] == KV_HEADS - 1:
        lax.fori_loop(0, lens[tile], find, 0)
    for index, g in enumerate(groups):
        query = jnp.concatenate([queries[:, head_columns(g * GROUP + h)] for h in range(GROUP)], axis=0)
        value = jnp.concatenate(
            [own[:, head_columns(KV_HEADS + g)], jnp.ones((tokens, HEAD_DIM), BF16)], axis=1
        )
        score = lax.dot_general(
            query, own[:, head_columns(g)], (((1,), (1,)), ((), ())), preferred_element_type=F32
        )
        top = jnp.max(score, axis=1, keepdims=True)
        weights = jnp.exp2((score - top) * SCALE).astype(BF16)
        mixed = jnp.dot(weights, value, preferred_element_type=F32)
        total = mixed[:, HEAD_DIM:]
        sums[index] = mixed[:, :HEAD_DIM] / total
        level = top + jnp.log2(total) * (1.0 / SCALE)
        high = level.astype(BF16).astype(F32)
        middle = (level - high).astype(BF16).astype(F32)
        low = level - high - middle
        lane = lax.broadcasted_iota(jnp.int32, level.shape, 1)
        extra = jnp.where(lane == 0, high, jnp.where(lane == 1, middle, jnp.where(lane == 2, low, 0.0)))
        packed[index, :, :HEAD_DIM] = query
        packed[index, :, HEAD_DIM:] = extra.astype(BF16)


def attend_own(groups, tile, block_home, block_list, list_len, query_rows, own_rows, turns, blocks_here):
    tokens, width = query_rows.shape
    rows = GROUP * tokens
    return pl.pallas_call(
        functools.partial(own_body, turns, blocks_here, groups),
        in_specs=[SCALARS] * 4 + [WHOLE] * 2,
        out_specs=[WHOLE, WHOLE, SCALARS],
        out_shape=[
            jax.ShapeDtypeStruct((len(groups), rows, 2 * HEAD_DIM), BF16),
            jax.ShapeDtypeStruct((len(groups), rows, HEAD_DIM), F32),
            jax.ShapeDtypeStruct((1 << len(turns),), jnp.int32),
        ],
        compiler_params=params(20),
        cost_estimate=pl.CostEstimate(
            flops=3 * len(groups) * tokens * tokens * width, bytes_accessed=0, transcendentals=0
        ),
        name="attend_own",
    )(tile, block_home, block_list, list_len, query_rows, own_rows)


def past_body(sizes, split, slots, *refs):
    packed, sums, refs = refs[:split], refs[split : 2 * split], refs[2 * split :]
    gathered, (out, keys, values, worst) = refs[: len(sizes)], refs[len(sizes) :]
    groups = KV_HEADS // split
    blocks_here = sum(ref.shape[0] for ref in gathered) // sum(sizes)
    block_tokens = gathered[0].shape[1]
    tokens = out.shape[0]
    lane = lax.broadcasted_iota(jnp.int32, (block_tokens, HEAD_DIM), 1)
    minus = jnp.where(lane < 3, -1.0, 0.0)
    zero = jnp.zeros((block_tokens, HEAD_DIM), BF16)
    homes = [(ref, k) for ref, size in zip(gathered, sizes) for k in range(size)]
    found = []
    for place, (ref, k) in enumerate(homes):
        slot = slots[place]
        found.append((ref, k * blocks_here + jnp.maximum(slot, 0), slot >= 0))

    def fill(g):
        for place, (ref, index, listed) in enumerate(found):
            live = jnp.where(listed, 1.0, 0.0)
            rows = slice(place * block_tokens, (place + 1) * block_tokens)
            keys[g, rows, :HEAD_DIM] = jnp.where(listed, ref[index, :, head_columns(g)], zero)
            keys[g, rows, HEAD_DIM:] = (minus * live).astype(BF16)
            values[g, rows, :HEAD_DIM] = jnp.where(listed, ref[index, :, head_columns(KV_HEADS + g)], zero)
            values[g, rows, HEAD_DIM:] = jnp.full((block_tokens, HEAD_DIM), live, F32).astype(BF16)

    heads = GROUP if keys.shape[1] <= 512 else 1
    steps = KV_HEADS * GROUP // heads

    def over_steps(one, start):
        if heads == GROUP:
            for step in range(steps):
                start = one(step, start)
            return start
        return lax.fori_loop(0, steps, one, start)

    def place(step):
        if heads == GROUP:
            return step, slice(None)
        return step // GROUP, pl.ds(pl.multiple_of((step % GROUP) * tokens, tokens), tokens)

    def own_part(arrays, g, rows):
        if split == 1:
            return arrays[0][g, rows]
        return arrays[g // groups][g % groups, rows]

    def scores(g, rows):
        return SCALE * lax.dot_general(
            own_part(packed, g, rows), keys[g], (((1,), (1,)), ((), ())), preferred_element_type=F32
        )

    def emit(step, attended):
        attended = attended.astype(BF16)
        for h in range(heads):
            columns = (step * heads + h) * HEAD_DIM
            if heads == 1:
                columns = pl.multiple_of(columns, HEAD_DIM)
            out[:, pl.ds(columns, HEAD_DIM)] = attended[h * tokens : (h + 1) * tokens]

    def quick(step, score, largest):
        g, rows = place(step)
        weights = jnp.exp2(score).astype(BF16)
        mixed = jnp.dot(weights, values[g], preferred_element_type=F32)
        below = mixed[:, HEAD_DIM:] + 1.0
        emit(step, (mixed[:, :HEAD_DIM] + own_part(sums, g, rows)) / below)
        return jnp.maximum(largest, jnp.max(below.reshape((-1,) + largest.shape), axis=0))

    largest = jnp.zeros(worst.shape, F32)
    if heads == GROUP:
        fill(0)
        score = scores(*place(0))
        for step in range(steps):
            ahead = None
            if step + 1 < steps:
                fill(step + 1)
                ahead = scores(*place(step + 1))
            largest = quick(step, score, largest)
            score = ahead
    else:
        for g in range(KV_HEADS):
            fill(g)
        largest = over_steps(lambda step, seen: quick(step, scores(*place(step)), seen), largest)
    worst[...] = largest

    @pl.when(jnp.logical_not(jnp.max(worst[...]) < SAFE))
    def _():
        def careful(step, carry):
            g, rows = place(step)
            score = scores(g, rows)
            top = jnp.maximum(jnp.max(score, axis=1, keepdims=True), 0.0)
            weights = jnp.exp2(score - top).astype(BF16)
            mixed = jnp.dot(weights, values[g], preferred_element_type=F32)
            share = jnp.exp2(-top)
            joined = mixed[:, :HEAD_DIM] + share * own_part(sums, g, rows)
            emit(step, joined / (mixed[:, HEAD_DIM:] + share))
            return carry

        over_steps(careful, 0)


def attend_past(slots, packed, sums, gathered, blocks_here):
    heads = KV_HEADS
    rows = packed[0].shape[1]
    tokens = rows // GROUP
    sizes = [array.shape[0] // blocks_here for array in gathered]
    keys = sum(sizes) * gathered[0].shape[1]
    return pl.pallas_call(
        functools.partial(past_body, sizes, len(packed)),
        in_specs=[SCALARS] + [WHOLE] * (2 * len(packed) + len(gathered)),
        out_specs=WHOLE,
        out_shape=jax.ShapeDtypeStruct((tokens, HEADS * HEAD_DIM), BF16),
        scratch_shapes=[
            pltpu.VMEM((heads, keys, 2 * HEAD_DIM), BF16),
            pltpu.VMEM((heads, keys, 2 * HEAD_DIM), BF16),
            pltpu.VMEM((8, HEAD_DIM), F32),
        ],
        compiler_params=params(40 if keys > 256 else 24),
        cost_estimate=pl.CostEstimate(
            flops=10**10, bytes_accessed=0, transcendentals=0
        ),
        name="attend_past",
    )(slots, *packed, *sums, *gathered)


def join_body(*refs):
    *parts, out = refs
    row = 0
    for part in parts:
        out[row : row + part.shape[0]] = part[...]
        row += part.shape[0]


def join(parts, name):
    rows = sum(part.shape[0] for part in parts)
    return pl.pallas_call(
        join_body,
        in_specs=[WHOLE] * len(parts),
        out_specs=WHOLE,
        out_shape=jax.ShapeDtypeStruct((rows,) + parts[0].shape[1:], BF16),
        compiler_params=params(4),
        name=name,
    )(*parts)


def parts_of(panel):
    return [panel[row : row + PART] for row in range(0, panel.shape[0], PART)]


def pack_body(final, decode, final_across, decode_across, out):
    for k, (left, right) in enumerate(((final, decode), (final_across, decode_across))):
        parts = parts_of(left) + parts_of(right)
        blank = out.shape[2] - sum(part.shape[1] for part in parts)
        out[k] = jnp.concatenate(parts + [jnp.zeros((PART, blank), BF16)], axis=1)


def pack(final, decode, final_across, decode_across):
    lanes = (final.size + decode.size) // PART
    return pl.pallas_call(
        pack_body,
        in_specs=[WHOLE] * 4,
        out_specs=WHOLE,
        out_shape=jax.ShapeDtypeStruct((2, PART, -(-lanes // 128) * 128), BF16),
        compiler_params=params(4),
        name="pack",
    )(final, decode, final_across, decode_across)


def project_pairs(offsets, depth, columns, tile, attended, ours, theirs):
    even = tile % 2 == 0
    total = jnp.zeros((attended.shape[0], columns), F32)
    ours = [(ref, k) for ref in ours for k in range(ref.shape[0])]
    theirs = [(ref, k) for ref in theirs for k in range(ref.shape[0])]
    for offset, (our, i), (their, j) in zip(offsets, ours, theirs):
        left, right = our[i], their[j]
        left, right = jnp.where(even, left, right), jnp.where(even, right, left)
        rows = [
            jnp.concatenate([panel[:, part * depth : (part + 1) * depth] for panel in (left, right)], axis=1)
            for part in range(columns // PART)
        ]
        start = pl.multiple_of(((tile ^ offset) // 2) * (2 * depth), 128)
        total += lax.dot_general(
            attended[:, pl.ds(start, 2 * depth)],
            jnp.concatenate(rows, axis=0),
            (((1,), (1,)), ((), ())),
            preferred_element_type=F32,
        )
    return total


def project_body(offsets, depth, tile_ref, attended, ours, theirs, out):
    out[...] = project_pairs(offsets, depth, out.shape[1], tile_ref[0], attended, [ours], [theirs])


def project(tile, attended, ours, theirs, offsets, depth, columns):
    return pl.pallas_call(
        functools.partial(project_body, offsets, depth),
        in_specs=[SCALARS] + [WHOLE] * 3,
        out_specs=WHOLE,
        out_shape=jax.ShapeDtypeStruct((attended.shape[0], columns), F32),
        compiler_params=params(16),
        name="project",
    )(tile, attended, ours, theirs)


def finish_body(offsets, depth, shape, tile_ref, attended, ours, theirs, part, out, to_pair, to_next):
    frames, patch_rows, patches = shape
    tile = tile_ref[0]
    predicted = part[...] + project_pairs(offsets, depth, part.shape[1], tile, attended, [ours], [theirs])
    predicted = predicted.astype(BF16)
    out[...] = predicted
    even = tile % 2 == 0
    values = predicted.shape[1] // 2
    folds = 128 // values
    count = patches // folds

    def folded(rows):
        return jnp.concatenate([rows[k * count : (k + 1) * count] for k in range(folds)], axis=1)

    for frame in range(frames):
        rows = predicted[frame * patch_rows * patches : (frame + 1) * patch_rows * patches]
        first, last = folded(rows[:patches, :values]), folded(rows[(patch_rows - 1) * patches :, values:])
        to_pair[frame] = jnp.where(even, last, first)
        to_next[frame] = jnp.where(even, first, last)


def finish(tile, attended, ours, theirs, part, offsets, depth, shape):
    tokens, columns = part.shape
    border = jax.ShapeDtypeStruct((shape[0], shape[2] * (columns // 2) // 128, 128), BF16)
    return pl.pallas_call(
        functools.partial(finish_body, offsets, depth, shape),
        in_specs=[SCALARS] + [WHOLE] * 4,
        out_specs=[WHOLE] * 3,
        out_shape=[jax.ShapeDtypeStruct((tokens, columns), BF16), border, border],
        compiler_params=params(16),
        name="finish",
    )(tile, attended, ours, theirs, part)


def unpack_body(order, skip, tile_ref, *refs):
    *panels, out, staged = refs
    taps = out.shape[0]
    place = 0
    for panel in panels:
        for k in range(panel.shape[0]):
            staged[tile_ref[0] ^ order[place]] = panel[k]
            place += 1
    width = out.shape[1] // len(order)
    whole = [
        staged[device, :, skip + part * taps : skip + (part + 1) * taps]
        for device in range(len(order))
        for part in range(width // PART)
    ]
    out[...] = jnp.concatenate(whole, axis=0).T


def unpack(tile, panels, order, skip, taps, width):
    return pl.pallas_call(
        functools.partial(unpack_body, order, skip),
        in_specs=[SCALARS] + [WHOLE] * len(panels),
        out_specs=WHOLE,
        out_shape=jax.ShapeDtypeStruct((taps, width * len(order)), BF16),
        scratch_shapes=[pltpu.VMEM((len(order),) + panels[0].shape[1:], BF16)],
        compiler_params=params(16),
        name="unpack",
    )(tile, *panels)


def tap_rows(frames, cells, width):
    stacks = []
    for shift_t in range(3):
        rows = []
        for frame in range(frames):
            source = frame + shift_t - 2
            rows.append(cells[source] if source >= 0 else jnp.zeros((width, cells[0].shape[1]), BF16))
        stacks.append(jnp.concatenate(rows, axis=0))
    return stacks


def shifted(wide, frame, width, lat):
    chunks = []
    for chunk in range(wide.shape[1]):
        lane = lax.broadcasted_iota(jnp.int32, (width, 128), 1) + 128 * chunk
        shift = (lane // lat) % 3
        near = jnp.where(shift == 1, wide[frame, chunk, 8 : 8 + width], wide[frame, chunk, 9 : 9 + width])
        chunks.append(jnp.where(shift == 0, wide[frame, chunk, 7 : 7 + width], near).astype(BF16))
    return jnp.concatenate(chunks, axis=1)


def spread_body(lat, patch_rows, inner, outer):
    span = 3 * lat
    for side in range(2):
        source = lax.broadcasted_iota(jnp.int32, inner.shape[2:], 0)
        target = lax.broadcasted_iota(jnp.int32, inner.shape[2:], 1)
        for r in range(patch_rows):
            upper = target // span - 2 * r
            wanted = (upper >= 0) & (upper < 2) & (source == upper * 2 * lat + side * lat + target % lat)
            inner[side, r] = jnp.where(wanted, 1.0, 0.0).astype(BF16)
        source = lax.broadcasted_iota(jnp.int32, outer.shape[1:], 0)
        target = lax.broadcasted_iota(jnp.int32, outer.shape[1:], 1)
        wanted = (source == side * lat + target % lat) & (target < 3 * span)
        outer[side] = jnp.where(wanted, 1.0, 0.0).astype(BF16)


def spreads(lat, patch_rows):
    tall = 2 * patch_rows
    return pl.pallas_call(
        functools.partial(spread_body, lat, patch_rows),
        out_specs=[WHOLE, WHOLE],
        out_shape=[
            jax.ShapeDtypeStruct((2, patch_rows, 4 * lat, -(-tall * 3 * lat // 128) * 128), BF16),
            jax.ShapeDtypeStruct((2, 2 * lat, -(-9 * lat // 128) * 128), BF16),
        ],
        compiler_params=params(4),
        cost_estimate=pl.CostEstimate(flops=5 * 10**9, bytes_accessed=0, transcendentals=0),
        name="spreads",
    )()


def border_taps(lat, cells, picks, wide):
    frames, values = cells.shape[0], picks.shape[1]
    folds = 128 // values
    patches = cells.shape[1] * folds
    broad = 2 * patches
    chunks = wide.shape[1]
    span = 3 * lat
    wide[:, :, 0:8] = jnp.zeros((frames, chunks, 8, 128), F32)
    wide[:, :, 8 + broad :] = jnp.zeros((frames, chunks, 8, 128), F32)
    for frame in range(frames):
        folded = cells[frame]
        row = jnp.concatenate([folded[:, k * values : (k + 1) * values] for k in range(folds)], axis=0)
        for side in range(2):
            spread = jnp.dot(row, picks[side], preferred_element_type=F32)
            for chunk in range(chunks):
                wide[frame, chunk, pl.ds(8 + side, patches, stride=2), :] = spread[
                    :, 128 * chunk : 128 * (chunk + 1)
                ]
    ready = [shifted(wide, frame, broad, lat) for frame in range(frames)]
    lane = lax.broadcasted_iota(jnp.int32, ready[0].shape, 1)
    rows = []
    for frame in range(frames):
        taps = jnp.zeros(ready[0].shape, BF16)
        for shift_t in range(3):
            if frame + shift_t - 2 >= 0:
                taps = jnp.where(lane // span == shift_t, ready[frame + shift_t - 2], taps)
        rows.append(taps[:, : 3 * span])
    return rows


def border_panel(lat, kernel, edge):
    span = 3 * lat
    starts = [pl.multiple_of((3 * shift_t + 2 * edge) * span, lat) for shift_t in range(3)]
    return jnp.concatenate([kernel[pl.ds(start, span)] for start in starts], axis=0)


def inner_body(
    lat, tile_ref, predicted, from_pair, inner_picks, outer_picks, kernel, features, edge_sum, pair_row,
    next_panel, wide, border, done, sems
):
    frames, patch_rows, patches, _ = predicted.shape
    tall, broad = 2 * patch_rows, 2 * patches
    span = 3 * lat
    chunks = wide.shape[1]
    even = tile_ref[0] % 2 == 0
    pair_edge = jnp.where(even, 1, 0)
    wide[:, :, 0:8] = jnp.zeros((frames, chunks, 8, 128), F32)
    wide[:, :, 8 + broad :] = jnp.zeros((frames, chunks, 8, 128), F32)
    for side in range(2):
        for frame in range(frames):
            cells = jnp.zeros((patches, 128 * chunks), F32)
            for r in range(patch_rows):
                cells += jnp.dot(predicted[frame, r], inner_picks[side, r], preferred_element_type=F32)
            for chunk in range(chunks):
                wide[frame, chunk, pl.ds(8 + side, patches, stride=2), :] = cells[:, 128 * chunk : 128 * (chunk + 1)]
    stacks = tap_rows(frames, [shifted(wide, f, broad, lat) for f in range(frames)], broad)

    def own_sum(row):
        first, last = max(row - 1, 0), min(row + 1, tall - 1)
        total = jnp.zeros((frames * broad, kernel.shape[1]), F32)
        for shift_t in range(3):
            start = (3 * shift_t + first - (row - 1)) * span
            total += jnp.dot(
                stacks[shift_t][:, first * span : (last + 1) * span],
                kernel[start : start + (last + 1 - first) * span],
                preferred_element_type=F32,
            )
        return total

    copies = []

    def send(index, row, total):
        done[index] = total.astype(BF16).reshape(done.shape[1:])
        copy = pltpu.make_async_copy(done.at[index], features.at[:, row], sems.at[index])
        copy.start()
        copies.append(copy)

    for row in range(1, tall - 1):
        send(row - 1, row, own_sum(row))
    first, last = own_sum(0), own_sum(tall - 1)
    edge_sum[...] = jnp.where(even, first, last)
    taps = jnp.concatenate(border_taps(lat, from_pair, outer_picks, border), axis=0)
    total = jnp.where(even, last, first) + jnp.dot(
        taps, border_panel(lat, kernel, pair_edge), preferred_element_type=F32
    )
    pair_row[...] = total.astype(BF16).reshape(pair_row.shape)
    next_panel[...] = border_panel(lat, kernel, 1 - pair_edge)
    for copy in copies:
        copy.wait()


def border_lanes(lat):
    return -(-9 * lat // 128)


def convolve_inner(tile, predicted, from_pair, inner_picks, outer_picks, kernel):
    frames, patch_rows, patches, values = predicted.shape
    lat = values // 4
    tall, broad = 2 * patch_rows, 2 * patches
    channels = kernel.shape[1]
    lanes = -(-tall * 3 * lat // 128) * 128
    return pl.pallas_call(
        functools.partial(inner_body, lat),
        in_specs=[SCALARS] + [WHOLE] * 5,
        out_specs=[ANYWHERE, WHOLE, WHOLE, WHOLE],
        out_shape=[
            jax.ShapeDtypeStruct((frames, tall, broad, channels), BF16),
            jax.ShapeDtypeStruct((frames * broad, channels), F32),
            jax.ShapeDtypeStruct((frames, broad, channels), BF16),
            jax.ShapeDtypeStruct((9 * lat, channels), BF16),
        ],
        scratch_shapes=[
            pltpu.VMEM((frames, lanes // 128, broad + 16, 128), F32),
            pltpu.VMEM((frames, border_lanes(lat), broad + 16, 128), F32),
            pltpu.VMEM((tall - 2, frames, broad, channels), BF16),
            pltpu.SemaphoreType.DMA((tall - 2,)),
        ],
        compiler_params=params(16),
        cost_estimate=pl.CostEstimate(
            flops=2 * frames * tall * broad * 27 * lat * channels,
            bytes_accessed=2 * frames * tall * broad * channels,
            transcendentals=0,
        ),
        name="convolve_inner",
    )(tile, predicted, from_pair, inner_picks, outer_picks, kernel)


def outer_body(lat, tile_ref, from_next, picks, panel, edge_sum, pair_row, given, features, wide, done, sems):
    frames, tall, broad, _ = features.shape
    edge = jnp.where(tile_ref[0] % 2 == 0, 0, 1)
    copies = [pltpu.make_async_copy(pair_row, features.at[:, (1 - edge) * (tall - 1)], sems.at[frames])]
    copies[0].start()
    for frame, taps in enumerate(border_taps(lat, from_next, picks, wide)):
        total = edge_sum[frame * broad : (frame + 1) * broad] + jnp.dot(
            taps, panel[...], preferred_element_type=F32
        )
        done[frame] = total.astype(BF16)
        copy = pltpu.make_async_copy(done.at[frame], features.at[frame, edge * (tall - 1)], sems.at[frame])
        copy.start()
        copies.append(copy)
    for copy in copies:
        copy.wait()


def convolve_outer(tile, from_next, picks, panel, edge_sum, pair_row, features):
    frames, tall, broad, channels = features.shape
    lat = picks.shape[1] // 2
    return pl.pallas_call(
        functools.partial(outer_body, lat),
        in_specs=[SCALARS] + [WHOLE] * 5 + [ANYWHERE],
        out_specs=ANYWHERE,
        out_shape=jax.ShapeDtypeStruct(features.shape, BF16),
        input_output_aliases={6: 0},
        scratch_shapes=[
            pltpu.VMEM((frames, border_lanes(lat), broad + 16, 128), F32),
            pltpu.VMEM((frames, broad, channels), BF16),
            pltpu.SemaphoreType.DMA((frames + 1,)),
        ],
        compiler_params=params(16),
        name="convolve_outer",
    )(tile, from_next, picks, panel, edge_sum, pair_row, features)


def exchange(value, offset):
    count = lax.axis_size("seq")
    return lax.ppermute(value, "seq", [(i, i ^ offset) for i in range(count)])


def local(queries, own_kv, past_kv, block_home, block_list, list_len, final_weight, decoder_weight):
    frames, patch_rows, patches, width = queries.shape
    tokens = frames * patch_rows * patches
    count = lax.axis_size("seq")
    assert count & (count - 1) == 0
    bits = count.bit_length() - 1
    blocks_here = past_kv.shape[0]
    columns = final_weight.shape[1]
    tile = lax.axis_index("seq").astype(jnp.int32).reshape(1)
    query_rows = queries.reshape(tokens, width)
    own_rows = own_kv.reshape(tokens, own_kv.shape[3])
    shape = (frames, patch_rows, patches)
    inner_picks, outer_picks = spreads(columns // 4, patch_rows)
    half = KV_HEADS // 2
    lists = (tile, block_home, block_list, list_len)
    if count == 16 and columns % PART == 0 and decoder_weight.shape[1] % PART == 0:
        far = [4, 8, 12]
        turns = [(2, 0), (3, 1), (1, 2), (0, 3)]
        line = [exchange(past_kv, k) for k in reversed(far)][::-1]
        final, decode, own_rows, inner_picks, outer_picks = lax.optimization_barrier(
            (final_weight.T, decoder_weight.T, own_rows, inner_picks, outer_picks)
        )
        final_across, decode_across = exchange(final, 2), exchange(decode, 2)
        packed, sums, _ = attend_own(range(half), *lists, query_rows, own_rows, turns, blocks_here)
        *line, final_across, decode_across, packed = lax.optimization_barrier(
            (*line, final_across, decode_across, packed)
        )
        near = join([past_kv] + line, "join_near")
        across = exchange(near, 2)
        panels = pack(final, decode, final_across, decode_across)
        panels_far, panels_near = exchange(panels, 8), exchange(panels, 4)
        own_rows, near = lax.optimization_barrier((own_rows, near))
        others = attend_own(range(half, KV_HEADS), *lists, query_rows, own_rows, turns, blocks_here)
        packed, sums, slots = [packed, others[0]], [sums, others[1]], others[2]
        across, panels_far, panels_near, slots = lax.optimization_barrier((across, panels_far, panels_near, slots))
        gathered = join([near, across], "join_chip")
        gathered = [gathered, exchange(gathered, 1)]
        panels_last = exchange(panels_far, 4)
        panels = join([panels, panels_far, panels_near], "join_panels")
        panels_beside = exchange(panels, 1)
        attended = attend_past(slots, packed, sums, gathered, blocks_here)
        panels_last, panels_beside, attended = lax.optimization_barrier((panels_last, panels_beside, attended))
        panels = [panels, panels_last, panels_beside, exchange(panels_last, 1)]
        order = [k ^ x for k in (0, 8, 4, 12) for x in (0, 2)]
        order = order + [k ^ 1 for k in order]
        depth = final_weight.shape[0]
        part = project(tile, attended, panels[0], panels[2], order[:6], depth, columns)
        predicted, to_pair, to_next = finish(
            tile, attended, panels[1], panels[3], part, order[6:8], depth, shape
        )
        decode = unpack(tile, panels, order, final_weight.size // PART, *decoder_weight.shape)
    else:
        turns = [(bit, bits - 1 - bit) for bit in range(bits)]
        held = past_kv
        for bit in reversed(range(bits)):
            held = jnp.concatenate([held, exchange(held, 1 << bit)], axis=0)
        packed, sums, slots = attend_own(
            range(KV_HEADS), *lists, query_rows, own_rows, turns, blocks_here
        )
        attended = attend_past(slots, [packed], [sums], [held], blocks_here)
        final = lax.all_gather(final_weight, "seq", axis=0, tiled=True)
        decode = lax.all_gather(decoder_weight, "seq", axis=1, tiled=True)
        predicted = jnp.dot(attended, final, preferred_element_type=F32).astype(BF16)
        rows = predicted.reshape(shape + (columns,))
        values = columns // 2
        folds = 128 // values

        def folded(cells):
            parts = cells.reshape(frames, folds, patches // folds, values)
            return parts.transpose(0, 2, 1, 3).reshape(frames, patches // folds, 128)

        first, last = folded(rows[:, 0, :, :values]), folded(rows[:, -1, :, values:])
        even = tile[0] % 2 == 0
        to_pair, to_next = jnp.where(even, last, first), jnp.where(even, first, last)
    predicted = predicted.reshape(shape + (columns,))
    swaps = [(i, i + 1) for i in range(1, count - 1, 2)] + [(i + 1, i) for i in range(1, count - 1, 2)]
    from_next = lax.ppermute(to_next, "seq", swaps)
    from_pair = exchange(to_pair, 1)
    features, edge_sum, pair_row, next_panel = convolve_inner(tile, predicted, from_pair, inner_picks, outer_picks, decode)
    return convolve_outer(tile, from_next, outer_picks, next_panel, edge_sum, pair_row, features)


def solution(mesh):
    return jax.shard_map(
        local,
        mesh=mesh,
        in_specs=(
            P("groups", "seq", None, None),
            P("groups", "seq", None, None),
            P(("groups", "seq"), None, None),
            P("groups"),
            P("groups", None),
            P("groups"),
            P("seq", None),
            P(None, "seq"),
        ),
        out_specs=P("groups", "seq", None, None),
        check_vma=False,
    )
```
